32 devices in a mesh: expert: 16 (over z, y, x), tensor: 2 (over core).
Axes of the slice: x: 2, y: 2, z: 4, core: 2. Of those that a mesh axis runs over, the one named last changes fastest.
Arguments:
- tokens: bfloat16 [6144, 768], P(('expert', 'tensor')), may hold values from -6 to 6
- lengths: int32 [16, 3], P('expert'), may hold values from 1 to 256, 384 in all within a row
- routes: int32 [6144, 1], P(('expert', 'tensor')), may hold values from 0 to 15; in each aligned block of 192 rows (0 to 191, 192 to 383, ...) at most 16 rows name the same one
- norm_gain: bfloat16 [768], replicated, may hold values from 0.5 to 1.5
- w_qkv: bfloat16 [3, 768, 768], P(None, None, 'tensor'), may hold values from -0.21875 to 0.21875
- rel_bias: bfloat16 [32, 12], P(None, 'tensor'), may hold values from -4 to 4
- w_out: bfloat16 [768, 768], P('tensor'), may hold values from -2.5 to 2.5
- moe_gain: bfloat16 [768], replicated, may hold values from 0.5 to 1.5
- w_router: bfloat16 [768, 16], replicated, may hold values from -0.109375 to 0.109375
- w_in: bfloat16 [16, 768, 3072], P('expert'), may hold values from -0.21875 to 0.21875
- w_down: bfloat16 [16, 3072, 768], P('expert')
- cotangent: bfloat16 [6144, 768], P(('expert', 'tensor')), may hold values from -6 to 6
Outputs:
- output: bfloat16 [6144, 768], P(('expert', 'tensor'))
- grad_tokens: float32 [6144, 768], P(('expert', 'tensor'))
- grad_norm_gain: float32 [768], replicated
- grad_w_qkv: float32 [3, 768, 768], P(None, None, 'tensor')
- grad_rel_bias: float32 [32, 12], P(None, 'tensor')
- grad_w_out: float32 [768, 768], P('tensor')
- grad_moe_gain: float32 [768], replicated
- grad_w_router: float32 [768, 16], replicated
- grad_w_in: float32 [16, 768, 3072], P('expert', None, 'tensor')
- grad_w_down: float32 [16, 3072, 768], P('expert', 'tensor')
The draws below stay inside these ranges and needn't reach their ends.
Inputs may be any that keep to these rules, and one draw needn't show every extreme that they name: Each row packs 3 sequences into a group of 384 tokens: the lengths sum to 384, and the longest is exactly 256. `routes`: among the 192 rows of one device no expert is named more than 16 times.
All inputs are finite; a program needn't handle non-finite values.
Results may differ from the reference program's by a relative error of at most 0.012.
Values may be sent and summed in bfloat16 or wider, within the bound.
No kernel may reach another device: no remote copies, remote signals or barrier semaphores. Data moves between devices by JAX's collectives and lax.ppermute only.
A program may use at most 128 MiB of HBM per device.

```python
import math
import jax
import jax.numpy as jnp
import numpy as np
from jax import lax

D = 768
HEADS = 12
HEAD = 64
FF = 3072
BUCKETS = 32
SEQS = 3
TOK_DEV = 192
INNER = 768
EXPERTS = 16
GROUP = 384
GROUPS = 16
TOKENS = 6144
LONGEST = 256
CAP = 16
N_EXPERT = 16
N_TENSOR = 2


def draw_w_down(key, part):
    key = jax.random.fold_in(key, 7)
    spread = 0.7 * EXPERTS / math.sqrt(FF)
    values = jnp.clip(jax.random.normal(key, (EXPERTS, FF, D), jnp.float32), -4.0, 4.0)
    return (values * spread).astype(jnp.bfloat16)


def block_levels(own_key, shape, cuts, low, largest):
    def one(position, blocks):
        heights = jax.random.uniform(jax.random.fold_in(jax.random.fold_in(own_key, 6), position), (blocks,), jnp.float32, low / len(cuts), largest / len(cuts))
        return jnp.repeat(jnp.exp(heights), shape[position] // blocks).reshape((-1,) + (1,) * (len(shape) - position - 1))

    factor_of = one(*cuts[0])
    for cut in cuts[1:]:
        factor_of = factor_of * one(*cut)
    return factor_of


def profile(count, total, reach, lean):
    loads = [(1 << 20) // math.isqrt(standing ** lean) + 1 for standing in range(2, count + 1)]
    rest, counts = total - reach - (count - 1), [1] * (count - 1)
    while rest > 0:
        movable = [i for i in range(count - 1) if counts[i] < reach]
        whole, budget = sum([loads[i] for i in movable]), rest
        for i in movable:
            more = min(reach - counts[i], max(1, budget * loads[i] // whole), rest)
            counts[i] = counts[i] + more
            rest = rest - more
    return np.array([reach] + counts)


def ragged_sizes(rng, count, total, limit, skew):
    if count == 2:
        one = jax.random.randint(rng, (), max(1, total - limit), min(limit, total - 1) + 1)
        return jnp.stack([one, total - one])
    sizes = jnp.asarray(profile(count, total, limit, skew), jnp.int32)
    twos = (count - 1) // 2
    donor, sink = sizes[1:1 + 2 * twos:2], sizes[2:2 + 2 * twos:2]
    slack = jnp.minimum(donor - 1, limit - sink)
    passed = jax.random.randint(jax.random.fold_in(rng, 1), (twos,), 0, 1 << 20) % (slack + 1)
    sizes = sizes.at[1:1 + 2 * twos:2].set(donor - passed).at[2:2 + 2 * twos:2].set(sink + passed)
    return sizes[jax.random.permutation(jax.random.fold_in(rng, 2), count)]


def shared_out(stream_key, own, number, rows, count, top, reach, skew):
    sequence = jax.random.permutation(stream_key, count)
    heavy_load, ordinary = shares(count, rows * top, reach, skew, True), shares(count, rows * top, reach, skew, False)
    places = jnp.arange(count)

    def named(tallies, offset_by):
        used = int((tallies > 0).sum())
        fixed = max(1, used // 4)
        moved = fixed + (places - fixed + offset_by * (used - fixed)) % max(1, count - fixed)
        return jnp.zeros((count,), jnp.int32).at[sequence[jnp.where(places < fixed, places, moved)]].set(jnp.asarray(tallies, jnp.int32))

    tallies = jnp.where(number % 4 == 0, named(heavy_load, number // 4), named(ordinary, number - number // 4 - 1))
    mixed = jax.random.permutation(jax.random.fold_in(own, 3), count)
    source_of, receiver = mixed[0:count // 2 * 2:2], mixed[1:count // 2 * 2:2]
    room = jnp.minimum(tallies[source_of] - 1, reach - tallies[receiver]) // 2
    room = jnp.where((source_of == sequence[0]) | (receiver == sequence[0]) | (tallies[receiver] == 0), 0, jnp.maximum(room, 0))
    moved = jax.random.randint(jax.random.fold_in(own, 4), (count // 2,), 0, 1 << 20) % (room + 1)
    tallies = tallies.at[source_of].add(-moved).at[receiver].add(moved)
    labels = jnp.searchsorted(jnp.cumsum(tallies), jnp.arange(rows * top), side="right").astype(jnp.int32)
    listing = labels.reshape(top, rows).T
    listing = listing[jax.random.permutation(jax.random.fold_in(own, 1), rows)]
    offset_by = jax.random.randint(jax.random.fold_in(own, 2), (rows, 1), 0, top)
    return jnp.take_along_axis(listing, (jnp.arange(top)[None, :] + offset_by) % top, axis=1)


def shares(amount, total, limit, skew, full):
    weights = [(1 << 20) // math.isqrt(grade ** skew) + 1 for grade in range(1, amount + 1)]
    largest = limit if full else min(limit, max(-(-total // amount), total * weights[0] // sum(weights)))
    least = 1 if total - largest >= amount - 1 else 0
    counts, rest = [largest] + [least] * (amount - 1), total - largest - least * (amount - 1)
    while rest > 0:
        candidates = [i for i in range(1, amount) if counts[i] < largest] or [i for i in range(1, amount) if counts[i] < limit]
        whole, left = sum([weights[i] for i in candidates]), rest
        for i in candidates:
            more = min(limit - counts[i], max(1, left * weights[i] // whole), rest)
            counts[i] = counts[i] + more
            rest = rest - more
    return np.array(counts)


def normal_values(own_key, dims, width, bound, split=(), kind=jnp.bfloat16):
    level = block_levels(own_key, dims, split, -0.22, 0.18) if split else 1.0
    values = jax.random.normal(own_key, dims, jnp.float32) * width * level
    return jnp.minimum(jnp.maximum(values, -bound), bound).astype(kind)


def setup_inputs(seed: int = 0) -> dict:
    keys = jax.random.split(jax.random.key(seed), 13)
    tokens = normal_values(keys[0], (TOKENS, D), 1.0, 6.0, ((0, 32),))
    lengths = jax.vmap(lambda own: ragged_sizes(own, SEQS, GROUP, LONGEST, 1))(jax.random.split(keys[1], GROUPS)).reshape((GROUPS, SEQS)).astype(jnp.int32)
    routes_keys = jax.random.split(jax.random.fold_in(keys[2], 1), TOKENS // TOK_DEV)
    routes_turns = jax.random.permutation(jax.random.fold_in(keys[2], 3), TOKENS // TOK_DEV)
    routes = jax.vmap(lambda own, number: shared_out(jax.random.fold_in(keys[2], 2), own, number, TOK_DEV, EXPERTS, 1, CAP, 2))(routes_keys, routes_turns).reshape((TOKENS, 1))
    norm_gain = jnp.clip(1.0 + 0.1 * jax.random.normal(keys[3], (D,), jnp.float32), 0.5, 1.5).astype(jnp.bfloat16)
    w_qkv = normal_values(keys[4], (3, D, INNER), D ** -0.5, 0.21875, ((2, 2),))
    rel_bias = normal_values(keys[5], (BUCKETS, HEADS), 1.0, 4.0, ((1, 2),))
    w_out = normal_values(keys[6], (INNER, D), (max(1, INNER // 128)) ** -0.5, 2.5, ((0, 2),))
    moe_gain = jnp.clip(1.0 + 0.1 * jax.random.normal(keys[7], (D,), jnp.float32), 0.5, 1.5).astype(jnp.bfloat16)
    w_router = normal_values(keys[8], (D, EXPERTS), (4 * D) ** -0.5, 0.109375)
    w_in = normal_values(keys[9], (EXPERTS, D, FF), D ** -0.5, 0.21875, ((0, 16),))
    w_down = draw_w_down(jax.random.fold_in(keys[12], 71), 0)
    cotangent = normal_values(keys[11], (TOKENS, D), 1.0, 6.0, ((0, 32),))
    return {"tokens": tokens, "lengths": lengths, "routes": routes, "norm_gain": norm_gain, "w_qkv": w_qkv, "rel_bias": rel_bias, "w_out": w_out, "moe_gain": moe_gain, "w_router": w_router, "w_in": w_in, "w_down": w_down, "cotangent": cotangent}


epsilon = 1e-06
THRESHOLDS = (1, 2, 3, 4, 5, 6, 7, 8, 12, 16, 23, 32, 46, 64, 91)
halfway = 16

@jax.custom_vjp
def low(v):
    return lax.optimization_barrier(v.astype(jnp.bfloat16)).astype(jnp.float32)

@jax.custom_vjp
def low_back(v):
    return v

def low_keep(v):
    return (low(v), None)

def low_pass(kept, grad):
    return (grad,)

def back_keep(v):
    return (v, None)

def back_low(kept, grad):
    return (low(grad),)
low.defvjp(low_keep, low_pass)
low_back.defvjp(back_keep, back_low)

def rms_norm(inputs, weight):
    factor = lax.rsqrt(lax.optimization_barrier(jnp.mean(inputs * inputs, axis=-1, keepdims=True)) + epsilon)
    return inputs * factor * weight

def bucket_of(distance):
    magnitude = jnp.abs(distance)
    bucket = jnp.zeros(distance.shape, jnp.int32)
    for border in THRESHOLDS:
        bucket = bucket + (magnitude >= border).astype(jnp.int32)
    return bucket + jnp.where(distance > 0, halfway, 0).astype(jnp.int32)

def reference(tokens, lengths, routes, norm_gain, w_qkv, rel_bias, w_out, moe_gain, w_router, w_in, w_down, cotangent):
    highest = lax.Precision.HIGHEST
    device_total = N_EXPERT * N_TENSOR
    boundary = jnp.cumsum(lengths, axis=1).astype(jnp.int32)
    positions = jnp.arange(GROUP, dtype=jnp.int32)
    segments = lax.optimization_barrier(jnp.sum((positions[None, :, None] >= boundary[:, None, :]).astype(jnp.int32), axis=2))
    buckets = bucket_of(positions[None, :] - positions[:, None])
    chosen = routes[:, 0].astype(jnp.int32)
    blocks = chosen.reshape(device_total, TOK_DEV)
    hot_map = (blocks[:, :, None] == jnp.arange(EXPERTS, dtype=jnp.int32)[None, None, :]).astype(jnp.int32)
    ordinal = lax.optimization_barrier(jnp.sum((jnp.cumsum(hot_map, axis=1) - 1) * hot_map, axis=2))
    sources = jnp.arange(device_total, dtype=jnp.int32)[:, None]
    slot_index = ((blocks * device_total + sources) * CAP + ordinal).reshape(TOKENS).astype(jnp.int32)
    token_of_slot = jnp.full((EXPERTS * device_total * CAP,), TOKENS, jnp.int32)
    token_of_slot = token_of_slot.at[slot_index].set(jnp.arange(TOKENS, dtype=jnp.int32))
    token_of_slot = token_of_slot.reshape(EXPERTS, device_total * CAP)
    selected = (chosen[:, None] == jnp.arange(EXPERTS, dtype=jnp.int32)[None, :]).astype(jnp.float32)
    factor = HEAD ** (-0.5)

    def forward(inputs, gain_one, qkv_weight, bias_table, out_weight, gain_two, router_weight, up_weight, down_weight):
        normed = low(rms_norm(inputs, gain_one))
        grouped = normed.reshape(GROUPS, GROUP, D)

        def attend(operands):
            packed, segment = operands
            projected = jnp.einsum('ld,cde->cle', packed, qkv_weight, precision=highest)
            projected = low_back(low(projected))
            queries = projected[0].reshape(GROUP, HEADS, HEAD)
            keys_all = projected[1].reshape(GROUP, HEADS, HEAD)
            values_all = projected[2].reshape(GROUP, HEADS, HEAD)
            scores = jnp.einsum('qhd,khd->hqk', queries, keys_all, precision=highest) * factor
            scores = low_back(scores + jnp.transpose(bias_table[buckets], (2, 0, 1)))
            same_doc = segment[:, None] == segment[None, :]
            scores = jnp.where(same_doc[None], scores, -1e+30)
            chances = low(jax.nn.softmax(scores, axis=-1))
            context = jnp.einsum('hqk,khd->qhd', chances, values_all, precision=highest)
            return context.reshape(GROUP, INNER)
        context = lax.map(jax.checkpoint(attend), (grouped, segments))
        context = low_back(low(context.reshape(TOKENS, INNER)))
        attended = low_back(jnp.dot(context, out_weight, precision=highest))
        residual = inputs + attended
        moe_rows = low(rms_norm(residual, gain_two))
        logits = jnp.dot(moe_rows, router_weight, precision=highest)
        gating = lax.optimization_barrier(jnp.sum(jax.nn.softmax(logits, axis=-1) * selected, axis=1))
        dispatched = low_back(moe_rows)
        padded = jnp.concatenate([dispatched, jnp.zeros((1, D), dispatched.dtype)], axis=0)

        def expert(operands):
            up_one, down_one, index_row = operands
            stacked = padded[index_row]
            hidden_pre = low_back(jnp.dot(stacked, up_one, precision=highest))
            activated = low(jax.nn.gelu(hidden_pre, approximate=False))
            return low(low_back(jnp.dot(activated, down_one, precision=highest)))
        produced = lax.map(jax.checkpoint(expert), (up_weight, down_weight, token_of_slot))
        gathered = produced.reshape(-1, D)[slot_index]
        return residual + gating[:, None] * gathered
    output, pullback = jax.vjp(forward, tokens.astype(jnp.float32), norm_gain.astype(jnp.float32), w_qkv.astype(jnp.float32), rel_bias.astype(jnp.float32), w_out.astype(jnp.float32), moe_gain.astype(jnp.float32), w_router.astype(jnp.float32), w_in.astype(jnp.float32), w_down.astype(jnp.float32))
    grads = pullback(cotangent.astype(jnp.float32))
    return (output.astype(jnp.bfloat16), grads[0], grads[1], grads[2], grads[3], grads[4], grads[5], grads[6], grads[7], grads[8])
```

```python
import functools

import jax
import jax.numpy as jnp
from jax import lax
from jax.experimental import pallas as pl
from jax.experimental.pallas import tpu as pltpu
from jax.sharding import PartitionSpec as P

HEAD = 64
TILE = 128
FF_TILE = 512

epsilon = 1e-06
THRESHOLDS = (1, 2, 3, 4, 5, 6, 7, 8, 12, 16, 23, 32, 46, 64, 91)
halfway = 16
BF = jnp.bfloat16
F32 = jnp.float32
HIGH = lax.Precision.HIGHEST
MIB = 1 << 20


def mm(a, b):
    return lax.dot_general(a, b, (((1,), (0,)), ((), ())), preferred_element_type=F32)


def mm_nt(a, b):
    return lax.dot_general(a, b, (((1,), (1,)), ((), ())), preferred_element_type=F32)


def mm_tn(a, b):
    return lax.dot_general(a, b, (((0,), (0,)), ((), ())), preferred_element_type=F32)


def iota(shape, dim):
    return lax.broadcasted_iota(jnp.int32, shape, dim)


def vmem_specs(count):
    return [pl.BlockSpec(memory_space=pltpu.VMEM)] * count


SMEM = pl.BlockSpec(memory_space=pltpu.SMEM)


def shape_of(*pairs):
    return tuple(jax.ShapeDtypeStruct(shape, dtype) for shape, dtype in pairs)


def params(mib):
    return pltpu.CompilerParams(vmem_limit_bytes=mib * MIB)


def bucket_of(distance):
    magnitude = jnp.abs(distance)
    bucket = jnp.zeros(distance.shape, jnp.int32)
    for border in THRESHOLDS:
        bucket = bucket + (magnitude >= border).astype(jnp.int32)
    return bucket + jnp.where(distance > 0, halfway, 0).astype(jnp.int32)


def distance_hot(buckets, delta):
    distance = iota((buckets, 2 * TILE), 1) + (TILE * delta - (TILE - 1))
    return bucket_of(distance) == iota((buckets, 2 * TILE), 0)


def prep_body(capacity, experts, routes_ref, cot_ref, place_ref, out_ref):
    rows = cot_ref.shape[0]
    chosen = routes_ref[...]
    hot = chosen == iota((rows, experts), 1)
    below = (iota((rows, rows), 1) < iota((rows, rows), 0)).astype(F32).astype(BF)
    earlier = mm(below, hot.astype(F32).astype(BF))
    ordinal = jnp.sum(jnp.where(hot, earlier, 0.0), axis=1, keepdims=True)
    slot = chosen * capacity + ordinal.astype(jnp.int32)
    place = (slot == iota((rows, experts * capacity), 1)).astype(F32).astype(BF)
    place_ref[...] = place
    out_ref[...] = mm_tn(place, cot_ref[...]).astype(BF)


def attend_body(
    half_ref, lengths_ref, x_ref, gain_ref, w_ref, bias_ref,
    own_ref, other_ref, context_ref, qkv_ref, probs_ref, normed_ref,
):
    group = x_ref.shape[0]
    rows = own_ref.shape[0]
    local = w_ref.shape[2]
    heads = local // HEAD
    blocks = group // TILE
    x = x_ref[...].astype(F32)
    factor = lax.rsqrt(jnp.mean(x * x, axis=-1, keepdims=True) + epsilon)
    normed = (x * factor * gain_ref[...].astype(F32)).astype(BF)
    normed_ref[...] = normed
    for c in range(3):
        qkv_ref[:, c * local : (c + 1) * local] = mm(normed, w_ref[c]).astype(BF)
    buckets = bias_ref.shape[1]
    tables = [
        mm(bias_ref[...], distance_hot(buckets, delta).astype(F32).astype(BF))
        for delta in range(1 - blocks, blocks)
    ]
    segment_rows = jnp.zeros((group, 1), jnp.int32)
    segment_lanes = jnp.zeros((1, group), jnp.int32)
    border = jnp.int32(0)
    for s in range(lengths_ref.shape[1]):
        border = border + lengths_ref[0, s]
        segment_rows = segment_rows + (iota((group, 1), 0) >= border).astype(jnp.int32)
        segment_lanes = segment_lanes + (iota((1, group), 1) >= border).astype(jnp.int32)
    for h in range(heads):
        lo = h * HEAD
        keys = qkv_ref[:, local + lo : local + lo + HEAD]
        values = qkv_ref[:, 2 * local + lo : 2 * local + lo + HEAD]
        bands = []
        for number, delta in enumerate(range(1 - blocks, blocks)):
            row = tables[number][h : h + 1, :]
            if abs(delta) > 1:
                bands.append(jnp.broadcast_to(row[:, :1], (TILE, TILE)))
            else:
                wide = jnp.broadcast_to(row, (TILE, 2 * TILE))
                band = pltpu.roll(wide, TILE + 1, 1, stride=1, stride_axis=0)
                bands.append(band[:, :TILE])
        for b in range(blocks):
            at = slice(b * TILE, (b + 1) * TILE)
            queries = qkv_ref[at, lo : lo + HEAD]
            scores = mm_nt(queries, keys) * (HEAD**-0.5)
            scores = scores + jnp.concatenate(
                [bands[k - b + blocks - 1] for k in range(blocks)], axis=1
            )
            scores = jnp.where(segment_rows[at] == segment_lanes, scores, -1e30)
            exponent = jnp.exp(scores - jnp.max(scores, axis=-1, keepdims=True))
            probs = exponent * (1.0 / jnp.sum(exponent, axis=-1, keepdims=True))
            low = probs.astype(BF)
            probs_ref[h, at, :] = low
            context_ref[at, lo : lo + HEAD] = mm(low, values).astype(BF)
    own_at = pl.multiple_of(half_ref[0] * rows, rows)
    other_at = pl.multiple_of((1 - half_ref[0]) * rows, rows)
    own_ref[...] = context_ref[pl.ds(own_at, rows), :]
    other_ref[...] = context_ref[pl.ds(other_at, rows), :]


def project_body(
    own_ref, other_ref, w_own_ref, w_other_ref, x_ref, gain_ref, place_ref, residual_ref, out_ref
):
    attended = mm(own_ref[...], w_own_ref[...]) + mm(other_ref[...], w_other_ref[...])
    residual = x_ref[...].astype(F32) + attended
    residual_ref[...] = residual
    factor = lax.rsqrt(jnp.mean(residual * residual, axis=-1, keepdims=True) + epsilon)
    moe_rows = (residual * factor * gain_ref[...].astype(F32)).astype(BF)
    out_ref[...] = mm_tn(place_ref[...], moe_rows).astype(BF)


def expert_body(
    half_ref, expert_ref, rows_ref, cot_ref, router_ref, up_ref, down_ref,
    scaled_ref, back_ref, router_grad_ref, gp_ref, send_ref, act_ref, pre_ref,
    out_acc, back_acc, gating_ref, chances_ref,
):
    step = pl.program_id(0)
    steps = pl.num_programs(0)
    half_steps = steps // 2
    tile = up_ref.shape[1]
    width = rows_ref.shape[1]
    ff_half = act_ref.shape[1]
    rows = rows_ref[...]

    @pl.when(step == 0)
    def _():
        logits = mm(rows, router_ref[...])
        exponent = jnp.exp(logits - jnp.max(logits, axis=-1, keepdims=True))
        chances = exponent / jnp.sum(exponent, axis=-1, keepdims=True)
        mine = iota(chances.shape, 1) == expert_ref[0]
        gating = jnp.sum(jnp.where(mine, chances, 0.0), axis=-1, keepdims=True)
        gating_ref[...] = jnp.broadcast_to(gating, gating_ref.shape)
        chances_ref[...] = chances
        gp = (gating * cot_ref[...].astype(F32)).astype(BF)
        gp_ref[...] = gp
        send_ref[:, 2 * ff_half : 2 * ff_half + width] = rows
        send_ref[:, 2 * ff_half + width :] = gp
        out_acc[...] = jnp.zeros_like(out_acc)
        back_acc[...] = jnp.zeros_like(back_acc)

    hidden = mm(rows, up_ref[...])
    phi = 0.5 * (1.0 + lax.erf(hidden * (2.0**-0.5)))
    act = (hidden * phi).astype(BF)
    slope = phi + hidden * (jnp.exp(-0.5 * hidden * hidden) * 0.3989422804014327)
    pre = (mm_nt(gp_ref[...], down_ref[...]) * slope).astype(BF)
    out_acc[...] += mm(act, down_ref[...])
    back_acc[...] += mm_nt(pre, up_ref[...])

    @pl.when(step < half_steps)
    def _():
        at = pl.multiple_of(step * tile, tile)
        send_ref[:, pl.ds(at, tile)] = act
        send_ref[:, pl.ds(pl.multiple_of(ff_half + step * tile, tile), tile)] = pre

    @pl.when(step >= half_steps)
    def _():
        at = pl.multiple_of((step - half_steps) * tile, tile)
        act_ref[:, pl.ds(at, tile)] = act
        pre_ref[:, pl.ds(at, tile)] = pre

    @pl.when(step == steps - 1)
    def _():
        gating = gating_ref[:, :1]
        produced = out_acc[...].astype(BF).astype(F32)
        scaled_ref[...] = (gating * produced).astype(BF)
        grad_gate = jnp.sum(cot_ref[...].astype(F32) * produced, axis=-1, keepdims=True)
        chances = chances_ref[...]
        mine = (iota(chances.shape, 1) == expert_ref[0]).astype(F32)
        grad_logits = gating * (mine - chances) * grad_gate
        low = grad_logits.astype(BF)
        rest = (grad_logits - low.astype(F32)).astype(BF)
        back = back_acc[...] + (mm_nt(low, router_ref[...]) + mm_nt(rest, router_ref[...]))
        back_ref[...] = back.astype(BF)
        router_grad_ref[...] = mm_tn(low, rows) + mm_tn(rest, rows)


def expert_grads_body(
    act_ref, pre_ref, rows_ref, gp_ref, act2_ref, pre2_ref, rows2_ref, gp2_ref, down_ref, up_ref
):
    down_ref[...] = mm_tn(act_ref[...], gp_ref[...]) + mm_tn(act2_ref[...], gp2_ref[...])
    up_ref[...] = mm_tn(rows_ref[...], pre_ref[...]) + mm_tn(rows2_ref[...], pre2_ref[...])


def norm_back(grad, source, gain):
    factor = lax.rsqrt(jnp.mean(source * source, axis=-1, keepdims=True) + epsilon)
    unit = source * factor
    scaled = grad * gain
    inner = jnp.mean(scaled * unit, axis=-1, keepdims=True)
    return factor * (scaled - unit * inner), grad * unit


def moe_back_body(place_ref, back_ref, residual_ref, gain_ref, cot_ref, grad_ref, low_ref, gain_grad_ref):
    grad_in = mm(place_ref[...], back_ref[...])
    passed, terms = norm_back(grad_in, residual_ref[...], gain_ref[...].astype(F32))
    grad = cot_ref[...].astype(F32) + passed
    grad_ref[...] = grad
    low_ref[...] = grad.astype(BF)
    gain_grad_ref[...] = jnp.sum(terms, axis=0, keepdims=True)


def fold_diagonals(square):
    wide = jnp.concatenate([square, jnp.zeros_like(square)], axis=1)
    count = TILE
    while count > 8:
        count //= 2
        wide = wide[:count] + pltpu.roll(wide[count:], 2 * TILE - count, 1)
    total = wide[:1]
    for i in range(1, 8):
        total = total + pltpu.roll(wide[i : i + 1], 2 * TILE - i, 1)
    return total


def attend_back_body(
    half_ref, bit_ref, grad_ref, w_out_ref, context_ref, qkv_ref, probs_ref, normed_ref, w_ref, x_ref, gain_ref,
    router_grad_ref, moe_gain_grad_ref,
    send_ref, keep_ref, own_ref, other_ref,
    gqkv_ref, all_ref, gctx_ref,
):
    group = x_ref.shape[0]
    width = x_ref.shape[1]
    rows = own_ref.shape[0]
    local = w_ref.shape[2]
    heads = local // HEAD
    blocks = group // TILE
    grad = grad_ref[...]
    gctx_ref[...] = mm_nt(grad, w_out_ref[...]).astype(BF)
    heads_distance = []
    scale = HEAD**-0.5
    buckets = 2 * halfway
    table = jnp.zeros((8, buckets), F32)
    per_distance = [[] for _ in range(3)]
    edges = [[], []]
    for h in range(heads):
        lo = h * HEAD
        queries = qkv_ref[:, lo : lo + HEAD]
        keys = qkv_ref[:, local + lo : local + lo + HEAD]
        values = qkv_ref[:, 2 * local + lo : 2 * local + lo + HEAD]
        gctx = gctx_ref[:, lo : lo + HEAD]
        low_probs = probs_ref[h]
        grad_probs = mm_nt(gctx, values)
        probs = low_probs.astype(F32)
        inner = jnp.sum(probs * grad_probs, axis=-1, keepdims=True)
        grad_scores = probs * (grad_probs - inner)
        low = grad_scores.astype(BF)
        gqkv_ref[:, lo : lo + HEAD] = (mm(low, keys) * scale).astype(BF)
        gqkv_ref[:, local + lo : local + lo + HEAD] = (mm_tn(low, queries) * scale).astype(BF)
        gqkv_ref[:, 2 * local + lo : 2 * local + lo + HEAD] = mm_tn(low_probs, gctx).astype(BF)
        for number, delta in enumerate((-1, 0, 1)):
            band = None
            for b in range(blocks):
                k = b + delta
                if 0 <= k < blocks:
                    piece = grad_scores[
                        b * TILE : (b + 1) * TILE, k * TILE : (k + 1) * TILE
                    ]
                    band = piece if band is None else band + piece
            per_distance[number].append(fold_diagonals(band))
        for number, sign in enumerate((-1, 1)):
            total = jnp.zeros((1, 1), F32)
            for b in range(blocks):
                for k in range(blocks):
                    if (k - b) * sign > 1:
                        piece = grad_scores[
                            b * TILE : (b + 1) * TILE, k * TILE : (k + 1) * TILE
                        ]
                        total = total + jnp.sum(
                            jnp.sum(piece, axis=0, keepdims=True), axis=1, keepdims=True
                        )
            edges[number].append(total)
    pad = [jnp.zeros((8 - heads, 2 * TILE), F32)]
    for number, delta in enumerate((-1, 0, 1)):
        sums = jnp.concatenate(per_distance[number] + pad, axis=0)
        distance = iota((buckets, 2 * TILE), 1)
        distance = jnp.where(distance >= TILE, distance - 2 * TILE, distance) + TILE * delta
        hot = (bucket_of(distance) == iota((buckets, 2 * TILE), 0)).astype(F32)
        table = table + lax.dot_general(
            sums, hot, (((1,), (1,)), ((), ())), precision=HIGH, preferred_element_type=F32
        )
    for number, bucket in enumerate((halfway - 1, 2 * halfway - 1)):
        column = jnp.concatenate(edges[number] + [jnp.zeros((8 - heads, 1), F32)], axis=0)
        table = table + jnp.where(iota((8, buckets), 1) == bucket, column, 0.0)
    total = None
    for c in range(3):
        part = mm_nt(gqkv_ref[:, c * local : (c + 1) * local], w_ref[c])
        total = part if total is None else total + part
    all_ref[...] = total
    own_at = pl.multiple_of(half_ref[0] * rows, rows)
    other_at = pl.multiple_of((1 - half_ref[0]) * rows, rows)
    own_ref[...] = all_ref[pl.ds(own_at, rows), :]
    other_ref[...] = all_ref[pl.ds(other_at, rows), :]
    x = x_ref[...].astype(F32)
    factor = lax.rsqrt(jnp.mean(x * x, axis=-1, keepdims=True) + epsilon)
    gain_grad = jnp.sum(total * (x * factor), axis=0, keepdims=True)
    first = iota((8, width), 0)
    gains = jnp.where(first == 0, moe_gain_grad_ref[...], jnp.where(first == 1, gain_grad, 0.0))
    experts = router_grad_ref.shape[0]
    small = send_ref.shape[1] - 4 * local
    stacked = jnp.concatenate(
        [
            router_grad_ref[...],
            gains,
            jnp.concatenate([table, jnp.zeros((8, width - buckets), F32)], axis=1),
            jnp.zeros((small - experts - 16, width), F32),
        ],
        axis=0,
    )
    columns = stacked.T
    half_width = width // 2
    for part in range(2):
        at = slice(part * half_width, (part + 1) * half_width)
        w_qkv = mm_tn(normed_ref[:, at], gqkv_ref[...]).astype(BF)
        w_out = mm_tn(grad_ref[:, at], context_ref[...]).astype(BF)
        low = columns[at].astype(BF)
        for wanted, target in ((True, keep_ref), (False, send_ref)):

            @pl.when((bit_ref[0] == part) == wanted)
            def _(target=target, w_qkv=w_qkv, w_out=w_out, low=low):
                target[:, : 3 * local] = w_qkv
                target[:, 3 * local : 4 * local] = w_out
                target[:, 4 * local :] = low


def tokens_body(
    place_ref, scaled_ref, residual_ref, own_ref, got_ref, x_ref, gain_ref, grad_res_ref, out_ref, grad_ref
):
    out_ref[...] = (residual_ref[...] + mm(place_ref[...], scaled_ref[...])).astype(BF)
    passed, _ = norm_back(
        own_ref[...] + got_ref[...], x_ref[...].astype(F32), gain_ref[...].astype(F32)
    )
    grad_ref[...] = grad_res_ref[...] + passed


def unpack_body(bit_ref, own_ref, got_ref, small_ref, qkv_ref, out_ref, router_ref, rows_ref):
    local = qkv_ref.shape[2]
    half = own_ref.shape[0]
    experts = router_ref.shape[1]
    own_at = pl.multiple_of(bit_ref[0] * half, half)
    got_at = pl.multiple_of((1 - bit_ref[0]) * half, half)
    for ref, at in ((own_ref, own_at), (got_ref, got_at)):
        for c in range(3):
            qkv_ref[c, pl.ds(at, half), :] = ref[:, c * local : (c + 1) * local].astype(F32)
        out_ref[:, pl.ds(at, half)] = ref[:, 3 * local : 4 * local].astype(F32).T
    small = small_ref[...]
    router_ref[...] = small[:, :experts]
    rows_ref[...] = small.T[experts : experts + 16]


def per_device(
    tokens, lengths, routes, norm_gain, w_qkv, rel_bias, w_out, moe_gain, w_router, w_in, w_down, cotangent
):
    rows, width = tokens.shape
    sources = lax.axis_size("expert")
    group = rows * lax.axis_size("tensor")
    experts = w_router.shape[1]
    capacity = max(2, 4 * rows // (3 * experts))
    slots = experts * capacity
    local = w_qkv.shape[2]
    heads = local // HEAD
    buckets = rel_bias.shape[0]
    ff = w_in.shape[2]
    ff_half = ff // 2
    half = lax.axis_index("tensor").astype(jnp.int32)
    expert = lax.axis_index("expert").astype(jnp.int32)
    half_one = half.reshape(1)
    gain_a = norm_gain.reshape(1, width)
    gain_b = moe_gain.reshape(1, width)
    small = TILE * -(-(experts + 16) // TILE)
    packed = 4 * local + small

    def swap(value):
        return lax.ppermute(value, "tensor", [(0, 1), (1, 0)])

    def exchange(value):
        return lax.all_to_all(
            value.reshape(experts, capacity, width), "expert", split_axis=0, concat_axis=0, tiled=True
        ).reshape(slots, width)

    w_out_other = swap(w_out)
    place, cot_slots = pl.pallas_call(
        functools.partial(prep_body, capacity, experts),
        out_shape=shape_of(((rows, slots), BF), ((slots, width), BF)),
        in_specs=vmem_specs(2),
        out_specs=vmem_specs(2),
        name="place_cotangent",
    )(routes, cotangent)
    cot_rows = exchange(cot_slots)

    x_group = lax.all_gather(tokens, "tensor", axis=0, tiled=True)
    bias_rows = jnp.pad(rel_bias.T, ((0, 8 - heads), (0, 0)))
    own_ctx, other_ctx, context, qkv, probs, normed = pl.pallas_call(
        attend_body,
        out_shape=shape_of(
            ((rows, local), BF),
            ((rows, local), BF),
            ((group, local), BF),
            ((group, 3 * local), BF),
            ((heads, group, group), BF),
            ((group, width), BF),
        ),
        in_specs=[SMEM, SMEM] + vmem_specs(4),
        out_specs=vmem_specs(6),
        compiler_params=params(40),
        name="attention",
    )(half_one, lengths, x_group, gain_a, w_qkv, bias_rows)
    got_ctx = swap(other_ctx)

    residual, moe_slots = pl.pallas_call(
        project_body,
        out_shape=shape_of(((rows, width), F32), ((slots, width), BF)),
        in_specs=vmem_specs(7),
        out_specs=vmem_specs(2),
        compiler_params=params(24),
        name="projection",
    )(own_ctx, got_ctx, w_out, w_out_other, tokens, gain_b, place)
    stacked = exchange(moe_slots)

    count = sources * capacity
    tile = FF_TILE
    steps = ff // tile
    half_steps = steps // 2

    def weight_tile(step, half_ref, _):
        first = jnp.where(step < half_steps, 1 - half_ref[0], half_ref[0])
        return first * half_steps + lax.rem(step, half_steps)

    whole = lambda shape: pl.BlockSpec(shape, lambda i, *_: (0, 0))
    scaled, back, router_grad, gp, send, act, pre = pl.pallas_call(
        expert_body,
        grid_spec=pltpu.PrefetchScalarGridSpec(
            num_scalar_prefetch=2,
            grid=(steps,),
            in_specs=[
                whole((count, width)),
                whole((count, width)),
                whole((width, experts)),
                pl.BlockSpec((width, tile), lambda i, a, b: (0, weight_tile(i, a, b))),
                pl.BlockSpec((tile, width), lambda i, a, b: (weight_tile(i, a, b), 0)),
            ],
            out_specs=[
                whole((count, width)),
                whole((count, width)),
                whole((experts, width)),
                whole((count, width)),
                whole((count, 2 * ff_half + 2 * width)),
                whole((count, ff_half)),
                whole((count, ff_half)),
            ],
            scratch_shapes=[
                pltpu.VMEM((count, width), F32),
                pltpu.VMEM((count, width), F32),
                pltpu.VMEM((count, TILE), F32),
                pltpu.VMEM((count, experts), F32),
            ],
        ),
        out_shape=shape_of(
            ((count, width), BF),
            ((count, width), BF),
            ((experts, width), F32),
            ((count, width), BF),
            ((count, 2 * ff_half + 2 * width), BF),
            ((count, ff_half), BF),
            ((count, ff_half), BF),
        ),
        compiler_params=params(40),
        name="expert",
    )(half_one, expert.reshape(1), stacked, cot_rows, w_router, w_in[0], w_down[0])
    back_rows = exchange(back)
    peer = swap(send)
    scaled_rows = exchange(scaled)

    grad_res, grad_low, moe_gain_grad = pl.pallas_call(
        moe_back_body,
        out_shape=shape_of(((rows, width), F32), ((rows, width), BF), ((1, width), F32)),
        in_specs=vmem_specs(5),
        out_specs=vmem_specs(3),
        compiler_params=params(24),
        name="norm_back",
    )(place, back_rows, residual, gain_b, cotangent)
    grad_att = lax.all_gather(grad_low, "tensor", axis=0, tiled=True)

    bits = sources.bit_length() - 1
    bit_at = lambda b: (expert >> b) & 1
    first_bit = jnp.where(half == 0, bit_at(0), bit_at(1))
    second_bit = jnp.where(half == 0, bit_at(1), bit_at(0))
    half_width = width // 2
    send_a, keep_a, own_gn, other_gn = pl.pallas_call(
        attend_back_body,
        out_shape=shape_of(
            ((half_width, packed), BF),
            ((half_width, packed), BF),
            ((rows, width), F32),
            ((rows, width), F32),
        ),
        in_specs=[SMEM, SMEM] + vmem_specs(11),
        out_specs=vmem_specs(4),
        scratch_shapes=[
            pltpu.VMEM((group, 3 * local), BF),
            pltpu.VMEM((group, width), F32),
            pltpu.VMEM((group, local), BF),
        ],
        compiler_params=params(48),
        name="attention_back",
    )(
        half_one, first_bit.reshape(1), grad_att, w_out, context, qkv, probs, normed, w_qkv, x_group,
        gain_a, router_grad, moe_gain_grad,
    )
    got_gn = swap(other_gn)

    def pair(value, step):
        moves = []
        for e in range(sources):
            for t in range(2):
                b = step if step > 1 or t == 0 else 1 - step
                moves.append((2 * e + t, 2 * (e ^ (1 << b)) + t))
        return lax.ppermute(value, ("expert", "tensor"), moves)

    def add(a, b):
        return (a.astype(F32) + b.astype(F32)).astype(BF)

    got = pair(send_a, 0)
    step_bits = [first_bit, second_bit] + [bit_at(b) for b in range(2, bits)]
    held = [keep_a, got]
    size = half_width
    depth = 1
    while depth < bits and size % 32 == 0:
        size //= 2
        bit = step_bits[depth]
        cut = lambda v, at: lax.dynamic_slice_in_dim(v, at * size, size, axis=0)
        sent = add(cut(held[0], 1 - bit), cut(held[1], 1 - bit))
        kept = add(cut(held[0], bit), cut(held[1], bit))
        held = [kept, pair(sent, depth)]
        depth += 1
    total = add(*held)
    for later in range(depth, bits):
        total = add(total, pair(total, later))
    for back_step in range(depth - 1, 0, -1):
        received = pair(total, back_step)
        bit = step_bits[back_step]
        total = jnp.concatenate(
            [jnp.where(bit == 0, total, received), jnp.where(bit == 0, received, total)], axis=0
        )
    other_half = pair(total, 0)
    mine_small = total[:, 4 * local :].astype(F32)
    got_small = other_half[:, 4 * local :].astype(F32)
    small_all = jnp.concatenate(
        [jnp.where(first_bit == 0, mine_small, got_small), jnp.where(first_bit == 0, got_small, mine_small)],
        axis=0,
    )
    from_other = swap(small_all.astype(BF)).astype(F32)
    shared = (lax.iota(jnp.int32, small) < experts + 8)[None, :]
    small_sum = small_all + jnp.where(shared, from_other, 0.0)

    grad_qkv, grad_out, grad_router, small_rows = pl.pallas_call(
        unpack_body,
        out_shape=shape_of(
            ((3, width, local), F32),
            ((local, width), F32),
            ((width, experts), F32),
            ((16, width), F32),
        ),
        in_specs=[SMEM] + vmem_specs(3),
        out_specs=vmem_specs(4),
        compiler_params=params(40),
        name="unpack",
    )(first_bit.reshape(1), total, other_half, small_sum)

    output, grad_tokens = pl.pallas_call(
        tokens_body,
        out_shape=shape_of(((rows, width), BF), ((rows, width), F32)),
        in_specs=vmem_specs(8),
        out_specs=vmem_specs(2),
        compiler_params=params(24),
        name="token_outputs",
    )(place, scaled_rows, residual, own_gn, got_gn, tokens, gain_a, grad_res)

    col = lambda first: pl.BlockSpec((count, tile), lambda i: (0, first + i))
    fixed = lambda block: pl.BlockSpec((count, width), lambda i: (0, block))
    grad_down, grad_up = pl.pallas_call(
        expert_grads_body,
        grid=(half_steps,),
        in_specs=[
            col(0), col(0), fixed(0), fixed(0),
            col(0), col(half_steps), fixed(2 * ff_half // width), fixed(2 * ff_half // width + 1),
        ],
        out_specs=[
            pl.BlockSpec((tile, width), lambda i: (i, 0)),
            pl.BlockSpec((width, tile), lambda i: (0, i)),
        ],
        out_shape=shape_of(((ff_half, width), F32), ((width, ff_half), F32)),
        compiler_params=params(32),
        name="expert_grads",
    )(act, pre, stacked, gp, peer, peer, peer, peer)

    return (
        output,
        grad_tokens,
        small_rows[1],
        grad_qkv,
        small_rows[8 : 8 + heads, :buckets].T,
        grad_out,
        small_rows[0],
        grad_router,
        grad_up[None],
        grad_down[None],
    )


def solution(mesh):
    return jax.shard_map(
        per_device,
        mesh=mesh,
        in_specs=(
            P(("expert", "tensor"), None),
            P("expert", None),
            P(("expert", "tensor"), None),
            P(),
            P(None, None, "tensor"),
            P(None, "tensor"),
            P("tensor", None),
            P(),
            P(),
            P("expert", None, None),
            P("expert", None, None),
            P(("expert", "tensor"), None),
        ),
        out_specs=(
            P(("expert", "tensor"), None),
            P(("expert", "tensor"), None),
            P(),
            P(None, None, "tensor"),
            P(None, "tensor"),
            P("tensor", None),
            P(),
            P(),
            P("expert", None, "tensor"),
            P("expert", "tensor", None),
        ),
        check_vma=False,
    )
```

```python
import functools

import jax
import jax.numpy as jnp
from jax import lax
from jax.experimental import pallas as pl
from jax.experimental.pallas import tpu as pltpu
from jax.sharding import PartitionSpec as P

HEAD = 64
TILE = 128
FF_TILE = 512

epsilon = 1e-06
THRESHOLDS = (1, 2, 3, 4, 5, 6, 7, 8, 12, 16, 23, 32, 46, 64, 91)
halfway = 16
BF = jnp.bfloat16
F32 = jnp.float32
HIGH = lax.Precision.HIGHEST
MIB = 1 << 20


def mm(a, b):
    return lax.dot_general(a, b, (((1,), (0,)), ((), ())), preferred_element_type=F32)


def mm_nt(a, b):
    return lax.dot_general(a, b, (((1,), (1,)), ((), ())), preferred_element_type=F32)


def mm_tn(a, b):
    return lax.dot_general(a, b, (((0,), (0,)), ((), ())), preferred_element_type=F32)


def iota(shape, dim):
    return lax.broadcasted_iota(jnp.int32, shape, dim)


def vmem_specs(count):
    return [pl.BlockSpec(memory_space=pltpu.VMEM)] * count


SMEM = pl.BlockSpec(memory_space=pltpu.SMEM)


def shape_of(*pairs):
    return tuple(jax.ShapeDtypeStruct(shape, dtype) for shape, dtype in pairs)


ANY = pl.BlockSpec(memory_space=pl.ANY)


def params(mib):
    return pltpu.CompilerParams(vmem_limit_bytes=mib * MIB)


def hbm(shape, dtype):
    return pltpu.HBM(shape, dtype)


def in_hbm(value):
    return pltpu.with_memory_space_constraint(value, pltpu.HBM)


def fetch(sources, targets, sems):
    copies = []
    for number, (source, target) in enumerate(zip(sources, targets, strict=True)):
        copies.append(pltpu.make_async_copy(source, target, sems.at[number]))
        copies[-1].start()
    return copies


def cost(flops, loaded):
    return pl.CostEstimate(flops=int(flops), bytes_accessed=int(loaded), transcendentals=0)


def bucket_of(distance):
    magnitude = jnp.abs(distance)
    bucket = jnp.zeros(distance.shape, jnp.int32)
    for border in THRESHOLDS:
        bucket = bucket + (magnitude >= border).astype(jnp.int32)
    return bucket + jnp.where(distance > 0, halfway, 0).astype(jnp.int32)


def distance_hot(buckets, delta):
    distance = iota((buckets, 2 * TILE), 1) + (TILE * delta - (TILE - 1))
    return bucket_of(distance) == iota((buckets, 2 * TILE), 0)


def prep_body(capacity, experts, routes_ref, cot_ref, place_out, out_ref, place_ref, sem):
    rows = cot_ref.shape[0]
    chosen = routes_ref[...]
    hot = chosen == iota((experts, rows), 0)
    above = (iota((rows, rows), 0) < iota((rows, rows), 1)).astype(F32).astype(BF)
    earlier = mm(hot.astype(F32).astype(BF), above)
    ordinal = jnp.sum(jnp.where(hot, earlier, 0.0), axis=0, keepdims=True)
    slot = chosen * capacity + ordinal.astype(jnp.int32)
    place = (slot == iota((experts * capacity, rows), 0)).astype(F32).astype(BF)
    place_ref[...] = place
    store = pltpu.make_async_copy(place_ref, place_out, sem)
    store.start()
    out_ref[...] = mm(place, cot_ref[...]).astype(BF)
    store.wait()


def attend_body(
    half_ref, lengths_ref, x_ref, x_other_ref, gain_ref, w_ref, bias_ref,
    own_ref, other_ref, context_out, qkv_out, probs_out, normed_out,
    w_vmem, context_ref, qkv_ref, probs_ref, normed_ref, load_sems, store_sems,
):
    loads = fetch([w_ref.at[c] for c in range(3)], [w_vmem.at[c] for c in range(3)], load_sems)
    stores = []

    def store(source, target):
        stores.append(pltpu.make_async_copy(source, target, store_sems.at[len(stores)]))
        stores[-1].start()

    group = normed_ref.shape[0]
    rows = own_ref.shape[0]
    local = w_ref.shape[2]
    heads = local // HEAD
    blocks = group // TILE
    own_at = pl.multiple_of(half_ref[0] * rows, rows)
    other_at = pl.multiple_of((1 - half_ref[0]) * rows, rows)
    for ref, at in ((x_ref, own_at), (x_other_ref, other_at)):
        x = ref[...].astype(F32)
        factor = lax.rsqrt(jnp.mean(x * x, axis=-1, keepdims=True) + epsilon)
        normed_ref[pl.ds(at, rows), :] = (x * factor * gain_ref[...].astype(F32)).astype(BF)
    normed = normed_ref[...]
    store(normed_ref, normed_out)
    for c in range(3):
        loads[c].wait()
        qkv_ref[:, c * local : (c + 1) * local] = mm(normed, w_vmem[c]).astype(BF)
    store(qkv_ref, qkv_out)
    buckets = bias_ref.shape[1]
    tables = [
        mm(bias_ref[...], distance_hot(buckets, delta).astype(F32).astype(BF))
        for delta in range(1 - blocks, blocks)
    ]
    segment_rows = jnp.zeros((group, 1), jnp.int32)
    segment_lanes = jnp.zeros((1, group), jnp.int32)
    border = jnp.int32(0)
    for s in range(lengths_ref.shape[1]):
        border = border + lengths_ref[0, s]
        segment_rows = segment_rows + (iota((group, 1), 0) >= border).astype(jnp.int32)
        segment_lanes = segment_lanes + (iota((1, group), 1) >= border).astype(jnp.int32)
    for h in range(heads):
        lo = h * HEAD
        keys = qkv_ref[:, local + lo : local + lo + HEAD]
        values = qkv_ref[:, 2 * local + lo : 2 * local + lo + HEAD]
        bands = []
        for number, delta in enumerate(range(1 - blocks, blocks)):
            row = tables[number][h : h + 1, :]
            if abs(delta) > 1:
                bands.append(jnp.broadcast_to(row[:, :1], (TILE, TILE)))
            else:
                wide = jnp.broadcast_to(row, (TILE, 2 * TILE))
                band = pltpu.roll(wide, TILE + 1, 1, stride=1, stride_axis=0)
                bands.append(band[:, :TILE])
        for b in range(blocks):
            at = slice(b * TILE, (b + 1) * TILE)
            queries = qkv_ref[at, lo : lo + HEAD]
            scores = mm_nt(queries, keys) * (HEAD**-0.5)
            scores = scores + jnp.concatenate(
                [bands[k - b + blocks - 1] for k in range(blocks)], axis=1
            )
            scores = jnp.where(segment_rows[at] == segment_lanes, scores, -1e30)
            exponent = jnp.exp(scores - jnp.max(scores, axis=-1, keepdims=True))
            probs = exponent * (1.0 / jnp.sum(exponent, axis=-1, keepdims=True))
            low = probs.astype(BF)
            probs_ref[h, at, :] = low
            context_ref[at, lo : lo + HEAD] = mm(low, values).astype(BF)
        store(probs_ref.at[h], probs_out.at[h])
    store(context_ref, context_out)
    own_ref[...] = context_ref[pl.ds(own_at, rows), :]
    other_ref[...] = context_ref[pl.ds(other_at, rows), :]
    for copy in stores:
        copy.wait()


def project_body(
    own_ref, other_ref, w_other_ref, w_own_hbm, x_hbm, gain_ref, place_hbm, out_ref, residual_out,
    w_own_ref, x_ref, place_ref, residual_ref, sems,
):
    loads = fetch([w_own_hbm, x_hbm, place_hbm], [w_own_ref, x_ref, place_ref], sems)
    attended = mm(other_ref[...], w_other_ref[...])
    loads[0].wait()
    attended = attended + mm(own_ref[...], w_own_ref[...])
    loads[1].wait()
    residual = x_ref[...].astype(F32) + attended
    residual_ref[...] = residual
    store = pltpu.make_async_copy(residual_ref, residual_out, sems.at[3])
    store.start()
    factor = lax.rsqrt(jnp.mean(residual * residual, axis=-1, keepdims=True) + epsilon)
    moe_rows = (residual * factor * gain_ref[...].astype(F32)).astype(BF)
    loads[2].wait()
    out_ref[...] = mm(place_ref[...], moe_rows).astype(BF)
    store.wait()


def expert_body(
    half_ref, expert_ref, rows_ref, cot_ref, router_ref, up_ref, down_ref,
    back_ref, router_grad_ref, scaled_out, gp_out, send_out, act_out, pre_out,
    up_vmem, down_vmem, scaled_ref, gp_ref, send_ref, act_ref, pre_ref, out_acc, back_acc, load_sems, store_sems,
):
    steps, _, tile = up_vmem.shape
    half_steps = steps // 2
    width = rows_ref.shape[1]
    ff_half = act_ref.shape[1]
    loads = []
    for step in range(steps):
        side = 1 - half_ref[0] if step < half_steps else half_ref[0]
        at = pl.multiple_of((side * half_steps + step % half_steps) * tile, tile)
        loads.append(
            fetch(
                [up_ref.at[:, pl.ds(at, tile)], down_ref.at[pl.ds(at, tile), :]],
                [up_vmem.at[step], down_vmem.at[step]],
                load_sems.at[step],
            )
        )
    stores = []

    def store(source, target):
        stores.append(pltpu.make_async_copy(source, target, store_sems.at[len(stores)]))
        stores[-1].start()

    rows = rows_ref[...]
    logits = mm(rows, router_ref[...])
    exponent = jnp.exp(logits - jnp.max(logits, axis=-1, keepdims=True))
    chances = exponent / jnp.sum(exponent, axis=-1, keepdims=True)
    mine = iota(chances.shape, 1) == expert_ref[0]
    gating = jnp.sum(jnp.where(mine, chances, 0.0), axis=-1, keepdims=True)
    gp = (gating * cot_ref[...].astype(F32)).astype(BF)
    gp_ref[...] = gp
    store(gp_ref, gp_out)
    send_ref[:, 2 * ff_half : 2 * ff_half + width] = rows
    send_ref[:, 2 * ff_half + width :] = gp
    for step in range(steps):
        for copy in loads[step]:
            copy.wait()
        hidden = mm(rows, up_vmem[step])
        phi = 0.5 * (1.0 + lax.erf(hidden * (2.0**-0.5)))
        act = (hidden * phi).astype(BF)
        slope = phi + hidden * (jnp.exp(-0.5 * hidden * hidden) * 0.3989422804014327)
        pre = (mm_nt(gp, down_vmem[step]) * slope).astype(BF)
        if step == 0:
            out_acc[...] = mm(act, down_vmem[step])
            back_acc[...] = mm_nt(pre, up_vmem[step])
        else:
            out_acc[...] += mm(act, down_vmem[step])
            back_acc[...] += mm_nt(pre, up_vmem[step])
        if step < half_steps:
            send_ref[:, step * tile : (step + 1) * tile] = act
            send_ref[:, ff_half + step * tile : ff_half + (step + 1) * tile] = pre
        else:
            at = (step - half_steps) * tile
            act_ref[:, at : at + tile] = act
            pre_ref[:, at : at + tile] = pre
        if step == half_steps - 1:
            store(send_ref, send_out)
    store(act_ref, act_out)
    store(pre_ref, pre_out)
    produced = out_acc[...].astype(BF).astype(F32)
    scaled_ref[...] = (gating * produced).astype(BF)
    store(scaled_ref, scaled_out)
    grad_gate = jnp.sum(cot_ref[...].astype(F32) * produced, axis=-1, keepdims=True)
    grad_logits = gating * (mine.astype(F32) - chances) * grad_gate
    low = grad_logits.astype(BF)
    rest = (grad_logits - low.astype(F32)).astype(BF)
    back = back_acc[...] + (mm_nt(low, router_ref[...]) + mm_nt(rest, router_ref[...]))
    back_ref[...] = back.astype(BF)
    router_grad_ref[...] = mm_tn(low, rows) + mm_tn(rest, rows)
    for copy in stores:
        copy.wait()


def expert_grads_body(
    act_ref, pre_ref, rows_ref, gp_ref, act2_ref, pre2_ref, rows2_ref, gp2_ref, down_ref, up_ref
):
    down_ref[...] = mm_tn(act_ref[...], gp_ref[...]) + mm_tn(act2_ref[...], gp2_ref[...])
    up_ref[...] = mm_tn(rows_ref[...], pre_ref[...]) + mm_tn(rows2_ref[...], pre2_ref[...])


def norm_back(grad, source, gain):
    factor = lax.rsqrt(jnp.mean(source * source, axis=-1, keepdims=True) + epsilon)
    unit = source * factor
    scaled = grad * gain
    inner = jnp.mean(scaled * unit, axis=-1, keepdims=True)
    return factor * (scaled - unit * inner), grad * unit


def moe_back_body(
    place_hbm, back_ref, residual_hbm, gain_ref, cot_hbm, _scaled, _after,
    low_ref, gain_grad_ref, grad_out, _passed,
    place_ref, residual_ref, cot_ref, grad_ref, sems,
):
    loads = fetch([place_hbm, residual_hbm, cot_hbm], [place_ref, residual_ref, cot_ref], sems)
    loads[0].wait()
    grad_in = mm_tn(place_ref[...], back_ref[...])
    loads[1].wait()
    passed, terms = norm_back(grad_in, residual_ref[...], gain_ref[...].astype(F32))
    loads[2].wait()
    grad = cot_ref[...].astype(F32) + passed
    grad_ref[...] = grad
    store = pltpu.make_async_copy(grad_ref, grad_out, sems.at[3])
    store.start()
    low_ref[...] = grad.astype(BF)
    gain_grad_ref[...] = jnp.sum(terms, axis=0, keepdims=True)
    store.wait()


def fold_diagonals(square):
    wide = jnp.concatenate([square, jnp.zeros_like(square)], axis=1)
    count = TILE
    while count > 8:
        count //= 2
        wide = wide[:count] + pltpu.roll(wide[count:], 2 * TILE - count, 1)
    total = wide[:1]
    for i in range(1, 8):
        total = total + pltpu.roll(wide[i : i + 1], 2 * TILE - i, 1)
    return total


def attend_back_body(
    half_ref, bits_ref, grad_own_ref, grad_other_ref, w_out_hbm, qkv_hbm, probs_hbm, context_hbm, normed_hbm, w_hbm,
    x_hbm, x_other_hbm, router_grad_ref, moe_gain_grad_ref,
    a0_out, a1_out, a2_out, a3_out, c0_out, c1_out, c2_out, c3_out, small_out, own_out, other_out,
    a0_ref, a1_ref, a2_ref, a3_ref, c0_ref, c1_ref, c2_ref, c3_ref, small_ref, own_ref, other_ref,
    gqkv_ref, all_ref, gctx_ref, grad_ref,
    w_out_ref, qkv_ref, probs_ref, context_ref, normed_ref, w_ref, x_ref, x_other_ref, sems, store_sems,
):
    heads = probs_ref.shape[0]
    w_out_in, qkv_in, *probs_in = fetch(
        [w_out_hbm, qkv_hbm] + [probs_hbm.at[h] for h in range(heads)],
        [w_out_ref, qkv_ref] + [probs_ref.at[h] for h in range(heads)],
        sems,
    )
    context_in, *rest = fetch(
        [context_hbm, w_hbm, x_hbm, x_other_hbm, normed_hbm],
        [context_ref, w_ref, x_ref, x_other_ref, normed_ref],
        sems.at[pl.ds(2 + heads, 5)],
    )
    stores = []

    def store(source, target):
        stores.append(pltpu.make_async_copy(source, target, store_sems.at[len(stores)]))
        stores[-1].start()

    group, width = normed_ref.shape
    rows = own_ref.shape[0]
    local = w_ref.shape[2]
    heads = local // HEAD
    blocks = group // TILE
    own_at = pl.multiple_of(half_ref[0] * rows, rows)
    other_at = pl.multiple_of((1 - half_ref[0]) * rows, rows)
    grad_ref[pl.ds(own_at, rows), :] = grad_own_ref[...]
    grad_ref[pl.ds(other_at, rows), :] = grad_other_ref[...]
    grad = grad_ref[...]
    w_out_in.wait()
    gctx_ref[...] = mm_nt(grad, w_out_ref[...]).astype(BF)
    qkv_in.wait()
    heads_distance = []
    scale = HEAD**-0.5
    buckets = 2 * halfway
    table = jnp.zeros((8, buckets), F32)
    per_distance = [[] for _ in range(3)]
    edges = [[], []]
    for h in range(heads):
        lo = h * HEAD
        queries = qkv_ref[:, lo : lo + HEAD]
        keys = qkv_ref[:, local + lo : local + lo + HEAD]
        values = qkv_ref[:, 2 * local + lo : 2 * local + lo + HEAD]
        gctx = gctx_ref[:, lo : lo + HEAD]
        probs_in[h].wait()
        low_probs = probs_ref[h]
        grad_probs = mm_nt(gctx, values)
        probs = low_probs.astype(F32)
        inner = jnp.sum(probs * grad_probs, axis=-1, keepdims=True)
        grad_scores = probs * (grad_probs - inner)
        low = grad_scores.astype(BF)
        gqkv_ref[:, lo : lo + HEAD] = (mm(low, keys) * scale).astype(BF)
        gqkv_ref[:, local + lo : local + lo + HEAD] = (mm_tn(low, queries) * scale).astype(BF)
        gqkv_ref[:, 2 * local + lo : 2 * local + lo + HEAD] = mm_tn(low_probs, gctx).astype(BF)
        for number, delta in enumerate((-1, 0, 1)):
            band = None
            for b in range(blocks):
                k = b + delta
                if 0 <= k < blocks:
                    piece = grad_scores[
                        b * TILE : (b + 1) * TILE, k * TILE : (k + 1) * TILE
                    ]
                    band = piece if band is None else band + piece
            per_distance[number].append(fold_diagonals(band))
        for number, sign in enumerate((-1, 1)):
            total = jnp.zeros((1, 1), F32)
            for b in range(blocks):
                for k in range(blocks):
                    if (k - b) * sign > 1:
                        piece = grad_scores[
                            b * TILE : (b + 1) * TILE, k * TILE : (k + 1) * TILE
                        ]
                        total = total + jnp.sum(
                            jnp.sum(piece, axis=0, keepdims=True), axis=1, keepdims=True
                        )
            edges[number].append(total)
    plane, depth = bits_ref[0], bits_ref[1]
    shard = width // 16
    half = width // 2
    targets = (c0_ref, c1_ref, c2_ref, c3_ref)
    context_in.wait()
    for a in range(2):
        block = mm_tn(context_ref[...], grad_ref[:, a * half : (a + 1) * half]).astype(BF)
        for z in range(2):
            for number, target in enumerate(targets):

                @pl.when((depth ^ (2 * a + z)) == number)
                def _(target=target, block=block, z=z):
                    for p in range(4):
                        piece = block[(z * 4 + p) * shard : (z * 4 + p + 1) * shard]
                        at = pl.multiple_of((plane ^ p) * shard, shard)
                        target[pl.ds(at, shard), :] = piece
    for target, out in zip(targets, (c0_out, c1_out, c2_out, c3_out)):
        store(target, out)
    pad = [jnp.zeros((8 - heads, 2 * TILE), F32)]
    for number, delta in enumerate((-1, 0, 1)):
        sums = jnp.concatenate(per_distance[number] + pad, axis=0)
        distance = iota((buckets, 2 * TILE), 1)
        distance = jnp.where(distance >= TILE, distance - 2 * TILE, distance) + TILE * delta
        hot = (bucket_of(distance) == iota((buckets, 2 * TILE), 0)).astype(F32)
        table = table + lax.dot_general(
            sums, hot, (((1,), (1,)), ((), ())), precision=HIGH, preferred_element_type=F32
        )
    for number, bucket in enumerate((halfway - 1, 2 * halfway - 1)):
        column = jnp.concatenate(edges[number] + [jnp.zeros((8 - heads, 1), F32)], axis=0)
        table = table + jnp.where(iota((8, buckets), 1) == bucket, column, 0.0)
    for copy in rest:
        copy.wait()
    total = None
    for c in range(3):
        part = mm_nt(gqkv_ref[:, c * local : (c + 1) * local], w_ref[c])
        total = part if total is None else total + part
    all_ref[...] = total
    own_ref[...] = all_ref[pl.ds(own_at, rows), :]
    other_ref[...] = all_ref[pl.ds(other_at, rows), :]
    store(own_ref, own_out)
    store(other_ref, other_out)
    gain_grad = jnp.zeros((1, width), F32)
    for ref, part in ((x_ref, own_ref), (x_other_ref, other_ref)):
        x = ref[...].astype(F32)
        factor = lax.rsqrt(jnp.mean(x * x, axis=-1, keepdims=True) + epsilon)
        gain_grad = gain_grad + jnp.sum(part[...] * (x * factor), axis=0, keepdims=True)
    targets = (a0_ref, a1_ref, a2_ref, a3_ref)
    for a in range(2):
        block = mm_tn(normed_ref[:, a * half : (a + 1) * half], gqkv_ref[...]).astype(BF)
        for p in range(2):
            for number, target in enumerate(targets):

                @pl.when((plane ^ (2 * a + p)) == number)
                def _(target=target, block=block, p=p):
                    for z in range(4):
                        piece = block[(p * 4 + z) * shard : (p * 4 + z + 1) * shard]
                        at = pl.multiple_of((depth ^ z) * shard, shard)
                        target[pl.ds(at, shard), :] = piece
    for target, out in zip(targets, (a0_out, a1_out, a2_out, a3_out)):
        store(target, out)
    moe_gain_grad = moe_gain_grad_ref[...]
    row = iota((16, local), 0)
    extra = jnp.concatenate([table, jnp.zeros((8, local - buckets), F32)], axis=1)
    extra = jnp.concatenate([jnp.zeros((8, local), F32), extra], axis=0)
    for number, value in enumerate((moe_gain_grad, gain_grad)):
        for part in range(2):
            piece = value[:, part * local : (part + 1) * local]
            extra = extra + jnp.where(row == 2 * number + part, piece, 0.0)
    small = jnp.concatenate(
        [router_grad_ref[:, :local], router_grad_ref[:, local:], extra], axis=0
    ).astype(BF)
    small_ref[...] = small
    store(small_ref, small_out)
    for copy in stores:
        copy.wait()


def order_body(_value, _after, _out):
    pass


def total_of(*values):
    return functools.reduce(jnp.add, [v.astype(F32) for v in values]).astype(BF)


def pairs_of(a, b, c, d):
    return ((a.astype(F32) + b.astype(F32)) + (c.astype(F32) + d.astype(F32))).astype(BF)


def fold_first_body(
    a1_ref, a2_ref, a3_ref, c1_ref, c2_ref, c3_ref, a0_hbm, c0_hbm, small_hbm,
    s0_ref, s1_ref, s2_ref, s3_ref, e0_ref, e1_ref, e2_ref, e3_ref,
    a0_ref, c0_ref, small_ref, sems,
):
    for copy in fetch([a0_hbm, c0_hbm, small_hbm], [a0_ref, c0_ref, small_ref], sems):
        copy.wait()
    shard, lead = s0_ref.shape[0], small_ref.shape[0]
    for d, target in enumerate((s0_ref, s1_ref, s2_ref, s3_ref)):
        at = slice(d * shard, (d + 1) * shard)
        target[...] = pairs_of(a0_ref[at], a1_ref[at], a2_ref[at], a3_ref[at])
    for d, target in enumerate((e0_ref, e1_ref, e2_ref, e3_ref)):
        at = slice(d * shard, (d + 1) * shard)
        target[:lead] = small_ref[...]
        target[lead:] = pairs_of(c0_ref[at], c1_ref[at], c2_ref[at], c3_ref[at])


def fold_last_body(
    s0_ref, s1_ref, s2_ref, s3_ref, e0_ref, e1_ref, e2_ref, e3_ref, _after, total_ref, c_ref, small_ref
):
    lead = small_ref.shape[0]
    total_ref[...] = pairs_of(s0_ref[...], s1_ref[...], s2_ref[...], s3_ref[...])
    small_ref[...] = pairs_of(e0_ref[:lead], e1_ref[:lead], e2_ref[:lead], e3_ref[:lead])
    c_ref[...] = pairs_of(e0_ref[lead:], e1_ref[lead:], e2_ref[lead:], e3_ref[lead:])


def join_body(shared, *refs):
    total_refs, c_refs = refs[:4], refs[4:8]
    small_ref, other_ref, mine_ref, c_mine_ref = refs[8:]
    shard = c_refs[0].shape[0]
    for d in range(4):
        mine_ref[d * shard : (d + 1) * shard] = total_refs[d][...]
        c_mine_ref[d * shard : (d + 1) * shard] = c_refs[d][...]
    own = small_ref[...].astype(F32)
    both = own + other_ref[...].astype(F32)
    c_mine_ref[4 * shard :] = jnp.where(iota(own.shape, 0) < shared, both, own).astype(BF)


def tokens_body(
    place_ref, scaled_ref, residual_ref, own_ref, got_ref, x_ref, gain_ref, grad_res_ref, _after, out_ref, grad_ref
):
    out_ref[...] = (residual_ref[...] + mm_tn(place_ref[...], scaled_ref[...])).astype(BF)
    passed, _ = norm_back(
        own_ref[...] + got_ref[...], x_ref[...].astype(F32), gain_ref[...].astype(F32)
    )
    grad_ref[...] = grad_res_ref[...] + passed


def unpack_body(
    bits_ref, a0_ref, a1_ref, a2_ref, a3_ref, c0_ref, c1_ref, c2_ref, c3_ref,
    router_ref, norm_gain_ref, moe_gain_ref, bias_ref, qkv_out, w_out_out,
    wide_ref, w_out_ref, qkv_sems, out_sems,
):
    local = qkv_out.shape[2]
    shard = a0_ref.shape[0] // 4
    plane, depth = bits_ref[0], bits_ref[1]
    copies = []
    for number, ref in enumerate((a0_ref, a1_ref, a2_ref, a3_ref)):
        quarter = plane ^ number
        wide_ref[number] = ref[...].astype(F32)
        for d in range(4):
            at = pl.multiple_of((quarter * 4 + (depth ^ d)) * shard, shard)
            for c in range(3):
                copy = pltpu.make_async_copy(
                    wide_ref.at[number, pl.ds(d * shard, shard), pl.ds(c * local, local)],
                    qkv_out.at[c, pl.ds(at, shard), :],
                    qkv_sems.at[number, d, c],
                )
                copy.start()
                copies.append(copy)
    others = (c0_ref, c1_ref, c2_ref, c3_ref)
    for number, ref in enumerate(others):
        w_out_ref[number] = ref[: 4 * shard].astype(F32)
        slab = depth ^ number
        lane = pl.multiple_of((slab // 2) * local, local)
        for b in range(4):
            place = (slab % 2) * 4 + (plane ^ b)
            at = pl.multiple_of(place * shard, shard)
            copy = pltpu.make_async_copy(
                w_out_ref.at[number, pl.ds(b * shard, shard), :],
                w_out_out.at[pl.ds(at, shard), pl.ds(lane, local)],
                out_sems.at[number, b],
            )
            copy.start()
            copies.append(copy)
    parts = [ref[4 * shard :].astype(F32) for ref in others]
    small = (parts[0] + parts[1]) + (parts[2] + parts[3])
    experts = router_ref.shape[0]
    router_ref[:, :local] = small[:experts]
    router_ref[:, local:] = small[experts : 2 * experts]
    rest = small[2 * experts :]
    for number, ref in enumerate((moe_gain_ref, norm_gain_ref)):
        ref[:, :local] = rest[2 * number : 2 * number + 1]
        ref[:, local:] = rest[2 * number + 1 : 2 * number + 2]
    bias_ref[...] = rest[8 : 8 + bias_ref.shape[0], : bias_ref.shape[1]]
    for copy in copies:
        copy.wait()


def per_device(
    tokens, lengths, routes, norm_gain, w_qkv, rel_bias, w_out, moe_gain, w_router, w_in, w_down, cotangent
):
    rows, width = tokens.shape
    sources = lax.axis_size("expert")
    group = rows * lax.axis_size("tensor")
    experts = w_router.shape[1]
    capacity = max(2, 4 * rows // (3 * experts))
    slots = experts * capacity
    local = w_qkv.shape[2]
    heads = local // HEAD
    buckets = rel_bias.shape[0]
    ff = w_in.shape[2]
    ff_half = ff // 2
    half = lax.axis_index("tensor").astype(jnp.int32)
    expert = lax.axis_index("expert").astype(jnp.int32)
    half_one = half.reshape(1)
    gain_a = norm_gain.reshape(1, width)
    gain_b = moe_gain.reshape(1, width)

    def swap(value):
        return lax.ppermute(value, "tensor", [(0, 1), (1, 0)])

    def exchange(value):
        return lax.all_to_all(
            value.reshape(experts, capacity, width), "expert", split_axis=0, concat_axis=0, tiled=True
        ).reshape(slots, width)

    x_other = swap(tokens)
    w_out_other = swap(w_out)
    place, cot_slots = pl.pallas_call(
        functools.partial(prep_body, capacity, experts),
        out_shape=(hbm((slots, rows), BF),) + shape_of(((slots, width), BF)),
        in_specs=vmem_specs(2),
        out_specs=[ANY] + vmem_specs(1),
        scratch_shapes=[pltpu.VMEM((slots, rows), BF), pltpu.SemaphoreType.DMA],
        cost_estimate=cost(2e9, 1e6),
        name="place_cotangent",
    )(routes.reshape(1, rows), cotangent)
    cot_rows = exchange(cot_slots)

    bias_rows = jnp.pad(rel_bias.T, ((0, 8 - heads), (0, 0)))
    own_ctx, other_ctx, context, qkv, probs, normed = pl.pallas_call(
        attend_body,
        out_shape=shape_of(((rows, local), BF), ((rows, local), BF))
        + (
            hbm((group, local), BF),
            hbm((group, 3 * local), BF),
            hbm((heads, group, group), BF),
            hbm((group, width), BF),
        ),
        in_specs=[SMEM, SMEM] + vmem_specs(3) + [ANY] + vmem_specs(1),
        out_specs=vmem_specs(2) + [ANY] * 4,
        scratch_shapes=[
            pltpu.VMEM((3, width, local), BF),
            pltpu.VMEM((group, local), BF),
            pltpu.VMEM((group, 3 * local), BF),
            pltpu.VMEM((heads, group, group), BF),
            pltpu.VMEM((group, width), BF),
            pltpu.SemaphoreType.DMA((3,)),
            pltpu.SemaphoreType.DMA((heads + 3,)),
        ],
        compiler_params=params(20),
        cost_estimate=cost(8e9, 4e6),
        name="attention",
    )(half_one, lengths, tokens, x_other, gain_a, in_hbm(w_qkv), bias_rows)
    got_ctx = swap(other_ctx)

    moe_slots, residual = pl.pallas_call(
        project_body,
        out_shape=shape_of(((slots, width), BF)) + (hbm((rows, width), F32),),
        in_specs=vmem_specs(3) + [ANY] * 2 + vmem_specs(1) + [ANY],
        out_specs=vmem_specs(1) + [ANY],
        scratch_shapes=[
            pltpu.VMEM((local, width), BF),
            pltpu.VMEM((rows, width), BF),
            pltpu.VMEM((slots, rows), BF),
            pltpu.VMEM((rows, width), F32),
            pltpu.SemaphoreType.DMA((4,)),
        ],
        compiler_params=params(12),
        cost_estimate=cost(2e9, 2e6),
        name="projection",
    )(own_ctx, got_ctx, w_out_other, in_hbm(w_out), in_hbm(tokens), gain_b, in_hbm(place))
    stacked = exchange(moe_slots)

    count = sources * capacity
    tile = FF_TILE
    steps = ff // tile
    half_steps = steps // 2

    back, router_grad, scaled, gp, send, act, pre = pl.pallas_call(
        expert_body,
        out_shape=shape_of(((count, width), BF), ((experts, width), F32))
        + (
            hbm((count, width), BF),
            hbm((count, width), BF),
            hbm((count, 2 * ff_half + 2 * width), BF),
            hbm((count, ff_half), BF),
            hbm((count, ff_half), BF),
        ),
        in_specs=[SMEM, SMEM] + vmem_specs(3) + [ANY, ANY],
        out_specs=vmem_specs(2) + [ANY] * 5,
        scratch_shapes=[
            pltpu.VMEM((steps, width, tile), BF),
            pltpu.VMEM((steps, tile, width), BF),
            pltpu.VMEM((count, width), BF),
            pltpu.VMEM((count, width), BF),
            pltpu.VMEM((count, 2 * ff_half + 2 * width), BF),
            pltpu.VMEM((count, ff_half), BF),
            pltpu.VMEM((count, ff_half), BF),
            pltpu.VMEM((count, width), F32),
            pltpu.VMEM((count, width), F32),
            pltpu.SemaphoreType.DMA((steps, 2)),
            pltpu.SemaphoreType.DMA((5,)),
        ],
        compiler_params=params(32),
        cost_estimate=cost(10e9, 14e6),
        name="expert",
    )(half_one, expert.reshape(1), stacked, cot_rows, w_router, in_hbm(w_in[0]), in_hbm(w_down[0]))
    back_rows = exchange(back)
    peer = swap(send)

    col = lambda first: pl.BlockSpec((count, tile), lambda i: (0, first + i))
    fixed = lambda block: pl.BlockSpec((count, width), lambda i: (0, block))
    grad_down, grad_up = pl.pallas_call(
        expert_grads_body,
        grid=(half_steps,),
        in_specs=[
            col(0), col(0), fixed(0), fixed(0),
            col(0), col(half_steps), fixed(2 * ff_half // width), fixed(2 * ff_half // width + 1),
        ],
        out_specs=[
            pl.BlockSpec((tile, width), lambda i: (i, 0)),
            pl.BlockSpec((width, tile), lambda i: (0, i)),
        ],
        out_shape=shape_of(((ff_half, width), F32), ((width, ff_half), F32)),
        compiler_params=params(20),
        cost_estimate=cost(5e9, 14e6),
        name="expert_grads",
    )(in_hbm(act), in_hbm(pre), stacked, in_hbm(gp), *[in_hbm(peer)] * 4)

    grad_low, moe_gain_grad, grad_res, scaled_late = pl.pallas_call(
        moe_back_body,
        out_shape=shape_of(((rows, width), BF), ((1, width), F32))
        + (hbm((rows, width), F32), hbm((count, width), BF)),
        in_specs=[ANY] + vmem_specs(1) + [ANY] + vmem_specs(1) + [ANY] * 3,
        out_specs=vmem_specs(2) + [ANY, ANY],
        input_output_aliases={5: 3},
        scratch_shapes=[
            pltpu.VMEM((slots, rows), BF),
            pltpu.VMEM((rows, width), F32),
            pltpu.VMEM((rows, width), BF),
            pltpu.VMEM((rows, width), F32),
            pltpu.SemaphoreType.DMA((4,)),
        ],
        compiler_params=params(12),
        cost_estimate=cost(1e9, 2e6),
        name="norm_back",
    )(in_hbm(place), back_rows, in_hbm(residual), gain_b, in_hbm(cotangent), scaled, in_hbm(grad_down))
    grad_other = swap(grad_low)
    scaled_rows = exchange(scaled_late)

    position = jnp.stack([expert & 3, (expert >> 2) & 3])
    shard = width // 16
    lead = 2 * experts + 16
    big, slab, token_grad = (4 * shard, 3 * local), (4 * shard, local), (rows, width)
    parts = pl.pallas_call(
        attend_back_body,
        out_shape=(
            *[hbm(big, BF)] * 4, *[hbm(slab, BF)] * 4, hbm((lead, local), BF), *[hbm(token_grad, F32)] * 2
        ),
        in_specs=[SMEM, SMEM] + vmem_specs(2) + [ANY] * 8 + vmem_specs(2),
        out_specs=[ANY] * 11,
        scratch_shapes=[pltpu.VMEM(big, BF)] * 4
        + [pltpu.VMEM(slab, BF)] * 4
        + [pltpu.VMEM((lead, local), BF)]
        + [pltpu.VMEM(token_grad, F32)] * 2
        + [
            pltpu.VMEM((group, 3 * local), BF),
            pltpu.VMEM((group, width), F32),
            pltpu.VMEM((group, local), BF),
            pltpu.VMEM((group, width), BF),
            pltpu.VMEM((local, width), BF),
            pltpu.VMEM((group, 3 * local), BF),
            pltpu.VMEM((heads, group, group), BF),
            pltpu.VMEM((group, local), BF),
            pltpu.VMEM((group, width), BF),
            pltpu.VMEM((3, width, local), BF),
            pltpu.VMEM((rows, width), BF),
            pltpu.VMEM((rows, width), BF),
            pltpu.SemaphoreType.DMA((7 + heads,)),
            pltpu.SemaphoreType.DMA((11,)),
        ],
        compiler_params=params(32),
        cost_estimate=cost(10e9, 10e6),
        name="attention_back",
    )(
        half_one, position, grad_low, grad_other, in_hbm(w_out), in_hbm(qkv), in_hbm(probs), in_hbm(context), in_hbm(normed), in_hbm(w_qkv),
        in_hbm(tokens), in_hbm(x_other), router_grad, moe_gain_grad,
    )
    a0, a1, a2, a3, c0, c1, c2, c3, small, own_gn, other_gn = parts
    a1 = pl.pallas_call(
        order_body,
        out_shape=hbm(a1.shape, BF),
        in_specs=[ANY, ANY],
        out_specs=ANY,
        input_output_aliases={0: 0},
        name="order",
    )(a1, in_hbm(scaled_rows))

    def moves(flip):
        pairs = [(2 * e + t, 2 * (e ^ flip) + t) for e in range(sources) for t in range(2)]
        return lambda value: lax.ppermute(value, ("expert", "tensor"), pairs)

    flat = [moves(d) for d in range(1, 4)]
    along = [moves(4 * d) for d in range(1, 4)]

    def add(*values):
        return functools.reduce(jnp.add, [v.astype(F32) for v in values]).astype(BF)

    def fused(name, body, shapes, values, before=(), mib=8):
        return pl.pallas_call(
            body,
            out_shape=[jax.ShapeDtypeStruct(shape, dtype) for shape, dtype in shapes],
            in_specs=vmem_specs(len(values)) + [ANY] * len(before),
            out_specs=vmem_specs(len(shapes)),
            compiler_params=params(mib),
            cost_estimate=cost(1e3, 1e3),
            name=name,
        )(*values, *[in_hbm(value) for value in before])

    quarter = 4 * shard
    wide = 3 * local
    got_a = [flat[d](a) for d, a in enumerate((a1, a2, a3))]
    got_c = [along[d](c) for d, c in enumerate((c1, c2, c3))]
    got_gn = swap(other_gn)
    folded = pl.pallas_call(
        fold_first_body,
        out_shape=shape_of(*[((shard, wide), BF)] * 4, *[((lead + shard, local), BF)] * 4),
        in_specs=vmem_specs(6) + [ANY] * 3,
        out_specs=vmem_specs(8),
        scratch_shapes=[
            pltpu.VMEM(big, BF),
            pltpu.VMEM(slab, BF),
            pltpu.VMEM((lead, local), BF),
            pltpu.SemaphoreType.DMA((3,)),
        ],
        compiler_params=params(8),
        cost_estimate=cost(1e3, 1e3),
        name="fold_first",
    )(*got_a, *got_c, in_hbm(a0), in_hbm(c0), in_hbm(small))
    parts_z, parts_c = folded[:4], folded[4:]
    got_z = [along[d](parts_z[d + 1]) for d in range(3)]
    got_e = [flat[d](parts_c[d + 1]) for d in range(3)]
    output, grad_tokens = pl.pallas_call(
        tokens_body,
        out_shape=shape_of(((rows, width), BF), ((rows, width), F32)),
        in_specs=vmem_specs(8) + [ANY],
        out_specs=vmem_specs(2),
        compiler_params=params(12),
        cost_estimate=cost(1e3, 1e3),
        name="token_outputs",
    )(place, scaled_rows, residual, own_gn, got_gn, tokens, gain_a, grad_res, in_hbm(parts_z[0]))

    total, c_shard, small = fused(
        "fold_last",
        fold_last_body,
        [((shard, wide), BF), ((shard, local), BF), ((lead, local), BF)],
        (parts_z[0], *got_z, parts_c[0], *got_e),
        (grad_tokens,),
    )
    for b in range(4, sources.bit_length() - 1):
        further = moves(1 << b)
        total = add(total, further(total))
        c_shard = add(c_shard, further(c_shard))
        small = add(small, further(small))

    others = [along[d](total) for d in range(3)]
    c_beside = [flat[d](c_shard) for d in range(3)]
    mine, c_mine = fused(
        "join",
        functools.partial(join_body, 2 * experts + 8),
        [((quarter, wide), BF), ((quarter + lead, local), BF)],
        (total, *others, c_shard, *c_beside, small, swap(small)),
    )
    all_mine = [mine] + [flat[d](mine) for d in range(3)]
    c_others = [along[d](c_mine) for d in range(3)]
    grad_router, grad_norm_gain, grad_moe_gain, grad_rel, grad_qkv, grad_out = pl.pallas_call(
        unpack_body,
        out_shape=shape_of(
            ((experts, width), F32), ((1, width), F32), ((1, width), F32), ((heads, buckets), F32)
        )
        + (hbm((3, width, local), F32), hbm((local, width), F32)),
        in_specs=[SMEM] + vmem_specs(8),
        out_specs=vmem_specs(4) + [ANY] * 2,
        scratch_shapes=[
            pltpu.VMEM((4, quarter, wide), F32),
            pltpu.VMEM((4, quarter, local), F32),
            pltpu.SemaphoreType.DMA((4, 4, 3)),
            pltpu.SemaphoreType.DMA((4, 4)),
        ],
        compiler_params=params(12),
        cost_estimate=cost(1e3, 1e3),
        name="unpack",
    )(position, *all_mine, c_mine, *c_others)

    return (
        output,
        grad_tokens,
        grad_norm_gain[0],
        grad_qkv,
        grad_rel.T,
        grad_out,
        grad_moe_gain[0],
        grad_router.T,
        grad_up[None],
        grad_down[None],
    )


def solution(mesh):
    return jax.shard_map(
        per_device,
        mesh=mesh,
        in_specs=(
            P(("expert", "tensor"), None),
            P("expert", None),
            P(("expert", "tensor"), None),
            P(),
            P(None, None, "tensor"),
            P(None, "tensor"),
            P("tensor", None),
            P(),
            P(),
            P("expert", None, None),
            P("expert", None, None),
            P(("expert", "tensor"), None),
        ),
        out_specs=(
            P(("expert", "tensor"), None),
            P(("expert", "tensor"), None),
            P(),
            P(None, None, "tensor"),
            P(None, "tensor"),
            P("tensor", None),
            P(),
            P(),
            P("expert", None, "tensor"),
            P("expert", "tensor", None),
        ),
        check_vma=False,
    )
```

```python
import functools

import jax
import jax.numpy as jnp
from jax import lax
from jax.experimental import pallas as pl
from jax.experimental.pallas import tpu as pltpu
from jax.sharding import PartitionSpec as P

HEAD = 64
TILE = 128
FF_TILE = 512

epsilon = 1e-06
THRESHOLDS = (1, 2, 3, 4, 5, 6, 7, 8, 12, 16, 23, 32, 46, 64, 91)
halfway = 16
BF = jnp.bfloat16
F32 = jnp.float32
HIGH = lax.Precision.HIGHEST
MIB = 1 << 20


def mm(a, b):
    return lax.dot_general(a, b, (((1,), (0,)), ((), ())), preferred_element_type=F32)


def mm_nt(a, b):
    return lax.dot_general(a, b, (((1,), (1,)), ((), ())), preferred_element_type=F32)


def mm_tn(a, b):
    return lax.dot_general(a, b, (((0,), (0,)), ((), ())), preferred_element_type=F32)


def iota(shape, dim):
    return lax.broadcasted_iota(jnp.int32, shape, dim)


def vmem_specs(count):
    return [pl.BlockSpec(memory_space=pltpu.VMEM)] * count


SMEM = pl.BlockSpec(memory_space=pltpu.SMEM)


def shape_of(*pairs):
    return tuple(jax.ShapeDtypeStruct(shape, dtype) for shape, dtype in pairs)


ANY = pl.BlockSpec(memory_space=pl.ANY)


def params(mib):
    return pltpu.CompilerParams(vmem_limit_bytes=mib * MIB)


def hbm(shape, dtype):
    return pltpu.HBM(shape, dtype)


def in_hbm(value):
    return pltpu.with_memory_space_constraint(value, pltpu.HBM)


def fetch(sources, targets, sems):
    copies = []
    for number, (source, target) in enumerate(zip(sources, targets, strict=True)):
        copies.append(pltpu.make_async_copy(source, target, sems.at[number]))
        copies[-1].start()
    return copies


def cost(flops, loaded):
    return pl.CostEstimate(flops=int(flops), bytes_accessed=int(loaded), transcendentals=0)


def bucket_of(distance):
    magnitude = jnp.abs(distance)
    bucket = jnp.zeros(distance.shape, jnp.int32)
    for border in THRESHOLDS:
        bucket = bucket + (magnitude >= border).astype(jnp.int32)
    return bucket + jnp.where(distance > 0, halfway, 0).astype(jnp.int32)


def distance_hot(buckets, delta):
    distance = iota((buckets, 2 * TILE), 1) + (TILE * delta - (TILE - 1))
    return bucket_of(distance) == iota((buckets, 2 * TILE), 0)


def prep_body(capacity, experts, routes_ref, cot_ref, place_out, out_ref, place_ref, sem):
    rows = cot_ref.shape[0]
    chosen = routes_ref[...]
    hot = chosen == iota((experts, rows), 0)
    above = (iota((rows, rows), 0) < iota((rows, rows), 1)).astype(F32).astype(BF)
    earlier = mm(hot.astype(F32).astype(BF), above)
    ordinal = jnp.sum(jnp.where(hot, earlier, 0.0), axis=0, keepdims=True)
    slot = chosen * capacity + ordinal.astype(jnp.int32)
    place = (slot == iota((experts * capacity, rows), 0)).astype(F32).astype(BF)
    place_ref[...] = place
    store = pltpu.make_async_copy(place_ref, place_out, sem)
    store.start()
    out_ref[...] = mm(place, cot_ref[...]).astype(BF)
    store.wait()


def attend_body(
    half_ref, lengths_ref, x_ref, x_other_ref, gain_ref, w_ref, bias_ref, w_out_ref,
    own_ref, other_ref, context_out, qkv_out, probs_out, normed_out,
    w_vmem, w_out_vmem, context_ref, qkv_ref, probs_ref, normed_ref, mask_ref, load_sems, store_sems,
):
    loads = fetch(
        [w_ref.at[c] for c in range(3)] + [w_out_ref],
        [w_vmem.at[c] for c in range(3)] + [w_out_vmem],
        load_sems,
    )
    stores = []

    def store(source, target):
        stores.append(pltpu.make_async_copy(source, target, store_sems.at[len(stores)]))
        stores[-1].start()

    group = normed_ref.shape[0]
    rows = own_ref.shape[0]
    local = w_ref.shape[2]
    heads = local // HEAD
    blocks = group // TILE
    own_at = pl.multiple_of(half_ref[0] * rows, rows)
    other_at = pl.multiple_of((1 - half_ref[0]) * rows, rows)
    for ref, at in ((x_ref, own_at), (x_other_ref, other_at)):
        x = ref[...].astype(F32)
        factor = lax.rsqrt(jnp.mean(x * x, axis=-1, keepdims=True) + epsilon)
        normed_ref[pl.ds(at, rows), :] = (x * factor * gain_ref[...].astype(F32)).astype(BF)
    normed = normed_ref[...]
    store(normed_ref, normed_out)
    for c in range(3):
        loads[c].wait()
        qkv_ref[:, c * local : (c + 1) * local] = mm(normed, w_vmem[c]).astype(BF)
    store(qkv_ref, qkv_out)
    buckets = bias_ref.shape[1]
    tables = {
        delta: mm(bias_ref[...], distance_hot(buckets, delta).astype(F32).astype(BF))
        for delta in (-1, 0, 1)
    }
    bias = bias_ref[...].astype(F32)
    far = {-1: bias[:, halfway - 1 : halfway], 1: bias[:, 2 * halfway - 1 : 2 * halfway]}
    segment_rows = jnp.zeros((group, 1), jnp.int32)
    segment_lanes = jnp.zeros((1, group), jnp.int32)
    border = jnp.int32(0)
    for s in range(lengths_ref.shape[1]):
        border = border + lengths_ref[0, s]
        segment_rows = segment_rows + (iota((group, 1), 0) >= border).astype(jnp.int32)
        segment_lanes = segment_lanes + (iota((1, group), 1) >= border).astype(jnp.int32)
    mask_ref[...] = jnp.where(segment_rows == segment_lanes, 0.0, -1e30)
    for h in range(heads):
        lo = h * HEAD
        keys = qkv_ref[:, local + lo : local + lo + HEAD]
        values = qkv_ref[:, 2 * local + lo : 2 * local + lo + HEAD]
        bands = []
        for delta in range(1 - blocks, blocks):
            if abs(delta) > 1:
                value = far[1 if delta > 0 else -1][h : h + 1]
                bands.append(jnp.broadcast_to(value, (TILE, TILE)))
            else:
                wide = jnp.broadcast_to(tables[delta][h : h + 1, :], (TILE, 2 * TILE))
                band = pltpu.roll(wide, TILE + 1, 1, stride=1, stride_axis=0)
                bands.append(band[:, :TILE])
        bias = jnp.concatenate(
            [
                jnp.concatenate([bands[k - b + blocks - 1] for k in range(blocks)], axis=1)
                for b in range(blocks)
            ],
            axis=0,
        )
        queries = qkv_ref[:, lo : lo + HEAD] * (HEAD**-0.5)
        scores = mm_nt(queries, keys) + (bias + mask_ref[...])
        exponent = jnp.exp(scores - jnp.max(scores, axis=-1, keepdims=True))
        probs = exponent * (1.0 / jnp.sum(exponent, axis=-1, keepdims=True))
        low = probs.astype(BF)
        probs_ref[h] = low
        context_ref[:, lo : lo + HEAD] = mm(low, values).astype(BF)
        store(probs_ref.at[h], probs_out.at[h])
    store(context_ref, context_out)
    loads[3].wait()
    other_ref[...] = mm(context_ref[pl.ds(other_at, rows), :], w_out_vmem[...])
    own_ref[...] = mm(context_ref[pl.ds(own_at, rows), :], w_out_vmem[...])
    for copy in stores:
        copy.wait()


def project_body(
    _expert, own_ref, other_ref, x_ref, gain_ref, router_ref, place_hbm, _after,
    out_ref, router_out, residual_out,
    place_ref, residual_ref, sems,
):
    loads = fetch([place_hbm], [place_ref], sems)
    router_out[...] = router_ref[...]
    residual = x_ref[...].astype(F32) + (own_ref[...] + other_ref[...])
    residual_ref[...] = residual
    store = pltpu.make_async_copy(residual_ref, residual_out, sems.at[1])
    store.start()
    factor = lax.rsqrt(jnp.mean(residual * residual, axis=-1, keepdims=True) + epsilon)
    moe_rows = (residual * factor * gain_ref[...].astype(F32)).astype(BF)
    loads[0].wait()
    out_ref[...] = mm(place_ref[...], moe_rows).astype(BF)
    store.wait()


def expert_body(
    half_ref, expert_ref, rows_ref, cot_ref, router_ref, up_ref, down_ref,
    back_ref, router_grad_ref, scaled_out, gp_out, send_out, act_out, pre_out,
    up_vmem, down_vmem, scaled_ref, gp_ref, send_ref, act_ref, pre_ref, out_acc, back_acc, load_sems, store_sems,
):
    steps, _, tile = up_vmem.shape
    half_steps = steps // 2
    width = rows_ref.shape[1]
    ff_half = act_ref.shape[1]
    loads = []
    for step in range(steps):
        side = 1 - half_ref[0] if step < half_steps else half_ref[0]
        at = pl.multiple_of((side * half_steps + step % half_steps) * tile, tile)
        loads.append(
            fetch(
                [up_ref.at[:, pl.ds(at, tile)], down_ref.at[pl.ds(at, tile), :]],
                [up_vmem.at[step], down_vmem.at[step]],
                load_sems.at[step],
            )
        )
    stores = []

    def store(source, target):
        stores.append(pltpu.make_async_copy(source, target, store_sems.at[len(stores)]))
        stores[-1].start()

    rows = rows_ref[...]
    logits = mm(rows, router_ref[...])
    exponent = jnp.exp(logits - jnp.max(logits, axis=-1, keepdims=True))
    chances = exponent / jnp.sum(exponent, axis=-1, keepdims=True)
    mine = iota(chances.shape, 1) == expert_ref[0]
    gating = jnp.sum(jnp.where(mine, chances, 0.0), axis=-1, keepdims=True)
    gp = (gating * cot_ref[...].astype(F32)).astype(BF)
    gp_ref[...] = gp
    store(gp_ref, gp_out)
    send_ref[:, 2 * ff_half : 2 * ff_half + width] = rows
    send_ref[:, 2 * ff_half + width :] = gp
    for step in range(steps):
        for copy in loads[step]:
            copy.wait()
        hidden = mm(rows, up_vmem[step])
        phi = 0.5 * (1.0 + lax.erf(hidden * (2.0**-0.5)))
        act = (hidden * phi).astype(BF)
        slope = phi + hidden * (jnp.exp(-0.5 * hidden * hidden) * 0.3989422804014327)
        pre = (mm_nt(gp, down_vmem[step]) * slope).astype(BF)
        if step == 0:
            out_acc[...] = mm(act, down_vmem[step])
            back_acc[...] = mm_nt(pre, up_vmem[step])
        else:
            out_acc[...] += mm(act, down_vmem[step])
            back_acc[...] += mm_nt(pre, up_vmem[step])
        if step < half_steps:
            send_ref[:, step * tile : (step + 1) * tile] = act
            send_ref[:, ff_half + step * tile : ff_half + (step + 1) * tile] = pre
        else:
            at = (step - half_steps) * tile
            act_ref[:, at : at + tile] = act
            pre_ref[:, at : at + tile] = pre
        if step == half_steps - 1:
            store(send_ref, send_out)
    store(act_ref, act_out)
    store(pre_ref, pre_out)
    produced = out_acc[...].astype(BF).astype(F32)
    scaled_ref[...] = (gating * produced).astype(BF)
    store(scaled_ref, scaled_out)
    grad_gate = jnp.sum(cot_ref[...].astype(F32) * produced, axis=-1, keepdims=True)
    grad_logits = gating * (mine.astype(F32) - chances) * grad_gate
    low = grad_logits.astype(BF)
    rest = (grad_logits - low.astype(F32)).astype(BF)
    back = back_acc[...] + (mm_nt(low, router_ref[...]) + mm_nt(rest, router_ref[...]))
    back_ref[...] = back.astype(BF)
    router_grad_ref[...] = mm_tn(low, rows) + mm_tn(rest, rows)
    for copy in stores:
        copy.wait()


def expert_grads_body(
    act_ref, pre_ref, rows_ref, gp_ref, act2_ref, pre2_ref, rows2_ref, gp2_ref, down_ref, up_ref
):
    down_ref[...] = mm_tn(act_ref[...], gp_ref[...]) + mm_tn(act2_ref[...], gp2_ref[...])
    up_ref[...] = mm_tn(rows_ref[...], pre_ref[...]) + mm_tn(rows2_ref[...], pre2_ref[...])


def norm_back(grad, source, gain):
    factor = lax.rsqrt(jnp.mean(source * source, axis=-1, keepdims=True) + epsilon)
    unit = source * factor
    scaled = grad * gain
    inner = jnp.mean(scaled * unit, axis=-1, keepdims=True)
    return factor * (scaled - unit * inner), grad * unit


def moe_back_body(
    place_hbm, back_ref, residual_hbm, gain_ref, cot_hbm, _scaled, _after,
    low_ref, gain_grad_ref, grad_out, _passed,
    place_ref, residual_ref, cot_ref, grad_ref, sems,
):
    loads = fetch([place_hbm, residual_hbm, cot_hbm], [place_ref, residual_ref, cot_ref], sems)
    loads[0].wait()
    grad_in = mm_tn(place_ref[...], back_ref[...])
    loads[1].wait()
    passed, terms = norm_back(grad_in, residual_ref[...], gain_ref[...].astype(F32))
    loads[2].wait()
    grad = cot_ref[...].astype(F32) + passed
    grad_ref[...] = grad
    store = pltpu.make_async_copy(grad_ref, grad_out, sems.at[3])
    store.start()
    low_ref[...] = grad.astype(BF)
    gain_grad_ref[...] = jnp.sum(terms, axis=0, keepdims=True)
    store.wait()


def fold_diagonals(squares):
    wide = jnp.concatenate([squares, jnp.zeros_like(squares)], axis=2)
    count = TILE
    while count > 8:
        count //= 2
        wide = wide[:, :count] + pltpu.roll(wide[:, count:], 2 * TILE - count, 2)
    return wide


def attend_back_body(
    half_ref, bits_ref, grad_own_ref, grad_other_ref, w_out_hbm, qkv_hbm, probs_hbm, context_hbm, normed_hbm,
    folded_ref, edge_ref, a0_out, a1_out, a2_out, a3_out, c0_out, c2_out, near_out, gqkv_out,
    a0_ref, a1_ref, a2_ref, a3_ref, c0_ref, c1_ref, c2_ref, c3_ref,
    gqkv_ref, gctx_ref, grad_ref, kv_ref, band_ref,
    w_out_ref, qkv_ref, probs_ref, context_ref, normed_ref, sems, store_sems,
):
    heads = probs_ref.shape[0]
    w_out_in, qkv_in, *probs_in = fetch(
        [w_out_hbm, qkv_hbm] + [probs_hbm.at[h] for h in range(heads)],
        [w_out_ref, qkv_ref] + [probs_ref.at[h] for h in range(heads)],
        sems,
    )
    context_in, normed_in = fetch(
        [context_hbm, normed_hbm], [context_ref, normed_ref], sems.at[pl.ds(2 + heads, 2)]
    )
    stores = []

    def store(source, target):
        stores.append(pltpu.make_async_copy(source, target, store_sems.at[len(stores)]))
        stores[-1].start()

    group, width = normed_ref.shape
    rows = grad_own_ref.shape[0]
    local = context_ref.shape[1]
    blocks = group // TILE
    own_at = pl.multiple_of(half_ref[0] * rows, rows)
    other_at = pl.multiple_of((1 - half_ref[0]) * rows, rows)
    grad_ref[pl.ds(own_at, rows), :] = grad_own_ref[...]
    grad_ref[pl.ds(other_at, rows), :] = grad_other_ref[...]
    grad = grad_ref[...]
    w_out_in.wait()
    gctx_ref[...] = mm_nt(grad, w_out_ref[...]).astype(BF)
    qkv_in.wait()
    scale = HEAD**-0.5
    buckets = 2 * halfway
    edges = [[], []]
    for h in range(heads):
        lo = h * HEAD
        queries = qkv_ref[:, lo : lo + HEAD]
        keys = qkv_ref[:, local + lo : local + lo + HEAD]
        values = qkv_ref[:, 2 * local + lo : 2 * local + lo + HEAD]
        gctx = gctx_ref[:, lo : lo + HEAD]
        if h == 0:
            context_in.wait()
        terms = gctx.astype(F32) * context_ref[:, lo : lo + HEAD].astype(F32)
        inner = jnp.sum(terms, axis=-1, keepdims=True)
        grad_probs = mm_nt(gctx, values)
        probs_in[h].wait()
        low_probs = probs_ref[h]
        grad_scores = low_probs.astype(F32) * (grad_probs - inner)
        low = grad_scores.astype(BF)
        gqkv_ref[:, lo : lo + HEAD] = (mm(low, keys) * scale).astype(BF)
        kv_ref[lo : lo + HEAD, :] = mm_tn(queries, low) * scale
        kv_ref[local + lo : local + lo + HEAD, :] = mm_tn(gctx, low_probs)
        for number, delta in enumerate((-1, 0, 1)):
            band = None
            for b in range(blocks):
                k = b + delta
                if 0 <= k < blocks:
                    piece = grad_scores[
                        b * TILE : (b + 1) * TILE, k * TILE : (k + 1) * TILE
                    ]
                    band = piece if band is None else band + piece
            band_ref[number * heads + h] = band
        for number, sign in enumerate((-1, 1)):
            total = jnp.zeros((1, 1), F32)
            for b in range(blocks):
                for k in range(blocks):
                    if (k - b) * sign > 1:
                        piece = grad_scores[
                            b * TILE : (b + 1) * TILE, k * TILE : (k + 1) * TILE
                        ]
                        total = total + jnp.sum(
                            jnp.sum(piece, axis=0, keepdims=True), axis=1, keepdims=True
                        )
            edges[number].append(total)
    gqkv_ref[:, local : 2 * local] = kv_ref[:local].T.astype(BF)
    gqkv_ref[:, 2 * local :] = kv_ref[local:].T.astype(BF)
    plane, depth = bits_ref[0], bits_ref[1]
    shard = width // 16
    half = width // 2
    targets = (c0_ref, c1_ref, c2_ref, c3_ref)
    dense = mm_tn(context_ref[...], grad).astype(BF)
    for a in range(2):
        for z in range(2):
            for number, target in enumerate(targets):

                @pl.when((depth ^ (2 * a + z)) == number)
                def _(target=target, dense=dense, a=a, z=z):
                    rows_of = slice(z * 4 * shard, (z + 1) * 4 * shard)
                    target[...] = dense[rows_of, a * half : (a + 1) * half]
    size = 4 * shard
    outs = (c0_out, near_out.at[pl.ds(0, size), :], c2_out, near_out.at[pl.ds(size, size), :])
    for target, out in zip(targets, outs):
        store(target, out)
    normed_in.wait()
    targets = (a0_ref, a1_ref, a2_ref, a3_ref)
    dense = mm_tn(normed_ref[...], gqkv_ref[...]).astype(BF)
    for p in range(4):
        for number, target in enumerate(targets):

            @pl.when((plane ^ p) == number)
            def _(target=target, p=p):
                for z in range(4):
                    piece = dense[(p * 4 + z) * shard : (p * 4 + z + 1) * shard]
                    at = pl.multiple_of((depth ^ z) * shard, shard)
                    target[pl.ds(at, shard), :] = piece
    for target, out in zip(targets, (a0_out, a1_out, a2_out, a3_out)):
        store(target, out)
    store(gqkv_ref, gqkv_out)
    folded_ref[...] = fold_diagonals(band_ref[...])
    for number in range(2):
        for h in range(heads):
            edge_ref[h : h + 1, number * TILE : (number + 1) * TILE] = jnp.broadcast_to(
                edges[number][h], (1, TILE)
            )
    for copy in stores:
        copy.wait()


def small_grads_body(
    half_ref, folded_ref, edge_ref, router_grad_ref, moe_gain_grad_ref, gqkv_hbm, w_hbm, x_hbm, x_other_hbm,
    _after, small_ref, own_ref, other_ref,
    gqkv_ref, w_ref, x_ref, x_other_ref, all_ref, sems,
):
    loads = fetch([gqkv_hbm, w_hbm, x_hbm, x_other_hbm], [gqkv_ref, w_ref, x_ref, x_other_ref], sems)
    rows, width = own_ref.shape
    local = w_ref.shape[2]
    heads = local // HEAD
    buckets = 2 * halfway
    own_at = pl.multiple_of(half_ref[0] * rows, rows)
    other_at = pl.multiple_of((1 - half_ref[0]) * rows, rows)
    folded = folded_ref[...]
    spread = jnp.zeros((heads * 8, 8 * buckets), F32)
    for number, delta in enumerate((-1, 0, 1)):
        distance = iota((8, 2 * TILE), 1) - iota((8, 2 * TILE), 0)
        distance = jnp.where(distance >= TILE, distance - 2 * TILE, distance) + TILE * delta
        bucket = bucket_of(distance)
        hot = jnp.concatenate(
            [bucket[r : r + 1] == iota((buckets, 2 * TILE), 0) for r in range(8)], axis=0
        )
        hot = hot.astype(F32).astype(BF)
        sums = folded[number * heads : (number + 1) * heads].reshape(heads * 8, 2 * TILE)
        for _ in range(3):
            low = sums.astype(BF)
            spread = spread + mm_nt(low, hot)
            sums = sums - low.astype(F32)
    same = iota(spread.shape, 0) % 8 == iota(spread.shape, 1) // buckets
    table = jnp.sum(jnp.where(same, spread, 0.0).reshape(heads, 8, 8 * buckets), axis=1)
    step = 4 * buckets
    while step >= buckets:
        table = table + pltpu.roll(table, step, 1)
        step //= 2
    table = table[:, :buckets]
    table = jnp.concatenate([table, jnp.zeros((8 - heads, buckets), F32)], axis=0)
    for number, bucket in enumerate((halfway - 1, 2 * halfway - 1)):
        column = jnp.concatenate(
            [edge_ref[:heads, number * TILE : number * TILE + 1], jnp.zeros((8 - heads, 1), F32)], axis=0
        )
        table = table + jnp.where(iota((8, buckets), 1) == bucket, column, 0.0)
    for copy in loads:
        copy.wait()
    total = None
    for c in range(3):
        part = mm_nt(gqkv_ref[:, c * local : (c + 1) * local], w_ref[c])
        total = part if total is None else total + part
    all_ref[...] = total
    own_ref[...] = all_ref[pl.ds(own_at, rows), :]
    other_ref[...] = all_ref[pl.ds(other_at, rows), :]
    gain_grad = jnp.zeros((1, width), F32)
    for ref, part in ((x_ref, own_ref), (x_other_ref, other_ref)):
        x = ref[...].astype(F32)
        factor = lax.rsqrt(jnp.mean(x * x, axis=-1, keepdims=True) + epsilon)
        gain_grad = gain_grad + jnp.sum(part[...] * (x * factor), axis=0, keepdims=True)
    moe_gain_grad = moe_gain_grad_ref[...]
    row = iota((16, local), 0)
    extra = jnp.concatenate([table, jnp.zeros((8, local - buckets), F32)], axis=1)
    extra = jnp.concatenate([jnp.zeros((8, local), F32), extra], axis=0)
    for number, value in enumerate((moe_gain_grad, gain_grad)):
        for part in range(2):
            piece = value[:, part * local : (part + 1) * local]
            extra = extra + jnp.where(row == 2 * number + part, piece, 0.0)
    small = jnp.concatenate(
        [router_grad_ref[:, :local], router_grad_ref[:, local:], extra], axis=0
    ).astype(BF)
    small_ref[...] = small


def order_body(_value, _after, _out):
    pass


def total_of(*values):
    return functools.reduce(jnp.add, [v.astype(F32) for v in values]).astype(BF)


def pairs_of(a, b, c, d):
    return ((a.astype(F32) + b.astype(F32)) + (c.astype(F32) + d.astype(F32))).astype(BF)


def fold_near_body(got_ref, c0_hbm, c2_hbm, c0_out, c2_out, c0_ref, c2_ref, sems):
    for copy in fetch([c0_hbm, c2_hbm], [c0_ref, c2_ref], sems):
        copy.wait()
    size = c0_ref.shape[0]
    c0_out[...] = total_of(c0_ref[...], got_ref[:size])
    c2_out[...] = total_of(c2_ref[...], got_ref[size:])


def fold_first_body(
    a1_ref, a2_ref, a3_ref, c0_ref, got_ref, a0_hbm, small_ref,
    s0_ref, s1_ref, s2_ref, s3_ref, e_ref,
    a0_ref, sem,
):
    load = pltpu.make_async_copy(a0_hbm, a0_ref, sem)
    load.start()
    load.wait()
    shard, lead = s0_ref.shape[0], small_ref.shape[0]
    for d, target in enumerate((s0_ref, s1_ref, s2_ref, s3_ref)):
        at = slice(d * shard, (d + 1) * shard)
        target[...] = pairs_of(a0_ref[at], a1_ref[at], a2_ref[at], a3_ref[at])
    e_ref[:lead] = small_ref[...]
    e_ref[lead:] = total_of(c0_ref[...], got_ref[...])


def fold_last_body(
    s0_ref, s1_ref, s2_ref, s3_ref, e0_ref, e1_ref, e2_ref, e3_ref, total_ref, c_ref, small_ref
):
    lead = small_ref.shape[0]
    total_ref[...] = pairs_of(s0_ref[...], s1_ref[...], s2_ref[...], s3_ref[...])
    small_ref[...] = pairs_of(e0_ref[:lead], e1_ref[:lead], e2_ref[:lead], e3_ref[:lead])
    c_ref[...] = pairs_of(e0_ref[lead:], e1_ref[lead:], e2_ref[lead:], e3_ref[lead:])


def join_body(shared, t0_ref, t1_ref, t2_ref, t3_ref, c_ref, small_ref, other_ref, _after, mine_ref, c_mine_ref):
    shard, size = t0_ref.shape[0], c_ref.shape[0]
    for d, ref in enumerate((t0_ref, t1_ref, t2_ref, t3_ref)):
        mine_ref[d * shard : (d + 1) * shard] = ref[...]
    c_mine_ref[:size] = c_ref[...]
    own = small_ref[...].astype(F32)
    both = own + other_ref[...].astype(F32)
    c_mine_ref[size:] = jnp.where(iota(own.shape, 0) < shared, both, own).astype(BF)


def stack_body(a_ref, b_ref, out_ref):
    size = a_ref.shape[0]
    out_ref[:size] = a_ref[...]
    out_ref[size:] = b_ref[...]


def tokens_body(
    place_ref, scaled_ref, residual_ref, own_ref, got_ref, x_ref, gain_ref, grad_res_ref, _after, out_ref, grad_ref
):
    out_ref[...] = (residual_ref[...] + mm_tn(place_ref[...], scaled_ref[...])).astype(BF)
    passed, _ = norm_back(
        own_ref[...] + got_ref[...], x_ref[...].astype(F32), gain_ref[...].astype(F32)
    )
    grad_ref[...] = grad_res_ref[...] + passed


def unpack_body(
    bits_ref, a0_ref, a1_ref, a2_ref, a3_ref, c0_ref, c2_ref, near_ref,
    router_ref, norm_gain_ref, moe_gain_ref, bias_ref, qkv_out, w_out_out,
    wide_ref, w_out_ref, qkv_sems, out_sems,
):
    local = qkv_out.shape[2]
    shard = a0_ref.shape[0] // 4
    plane, depth = bits_ref[0], bits_ref[1]
    copies = []
    for number, ref in enumerate((a0_ref, a1_ref, a2_ref, a3_ref)):
        quarter = plane ^ number
        wide_ref[number] = ref[...].astype(F32)
        for d in range(4):
            at = pl.multiple_of((quarter * 4 + (depth ^ d)) * shard, shard)
            for c in range(3):
                copy = pltpu.make_async_copy(
                    wide_ref.at[number, pl.ds(d * shard, shard), pl.ds(c * local, local)],
                    qkv_out.at[c, pl.ds(at, shard), :],
                    qkv_sems.at[number, d, c],
                )
                copy.start()
                copies.append(copy)
    size = c0_ref.shape[0]
    others = (c0_ref, near_ref.at[:size], c2_ref, near_ref.at[size:])
    for number, ref in enumerate(others):
        w_out_ref[number] = ref[: 4 * shard].astype(F32)
        slab = depth ^ number
        lane = pl.multiple_of((slab // 2) * local, local)
        at = pl.multiple_of((slab % 2) * 4 * shard, 4 * shard)
        copy = pltpu.make_async_copy(
            w_out_ref.at[number], w_out_out.at[pl.ds(at, 4 * shard), pl.ds(lane, local)], out_sems.at[number]
        )
        copy.start()
        copies.append(copy)
    parts = [ref[4 * shard :].astype(F32) for ref in others]
    small = (parts[0] + parts[1]) + (parts[2] + parts[3])
    experts = router_ref.shape[0]
    router_ref[:, :local] = small[:experts]
    router_ref[:, local:] = small[experts : 2 * experts]
    rest = small[2 * experts :]
    for number, ref in enumerate((moe_gain_ref, norm_gain_ref)):
        ref[:local] = rest[2 * number]
        ref[local:] = rest[2 * number + 1]
    bias_ref[...] = rest[8 : 8 + bias_ref.shape[0], : bias_ref.shape[1]]
    for copy in copies:
        copy.wait()


def per_device(
    tokens, lengths, routes, norm_gain, w_qkv, rel_bias, w_out, moe_gain, w_router, w_in, w_down, cotangent
):
    rows, width = tokens.shape
    sources = lax.axis_size("expert")
    group = rows * lax.axis_size("tensor")
    experts = w_router.shape[1]
    capacity = max(2, 4 * rows // (3 * experts))
    slots = experts * capacity
    local = w_qkv.shape[2]
    heads = local // HEAD
    buckets = rel_bias.shape[0]
    ff = w_in.shape[2]
    ff_half = ff // 2
    half = lax.axis_index("tensor").astype(jnp.int32)
    expert = lax.axis_index("expert").astype(jnp.int32)
    half_one = half.reshape(1)
    gain_a = norm_gain.reshape(1, width)
    gain_b = moe_gain.reshape(1, width)

    def swap(value):
        return lax.ppermute(value, "tensor", [(0, 1), (1, 0)])

    def exchange(value):
        return lax.all_to_all(
            value.reshape(experts, capacity, width), "expert", split_axis=0, concat_axis=0, tiled=True
        ).reshape(slots, width)

    x_other = swap(tokens)
    place, cot_slots = pl.pallas_call(
        functools.partial(prep_body, capacity, experts),
        out_shape=(hbm((slots, rows), BF),) + shape_of(((slots, width), BF)),
        in_specs=vmem_specs(2),
        out_specs=[ANY] + vmem_specs(1),
        scratch_shapes=[pltpu.VMEM((slots, rows), BF), pltpu.SemaphoreType.DMA],
        cost_estimate=cost(2e9, 1e6),
        name="place_cotangent",
    )(routes.reshape(1, rows), cotangent)
    cot_rows = exchange(cot_slots)

    bias_rows = jnp.pad(rel_bias.T, ((0, 8 - heads), (0, 0)))
    own_sum, other_sum, context, qkv, probs, normed = pl.pallas_call(
        attend_body,
        out_shape=shape_of(((rows, width), F32), ((rows, width), F32))
        + (
            hbm((group, local), BF),
            hbm((group, 3 * local), BF),
            hbm((heads, group, group), BF),
            hbm((group, width), BF),
        ),
        in_specs=[SMEM, SMEM] + vmem_specs(3) + [ANY] + vmem_specs(1) + [ANY],
        out_specs=vmem_specs(2) + [ANY] * 4,
        scratch_shapes=[
            pltpu.VMEM((3, width, local), BF),
            pltpu.VMEM((local, width), BF),
            pltpu.VMEM((group, local), BF),
            pltpu.VMEM((group, 3 * local), BF),
            pltpu.VMEM((heads, group, group), BF),
            pltpu.VMEM((group, width), BF),
            pltpu.VMEM((group, group), F32),
            pltpu.SemaphoreType.DMA((4,)),
            pltpu.SemaphoreType.DMA((heads + 3,)),
        ],
        compiler_params=params(20),
        cost_estimate=cost(8e9, 4e6),
        name="attention",
    )(half_one, lengths, tokens, x_other, gain_a, in_hbm(w_qkv), bias_rows, in_hbm(w_out))
    got_sum = swap(other_sum)

    expert_one = expert.reshape(1)
    moe_slots, router, residual = pl.pallas_call(
        project_body,
        out_shape=shape_of(((slots, width), BF), ((width, experts), BF)) + (hbm((rows, width), F32),),
        in_specs=[SMEM] + vmem_specs(5) + [ANY, ANY],
        out_specs=vmem_specs(2) + [ANY],
        scratch_shapes=[
            pltpu.VMEM((slots, rows), BF),
            pltpu.VMEM((rows, width), F32),
            pltpu.SemaphoreType.DMA((2,)),
        ],
        compiler_params=params(12),
        cost_estimate=cost(2e9, 2e6),
        name="projection",
    )(expert_one, own_sum, got_sum, tokens, gain_b, w_router, in_hbm(place), cot_rows)
    stacked = exchange(moe_slots)

    count = sources * capacity
    tile = FF_TILE
    steps = ff // tile
    half_steps = steps // 2

    back, router_grad, scaled, gp, send, act, pre = pl.pallas_call(
        expert_body,
        out_shape=shape_of(((count, width), BF), ((experts, width), F32))
        + (
            hbm((count, width), BF),
            hbm((count, width), BF),
            hbm((count, 2 * ff_half + 2 * width), BF),
            hbm((count, ff_half), BF),
            hbm((count, ff_half), BF),
        ),
        in_specs=[SMEM, SMEM] + vmem_specs(3) + [ANY, ANY],
        out_specs=vmem_specs(2) + [ANY] * 5,
        scratch_shapes=[
            pltpu.VMEM((steps, width, tile), BF),
            pltpu.VMEM((steps, tile, width), BF),
            pltpu.VMEM((count, width), BF),
            pltpu.VMEM((count, width), BF),
            pltpu.VMEM((count, 2 * ff_half + 2 * width), BF),
            pltpu.VMEM((count, ff_half), BF),
            pltpu.VMEM((count, ff_half), BF),
            pltpu.VMEM((count, width), F32),
            pltpu.VMEM((count, width), F32),
            pltpu.SemaphoreType.DMA((steps, 2)),
            pltpu.SemaphoreType.DMA((5,)),
        ],
        compiler_params=params(32),
        cost_estimate=cost(10e9, 14e6),
        name="expert",
    )(half_one, expert_one, stacked, cot_rows, router, in_hbm(w_in[0]), in_hbm(w_down[0]))
    back_rows = exchange(back)
    peer = swap(send)

    col = lambda first: pl.BlockSpec((count, tile), lambda i: (0, first + i))
    fixed = lambda block: pl.BlockSpec((count, width), lambda i: (0, block))
    grad_down, grad_up = pl.pallas_call(
        expert_grads_body,
        grid=(half_steps,),
        in_specs=[
            col(0), col(0), fixed(0), fixed(0),
            col(0), col(half_steps), fixed(2 * ff_half // width), fixed(2 * ff_half // width + 1),
        ],
        out_specs=[
            pl.BlockSpec((tile, width), lambda i: (i, 0)),
            pl.BlockSpec((width, tile), lambda i: (0, i)),
        ],
        out_shape=shape_of(((ff_half, width), F32), ((width, ff_half), F32)),
        compiler_params=params(20),
        cost_estimate=cost(5e9, 14e6),
        name="expert_grads",
    )(in_hbm(act), in_hbm(pre), stacked, in_hbm(gp), *[in_hbm(peer)] * 4)

    grad_low, moe_gain_grad, grad_res, scaled_late = pl.pallas_call(
        moe_back_body,
        out_shape=shape_of(((rows, width), BF), ((1, width), F32))
        + (hbm((rows, width), F32), hbm((count, width), BF)),
        in_specs=[ANY] + vmem_specs(1) + [ANY] + vmem_specs(1) + [ANY] * 3,
        out_specs=vmem_specs(2) + [ANY, ANY],
        input_output_aliases={5: 3},
        scratch_shapes=[
            pltpu.VMEM((slots, rows), BF),
            pltpu.VMEM((rows, width), F32),
            pltpu.VMEM((rows, width), BF),
            pltpu.VMEM((rows, width), F32),
            pltpu.SemaphoreType.DMA((4,)),
        ],
        compiler_params=params(12),
        cost_estimate=cost(1e9, 2e6),
        name="norm_back",
    )(in_hbm(place), back_rows, in_hbm(residual), gain_b, in_hbm(cotangent), scaled, in_hbm(grad_down))
    grad_other = swap(grad_low)
    scaled_rows = exchange(scaled_late)

    position = jnp.stack([expert & 3, (expert >> 2) & 3])
    shard = width // 16
    lead = 2 * experts + 16
    big, slab = (4 * shard, 3 * local), (4 * shard, local)
    folded, edges, a0, a1, a2, a3, c0, c2, c_near, grad_joined = pl.pallas_call(
        attend_back_body,
        out_shape=(
            *shape_of(((3 * heads, 8, 2 * TILE), F32), ((8, 2 * TILE), F32)),
            *[hbm(big, BF)] * 4, *[hbm(slab, BF)] * 2, hbm((8 * shard, local), BF), hbm((group, 3 * local), BF),
        ),
        in_specs=[SMEM, SMEM] + vmem_specs(2) + [ANY] * 5,
        out_specs=vmem_specs(2) + [ANY] * 8,
        scratch_shapes=[pltpu.VMEM(big, BF)] * 4
        + [pltpu.VMEM(slab, BF)] * 4
        + [
            pltpu.VMEM((group, 3 * local), BF),
            pltpu.VMEM((group, local), BF),
            pltpu.VMEM((group, width), BF),
            pltpu.VMEM((2 * local, group), F32),
            pltpu.VMEM((3 * heads, TILE, TILE), F32),
            pltpu.VMEM((local, width), BF),
            pltpu.VMEM((group, 3 * local), BF),
            pltpu.VMEM((heads, group, group), BF),
            pltpu.VMEM((group, local), BF),
            pltpu.VMEM((group, width), BF),
            pltpu.SemaphoreType.DMA((4 + heads,)),
            pltpu.SemaphoreType.DMA((9,)),
        ],
        compiler_params=params(32),
        cost_estimate=cost(10e9, 10e6),
        name="attention_back",
    )(
        half_one, position, grad_low, grad_other, in_hbm(w_out), in_hbm(qkv), in_hbm(probs), in_hbm(context),
        in_hbm(normed),
    )
    a1 = pl.pallas_call(
        order_body,
        out_shape=hbm(a1.shape, BF),
        in_specs=[ANY, ANY],
        out_specs=ANY,
        input_output_aliases={0: 0},
        name="order",
    )(a1, scaled_rows)

    def moves(flip):
        pairs = [(2 * e + t, 2 * (e ^ flip) + t) for e in range(sources) for t in range(2)]
        return lambda value: lax.ppermute(value, ("expert", "tensor"), pairs)

    flat = [moves(d) for d in range(1, 4)]
    along = [moves(4 * d) for d in range(1, 4)]

    def add(*values):
        return functools.reduce(jnp.add, [v.astype(F32) for v in values]).astype(BF)

    def fused(name, body, shapes, values, before=(), mib=8):
        return pl.pallas_call(
            body,
            out_shape=[jax.ShapeDtypeStruct(shape, dtype) for shape, dtype in shapes],
            in_specs=vmem_specs(len(values)) + [ANY] * len(before),
            out_specs=vmem_specs(len(shapes)),
            compiler_params=params(mib),
            cost_estimate=cost(1e3, 1e3),
            name=name,
        )(*values, *before)

    quarter = 4 * shard
    wide = 3 * local
    got_a = [flat[d](a) for d, a in enumerate((a1, a2, a3))]
    c0, c2 = pl.pallas_call(
        fold_near_body,
        out_shape=shape_of(*[(slab, BF)] * 2),
        in_specs=vmem_specs(1) + [ANY] * 2,
        out_specs=vmem_specs(2),
        scratch_shapes=[pltpu.VMEM(slab, BF)] * 2 + [pltpu.SemaphoreType.DMA((2,))],
        compiler_params=params(8),
        cost_estimate=cost(1e3, 1e3),
        name="fold_near",
    )(along[0](c_near), in_hbm(c0), in_hbm(c2))
    got_c = along[1](c2)
    small, own_gn, other_gn = pl.pallas_call(
        small_grads_body,
        out_shape=shape_of(((lead, local), BF), ((rows, width), F32), ((rows, width), F32)),
        in_specs=[SMEM] + vmem_specs(4) + [ANY] * 5,
        out_specs=vmem_specs(3),
        scratch_shapes=[
            pltpu.VMEM((group, 3 * local), BF),
            pltpu.VMEM((3, width, local), BF),
            pltpu.VMEM((rows, width), BF),
            pltpu.VMEM((rows, width), BF),
            pltpu.VMEM((group, width), F32),
            pltpu.SemaphoreType.DMA((4,)),
        ],
        compiler_params=params(16),
        cost_estimate=cost(1e3, 1e3),
        name="small_grads",
    )(
        half_one, folded, edges, router_grad, moe_gain_grad, in_hbm(grad_joined), in_hbm(w_qkv), in_hbm(tokens),
        in_hbm(x_other), c0,
    )
    got_gn = swap(other_gn)
    output, grad_tokens = pl.pallas_call(
        tokens_body,
        out_shape=shape_of(((rows, width), BF), ((rows, width), F32)),
        in_specs=vmem_specs(8) + [ANY],
        out_specs=vmem_specs(2),
        compiler_params=params(12),
        cost_estimate=cost(1e3, 1e3),
        name="token_outputs",
    )(place, scaled_rows, residual, own_gn, got_gn, tokens, gain_a, grad_res, c0)

    *parts_z, part_c = pl.pallas_call(
        fold_first_body,
        out_shape=shape_of(*[((shard, wide), BF)] * 4, ((lead + 4 * shard, local), BF)),
        in_specs=vmem_specs(5) + [ANY] + vmem_specs(1),
        out_specs=vmem_specs(5),
        scratch_shapes=[pltpu.VMEM(big, BF), pltpu.SemaphoreType.DMA],
        compiler_params=params(8),
        cost_estimate=cost(1e3, 1e3),
        name="fold_first",
    )(*got_a, c0, got_c, in_hbm(a0), small)
    got_z = [along[d](parts_z[d + 1]) for d in range(3)]
    got_e = [flat[d](part_c) for d in range(3)]
    total, c_full, small = fused(
        "fold_last",
        fold_last_body,
        [((shard, wide), BF), (slab, BF), ((lead, local), BF)],
        (parts_z[0], *got_z, part_c, *got_e),
    )
    for b in range(4, sources.bit_length() - 1):
        further = moves(1 << b)
        total = add(total, further(total))
        c_full = add(c_full, further(c_full))
        small = add(small, further(small))

    others = [along[d](total) for d in range(3)]
    mine, c_mine = fused(
        "join",
        functools.partial(join_body, 2 * experts + 8),
        [((quarter, wide), BF), ((quarter + lead, local), BF)],
        (total, *others, c_full, small, swap(small)),
        (grad_tokens,),
    )
    all_mine = [mine] + [flat[d](mine) for d in range(3)]
    c_far = along[1](c_mine)
    (c_two,) = fused("stack", stack_body, [((2 * (quarter + lead), local), BF)], (c_mine, c_far))
    c_near = along[0](c_two)
    grad_router, grad_norm_gain, grad_moe_gain, grad_rel, grad_qkv, grad_out = pl.pallas_call(
        unpack_body,
        out_shape=shape_of(
            ((experts, width), F32), ((width,), F32), ((width,), F32), ((heads, buckets), F32)
        )
        + (hbm((3, width, local), F32), hbm((local, width), F32)),
        in_specs=[SMEM] + vmem_specs(7),
        out_specs=vmem_specs(4) + [ANY] * 2,
        scratch_shapes=[
            pltpu.VMEM((4, quarter, wide), F32),
            pltpu.VMEM((4, quarter, local), F32),
            pltpu.SemaphoreType.DMA((4, 4, 3)),
            pltpu.SemaphoreType.DMA((4,)),
        ],
        compiler_params=params(12),
        cost_estimate=cost(1e3, 1e3),
        name="unpack",
    )(position, *all_mine, c_mine, c_far, c_near)

    return (
        output,
        grad_tokens,
        grad_norm_gain,
        grad_qkv,
        grad_rel.T,
        grad_out,
        grad_moe_gain,
        grad_router.T,
        grad_up[None],
        grad_down[None],
    )


def solution(mesh):
    return jax.shard_map(
        per_device,
        mesh=mesh,
        in_specs=(
            P(("expert", "tensor"), None),
            P("expert", None),
            P(("expert", "tensor"), None),
            P(),
            P(None, None, "tensor"),
            P(None, "tensor"),
            P("tensor", None),
            P(),
            P(),
            P("expert", None, None),
            P("expert", None, None),
            P(("expert", "tensor"), None),
        ),
        out_specs=(
            P(("expert", "tensor"), None),
            P(("expert", "tensor"), None),
            P(),
            P(None, None, "tensor"),
            P(None, "tensor"),
            P("tensor", None),
            P(),
            P(),
            P("expert", None, "tensor"),
            P("expert", "tensor", None),
        ),
        check_vma=False,
    )
```

```python
import functools

import jax
import jax.numpy as jnp
from jax import lax
from jax.experimental import pallas as pl
from jax.experimental.pallas import tpu as pltpu
from jax.sharding import PartitionSpec as P

HEAD = 64
TILE = 128
FF_TILE = 512

epsilon = 1e-06
THRESHOLDS = (1, 2, 3, 4, 5, 6, 7, 8, 12, 16, 23, 32, 46, 64, 91)
halfway = 16
BF = jnp.bfloat16
F32 = jnp.float32
HIGH = lax.Precision.HIGHEST
MIB = 1 << 20


def mm(a, b):
    return lax.dot_general(a, b, (((1,), (0,)), ((), ())), preferred_element_type=F32)


def mm_nt(a, b):
    return lax.dot_general(a, b, (((1,), (1,)), ((), ())), preferred_element_type=F32)


def mm_tn(a, b):
    return lax.dot_general(a, b, (((0,), (0,)), ((), ())), preferred_element_type=F32)


def iota(shape, dim):
    return lax.broadcasted_iota(jnp.int32, shape, dim)


def vmem_specs(count):
    return [pl.BlockSpec(memory_space=pltpu.VMEM)] * count


SMEM = pl.BlockSpec(memory_space=pltpu.SMEM)


def shape_of(*pairs):
    return tuple(jax.ShapeDtypeStruct(shape, dtype) for shape, dtype in pairs)


ANY = pl.BlockSpec(memory_space=pl.ANY)


def params(mib):
    return pltpu.CompilerParams(vmem_limit_bytes=mib * MIB)


def hbm(shape, dtype):
    return pltpu.HBM(shape, dtype)


def in_hbm(value):
    return pltpu.with_memory_space_constraint(value, pltpu.HBM)


def fetch(sources, targets, sems):
    copies = []
    for number, (source, target) in enumerate(zip(sources, targets, strict=True)):
        copies.append(pltpu.make_async_copy(source, target, sems.at[number]))
        copies[-1].start()
    return copies


def cost(flops, loaded):
    return pl.CostEstimate(flops=int(flops), bytes_accessed=int(loaded), transcendentals=0)


def bucket_of(distance):
    magnitude = jnp.abs(distance)
    bucket = jnp.zeros(distance.shape, jnp.int32)
    for border in THRESHOLDS:
        bucket = bucket + (magnitude >= border).astype(jnp.int32)
    return bucket + jnp.where(distance > 0, halfway, 0).astype(jnp.int32)


def distance_hot(buckets, delta):
    distance = iota((buckets, 2 * TILE), 1) + (TILE * delta - (TILE - 1))
    return bucket_of(distance) == iota((buckets, 2 * TILE), 0)


def prep_body(capacity, experts, routes_ref, cot_ref, place_out, out_ref, place_ref, sem):
    rows = cot_ref.shape[0]
    chosen = routes_ref[...]
    hot = chosen == iota((experts, rows), 0)
    above = (iota((rows, rows), 0) < iota((rows, rows), 1)).astype(F32).astype(BF)
    earlier = mm(hot.astype(F32).astype(BF), above)
    ordinal = jnp.sum(jnp.where(hot, earlier, 0.0), axis=0, keepdims=True)
    slot = chosen * capacity + ordinal.astype(jnp.int32)
    place = (slot == iota((experts * capacity, rows), 0)).astype(F32).astype(BF)
    place_ref[...] = place
    store = pltpu.make_async_copy(place_ref, place_out, sem)
    store.start()
    out_ref[...] = mm(place, cot_ref[...]).astype(BF)
    store.wait()


def attend_body(
    half_ref, lengths_ref, x_ref, x_other_ref, gain_ref, w_ref, bias_ref, w_out_ref,
    own_ref, other_ref, context_out, qkv_out, probs_out, normed_out,
    w_vmem, w_out_vmem, context_ref, qkv_ref, probs_ref, normed_ref, mask_ref, load_sems, store_sems,
):
    loads = fetch(
        [w_ref.at[c] for c in range(3)] + [w_out_ref],
        [w_vmem.at[c] for c in range(3)] + [w_out_vmem],
        load_sems,
    )
    stores = []

    def store(source, target):
        stores.append(pltpu.make_async_copy(source, target, store_sems.at[len(stores)]))
        stores[-1].start()

    group = normed_ref.shape[0]
    rows = own_ref.shape[0]
    local = w_ref.shape[2]
    heads = local // HEAD
    blocks = group // TILE
    own_at = pl.multiple_of(half_ref[0] * rows, rows)
    other_at = pl.multiple_of((1 - half_ref[0]) * rows, rows)
    for ref, at in ((x_ref, own_at), (x_other_ref, other_at)):
        x = ref[...].astype(F32)
        factor = lax.rsqrt(jnp.mean(x * x, axis=-1, keepdims=True) + epsilon)
        normed_ref[pl.ds(at, rows), :] = (x * factor * gain_ref[...].astype(F32)).astype(BF)
    normed = normed_ref[...]
    store(normed_ref, normed_out)
    for c in range(3):
        loads[c].wait()
        qkv_ref[:, c * local : (c + 1) * local] = mm(normed, w_vmem[c]).astype(BF)
    store(qkv_ref, qkv_out)
    buckets = bias_ref.shape[1]
    tables = {
        delta: mm(bias_ref[...], distance_hot(buckets, delta).astype(F32).astype(BF))
        for delta in (-1, 0, 1)
    }
    bias = bias_ref[...].astype(F32)
    far = {-1: bias[:, halfway - 1 : halfway], 1: bias[:, 2 * halfway - 1 : 2 * halfway]}
    segment_rows = jnp.zeros((group, 1), jnp.int32)
    segment_lanes = jnp.zeros((1, group), jnp.int32)
    border = jnp.int32(0)
    for s in range(lengths_ref.shape[1]):
        border = border + lengths_ref[0, s]
        segment_rows = segment_rows + (iota((group, 1), 0) >= border).astype(jnp.int32)
        segment_lanes = segment_lanes + (iota((1, group), 1) >= border).astype(jnp.int32)
    mask_ref[...] = jnp.where(segment_rows == segment_lanes, 0.0, -1e30)
    for h in range(heads):
        lo = h * HEAD
        keys = qkv_ref[:, local + lo : local + lo + HEAD]
        values = qkv_ref[:, 2 * local + lo : 2 * local + lo + HEAD]
        bands = []
        for delta in range(1 - blocks, blocks):
            if abs(delta) > 1:
                value = far[1 if delta > 0 else -1][h : h + 1]
                bands.append(jnp.broadcast_to(value, (TILE, TILE)))
            else:
                wide = jnp.broadcast_to(tables[delta][h : h + 1, :], (TILE, 2 * TILE))
                band = pltpu.roll(wide, TILE + 1, 1, stride=1, stride_axis=0)
                bands.append(band[:, :TILE])
        bias = jnp.concatenate(
            [
                jnp.concatenate([bands[k - b + blocks - 1] for k in range(blocks)], axis=1)
                for b in range(blocks)
            ],
            axis=0,
        )
        queries = qkv_ref[:, lo : lo + HEAD] * (HEAD**-0.5)
        scores = mm_nt(queries, keys) + (bias + mask_ref[...])
        exponent = jnp.exp(scores - jnp.max(scores, axis=-1, keepdims=True))
        probs = exponent * (1.0 / jnp.sum(exponent, axis=-1, keepdims=True))
        low = probs.astype(BF)
        probs_ref[h] = low
        context_ref[:, lo : lo + HEAD] = mm(low, values).astype(BF)
        store(probs_ref.at[h], probs_out.at[h])
    store(context_ref, context_out)
    loads[3].wait()
    other_ref[...] = mm(context_ref[pl.ds(other_at, rows), :], w_out_vmem[...])
    own_ref[...] = mm(context_ref[pl.ds(own_at, rows), :], w_out_vmem[...])
    for copy in stores:
        copy.wait()


def project_body(
    _expert, own_ref, other_ref, x_ref, gain_ref, router_ref, place_hbm, _after,
    out_ref, router_out, residual_out,
    place_ref, residual_ref, sems,
):
    loads = fetch([place_hbm], [place_ref], sems)
    router_out[...] = router_ref[...]
    residual = x_ref[...].astype(F32) + (own_ref[...] + other_ref[...])
    residual_ref[...] = residual
    store = pltpu.make_async_copy(residual_ref, residual_out, sems.at[1])
    store.start()
    factor = lax.rsqrt(jnp.mean(residual * residual, axis=-1, keepdims=True) + epsilon)
    moe_rows = (residual * factor * gain_ref[...].astype(F32)).astype(BF)
    loads[0].wait()
    out_ref[...] = mm(place_ref[...], moe_rows).astype(BF)
    store.wait()


def expert_body(
    half_ref, expert_ref, rows_ref, cot_ref, router_ref, up_ref, down_ref,
    back_ref, router_grad_ref, scaled_out, gp_out, send_out, act_out, pre_out,
    up_vmem, down_vmem, scaled_ref, gp_ref, send_ref, act_ref, pre_ref, out_acc, back_acc, load_sems, store_sems,
):
    steps, _, tile = up_vmem.shape
    half_steps = steps // 2
    width = rows_ref.shape[1]
    ff_half = act_ref.shape[1]
    loads = []
    for step in range(steps):
        side = 1 - half_ref[0] if step < half_steps else half_ref[0]
        at = pl.multiple_of((side * half_steps + step % half_steps) * tile, tile)
        loads.append(
            fetch(
                [up_ref.at[:, pl.ds(at, tile)], down_ref.at[pl.ds(at, tile), :]],
                [up_vmem.at[step], down_vmem.at[step]],
                load_sems.at[step],
            )
        )
    stores = []

    def store(source, target):
        stores.append(pltpu.make_async_copy(source, target, store_sems.at[len(stores)]))
        stores[-1].start()

    rows = rows_ref[...]
    logits = mm(rows, router_ref[...])
    exponent = jnp.exp(logits - jnp.max(logits, axis=-1, keepdims=True))
    chances = exponent / jnp.sum(exponent, axis=-1, keepdims=True)
    mine = iota(chances.shape, 1) == expert_ref[0]
    gating = jnp.sum(jnp.where(mine, chances, 0.0), axis=-1, keepdims=True)
    gp = (gating * cot_ref[...].astype(F32)).astype(BF)
    gp_ref[...] = gp
    store(gp_ref, gp_out)
    send_ref[:, 2 * ff_half : 2 * ff_half + width] = rows
    send_ref[:, 2 * ff_half + width :] = gp
    for step in range(steps):
        for copy in loads[step]:
            copy.wait()
        hidden = mm(rows, up_vmem[step])
        phi = 0.5 * (1.0 + lax.erf(hidden * (2.0**-0.5)))
        act = (hidden * phi).astype(BF)
        slope = phi + hidden * (jnp.exp(-0.5 * hidden * hidden) * 0.3989422804014327)
        pre = (mm_nt(gp, down_vmem[step]) * slope).astype(BF)
        if step == 0:
            out_acc[...] = mm(act, down_vmem[step])
            back_acc[...] = mm_nt(pre, up_vmem[step])
        else:
            out_acc[...] += mm(act, down_vmem[step])
            back_acc[...] += mm_nt(pre, up_vmem[step])
        if step < half_steps:
            send_ref[:, step * tile : (step + 1) * tile] = act
            send_ref[:, ff_half + step * tile : ff_half + (step + 1) * tile] = pre
        else:
            at = (step - half_steps) * tile
            act_ref[:, at : at + tile] = act
            pre_ref[:, at : at + tile] = pre
        if step == half_steps - 1:
            store(send_ref, send_out)
    store(act_ref, act_out)
    store(pre_ref, pre_out)
    produced = out_acc[...].astype(BF).astype(F32)
    scaled_ref[...] = (gating * produced).astype(BF)
    store(scaled_ref, scaled_out)
    grad_gate = jnp.sum(cot_ref[...].astype(F32) * produced, axis=-1, keepdims=True)
    grad_logits = gating * (mine.astype(F32) - chances) * grad_gate
    low = grad_logits.astype(BF)
    rest = (grad_logits - low.astype(F32)).astype(BF)
    back = back_acc[...] + (mm_nt(low, router_ref[...]) + mm_nt(rest, router_ref[...]))
    back_ref[...] = back.astype(BF)
    router_grad_ref[...] = mm_tn(low, rows) + mm_tn(rest, rows)
    for copy in stores:
        copy.wait()


def expert_grads_body(
    act_ref, pre_ref, rows_ref, gp_ref, act2_ref, pre2_ref, rows2_ref, gp2_ref, down_ref, up_ref
):
    down_ref[...] = mm_tn(act_ref[...], gp_ref[...]) + mm_tn(act2_ref[...], gp2_ref[...])
    up_ref[...] = mm_tn(rows_ref[...], pre_ref[...]) + mm_tn(rows2_ref[...], pre2_ref[...])


def norm_back(grad, source, gain):
    factor = lax.rsqrt(jnp.mean(source * source, axis=-1, keepdims=True) + epsilon)
    unit = source * factor
    scaled = grad * gain
    inner = jnp.mean(scaled * unit, axis=-1, keepdims=True)
    return factor * (scaled - unit * inner), grad * unit


def moe_back_body(
    place_hbm, back_ref, residual_hbm, gain_ref, cot_hbm, _scaled, _after,
    low_ref, gain_grad_ref, grad_out, _passed,
    place_ref, residual_ref, cot_ref, grad_ref, sems,
):
    loads = fetch([place_hbm, residual_hbm, cot_hbm], [place_ref, residual_ref, cot_ref], sems)
    loads[0].wait()
    grad_in = mm_tn(place_ref[...], back_ref[...])
    loads[1].wait()
    passed, terms = norm_back(grad_in, residual_ref[...], gain_ref[...].astype(F32))
    loads[2].wait()
    grad = cot_ref[...].astype(F32) + passed
    grad_ref[...] = grad
    store = pltpu.make_async_copy(grad_ref, grad_out, sems.at[3])
    store.start()
    low_ref[...] = grad.astype(BF)
    gain_grad_ref[...] = jnp.sum(terms, axis=0, keepdims=True)
    store.wait()


def fold_diagonals(squares):
    wide = jnp.concatenate([squares, jnp.zeros_like(squares)], axis=2)
    count = TILE
    while count > 8:
        count //= 2
        wide = wide[:, :count] + pltpu.roll(wide[:, count:], 2 * TILE - count, 2)
    return wide


def attend_back_body(
    half_ref, bits_ref, grad_own_ref, grad_other_ref, w_out_hbm, qkv_hbm, probs_hbm, context_hbm, normed_hbm,
    folded_ref, edge_ref, a0_out, a1_out, a2_out, a3_out, c0_out, c2_out, near_out, gqkv_out,
    a0_ref, a1_ref, a2_ref, a3_ref, c0_ref, c1_ref, c2_ref, c3_ref,
    gqkv_ref, gctx_ref, grad_ref, kv_ref, band_ref,
    w_out_ref, qkv_ref, probs_ref, context_ref, normed_ref, sems, store_sems,
):
    heads = probs_ref.shape[0]
    w_out_in, qkv_in, *probs_in = fetch(
        [w_out_hbm, qkv_hbm] + [probs_hbm.at[h] for h in range(heads)],
        [w_out_ref, qkv_ref] + [probs_ref.at[h] for h in range(heads)],
        sems,
    )
    context_in, normed_in = fetch(
        [context_hbm, normed_hbm], [context_ref, normed_ref], sems.at[pl.ds(2 + heads, 2)]
    )
    stores = []

    def store(source, target):
        stores.append(pltpu.make_async_copy(source, target, store_sems.at[len(stores)]))
        stores[-1].start()

    group, width = normed_ref.shape
    rows = grad_own_ref.shape[0]
    local = context_ref.shape[1]
    blocks = group // TILE
    own_at = pl.multiple_of(half_ref[0] * rows, rows)
    other_at = pl.multiple_of((1 - half_ref[0]) * rows, rows)
    grad_ref[pl.ds(own_at, rows), :] = grad_own_ref[...]
    grad_ref[pl.ds(other_at, rows), :] = grad_other_ref[...]
    grad = grad_ref[...]
    w_out_in.wait()
    gctx_ref[...] = mm_nt(grad, w_out_ref[...]).astype(BF)
    qkv_in.wait()
    scale = HEAD**-0.5
    buckets = 2 * halfway
    edges = [[], []]
    for h in range(heads):
        lo = h * HEAD
        queries = qkv_ref[:, lo : lo + HEAD]
        keys = qkv_ref[:, local + lo : local + lo + HEAD]
        values = qkv_ref[:, 2 * local + lo : 2 * local + lo + HEAD]
        gctx = gctx_ref[:, lo : lo + HEAD]
        if h == 0:
            context_in.wait()
        terms = gctx.astype(F32) * context_ref[:, lo : lo + HEAD].astype(F32)
        inner = jnp.sum(terms, axis=-1, keepdims=True)
        grad_probs = mm_nt(gctx, values)
        probs_in[h].wait()
        low_probs = probs_ref[h]
        grad_scores = low_probs.astype(F32) * (grad_probs - inner)
        low = grad_scores.astype(BF)
        gqkv_ref[:, lo : lo + HEAD] = (mm(low, keys) * scale).astype(BF)
        kv_ref[lo : lo + HEAD, :] = mm_tn(queries, low) * scale
        kv_ref[local + lo : local + lo + HEAD, :] = mm_tn(gctx, low_probs)
        for number, delta in enumerate((-1, 0, 1)):
            band = None
            for b in range(blocks):
                k = b + delta
                if 0 <= k < blocks:
                    piece = grad_scores[
                        b * TILE : (b + 1) * TILE, k * TILE : (k + 1) * TILE
                    ]
                    band = piece if band is None else band + piece
            band_ref[number * heads + h] = band
        for number, sign in enumerate((-1, 1)):
            total = jnp.zeros((1, 1), F32)
            for b in range(blocks):
                for k in range(blocks):
                    if (k - b) * sign > 1:
                        piece = grad_scores[
                            b * TILE : (b + 1) * TILE, k * TILE : (k + 1) * TILE
                        ]
                        total = total + jnp.sum(
                            jnp.sum(piece, axis=0, keepdims=True), axis=1, keepdims=True
                        )
            edges[number].append(total)
    gqkv_ref[:, local : 2 * local] = kv_ref[:local].T.astype(BF)
    gqkv_ref[:, 2 * local :] = kv_ref[local:].T.astype(BF)
    plane, depth = bits_ref[0], bits_ref[1]
    shard = width // 16
    half = width // 2
    targets = (c0_ref, c1_ref, c2_ref, c3_ref)
    dense = mm_tn(context_ref[...], grad).astype(BF)
    for a in range(2):
        for z in range(2):
            for number, target in enumerate(targets):

                @pl.when((depth ^ (2 * a + z)) == number)
                def _(target=target, dense=dense, a=a, z=z):
                    rows_of = slice(z * 4 * shard, (z + 1) * 4 * shard)
                    target[...] = dense[rows_of, a * half : (a + 1) * half]
    size = 4 * shard
    outs = (c0_out, near_out.at[pl.ds(0, size), :], c2_out, near_out.at[pl.ds(size, size), :])
    for target, out in zip(targets, outs):
        store(target, out)
    normed_in.wait()
    targets = (a0_ref, a1_ref, a2_ref, a3_ref)
    dense = mm_tn(normed_ref[...], gqkv_ref[...]).astype(BF)
    for p in range(4):
        for number, target in enumerate(targets):

            @pl.when((plane ^ p) == number)
            def _(target=target, p=p):
                for z in range(4):
                    piece = dense[(p * 4 + z) * shard : (p * 4 + z + 1) * shard]
                    at = pl.multiple_of((depth ^ z) * shard, shard)
                    target[pl.ds(at, shard), :] = piece
    for target, out in zip(targets, (a0_out, a1_out, a2_out, a3_out)):
        store(target, out)
    store(gqkv_ref, gqkv_out)
    folded_ref[...] = fold_diagonals(band_ref[...])
    for number in range(2):
        for h in range(heads):
            edge_ref[h : h + 1, number * TILE : (number + 1) * TILE] = jnp.broadcast_to(
                edges[number][h], (1, TILE)
            )
    for copy in stores:
        copy.wait()


def small_grads_body(
    half_ref, folded_ref, edge_ref, router_grad_ref, moe_gain_grad_ref, gqkv_hbm, w_hbm, x_hbm, x_other_hbm,
    _after, small_ref, own_ref, other_ref,
    gqkv_ref, w_ref, x_ref, x_other_ref, all_ref, sems,
):
    loads = fetch([gqkv_hbm, w_hbm, x_hbm, x_other_hbm], [gqkv_ref, w_ref, x_ref, x_other_ref], sems)
    rows, width = own_ref.shape
    local = w_ref.shape[2]
    heads = local // HEAD
    buckets = 2 * halfway
    own_at = pl.multiple_of(half_ref[0] * rows, rows)
    other_at = pl.multiple_of((1 - half_ref[0]) * rows, rows)
    folded = folded_ref[...]
    spread = jnp.zeros((heads * 8, 8 * buckets), F32)
    for number, delta in enumerate((-1, 0, 1)):
        distance = iota((8, 2 * TILE), 1) - iota((8, 2 * TILE), 0)
        distance = jnp.where(distance >= TILE, distance - 2 * TILE, distance) + TILE * delta
        bucket = bucket_of(distance)
        hot = jnp.concatenate(
            [bucket[r : r + 1] == iota((buckets, 2 * TILE), 0) for r in range(8)], axis=0
        )
        hot = hot.astype(F32).astype(BF)
        sums = folded[number * heads : (number + 1) * heads].reshape(heads * 8, 2 * TILE)
        for _ in range(3):
            low = sums.astype(BF)
            spread = spread + mm_nt(low, hot)
            sums = sums - low.astype(F32)
    same = iota(spread.shape, 0) % 8 == iota(spread.shape, 1) // buckets
    table = jnp.sum(jnp.where(same, spread, 0.0).reshape(heads, 8, 8 * buckets), axis=1)
    step = 4 * buckets
    while step >= buckets:
        table = table + pltpu.roll(table, step, 1)
        step //= 2
    table = table[:, :buckets]
    table = jnp.concatenate([table, jnp.zeros((8 - heads, buckets), F32)], axis=0)
    for number, bucket in enumerate((halfway - 1, 2 * halfway - 1)):
        column = jnp.concatenate(
            [edge_ref[:heads, number * TILE : number * TILE + 1], jnp.zeros((8 - heads, 1), F32)], axis=0
        )
        table = table + jnp.where(iota((8, buckets), 1) == bucket, column, 0.0)
    for copy in loads:
        copy.wait()
    total = None
    for c in range(3):
        part = mm_nt(gqkv_ref[:, c * local : (c + 1) * local], w_ref[c])
        total = part if total is None else total + part
    all_ref[...] = total
    own_ref[...] = all_ref[pl.ds(own_at, rows), :]
    other_ref[...] = all_ref[pl.ds(other_at, rows), :]
    gain_grad = jnp.zeros((1, width), F32)
    for ref, part in ((x_ref, own_ref), (x_other_ref, other_ref)):
        x = ref[...].astype(F32)
        factor = lax.rsqrt(jnp.mean(x * x, axis=-1, keepdims=True) + epsilon)
        gain_grad = gain_grad + jnp.sum(part[...] * (x * factor), axis=0, keepdims=True)
    moe_gain_grad = moe_gain_grad_ref[...]
    row = iota((16, local), 0)
    extra = jnp.concatenate([table, jnp.zeros((8, local - buckets), F32)], axis=1)
    extra = jnp.concatenate([jnp.zeros((8, local), F32), extra], axis=0)
    for number, value in enumerate((moe_gain_grad, gain_grad)):
        for part in range(2):
            piece = value[:, part * local : (part + 1) * local]
            extra = extra + jnp.where(row == 2 * number + part, piece, 0.0)
    small = jnp.concatenate(
        [router_grad_ref[:, :local], router_grad_ref[:, local:], extra], axis=0
    ).astype(BF)
    small_ref[...] = small


def order_body(_value, _after, _out):
    pass


def total_of(*values):
    return functools.reduce(jnp.add, [v.astype(F32) for v in values]).astype(BF)


def pairs_of(a, b, c, d):
    return ((a.astype(F32) + b.astype(F32)) + (c.astype(F32) + d.astype(F32))).astype(BF)


def fold_near_body(got_ref, c0_hbm, c2_hbm, c0_out, c2_out, c0_ref, c2_ref, sems):
    for copy in fetch([c0_hbm, c2_hbm], [c0_ref, c2_ref], sems):
        copy.wait()
    size = c0_ref.shape[0]
    c0_out[...] = total_of(c0_ref[...], got_ref[:size])
    c2_out[...] = total_of(c2_ref[...], got_ref[size:])


def fold_first_body(
    a1_ref, a2_ref, a3_ref, c0_ref, got_ref, a0_hbm, small_ref,
    s0_ref, s2_ref, near_ref, e_ref,
    a0_ref, sem,
):
    load = pltpu.make_async_copy(a0_hbm, a0_ref, sem)
    load.start()
    load.wait()
    shard, lead = s0_ref.shape[0], small_ref.shape[0]
    for d, target in enumerate((s0_ref, near_ref.at[:shard], s2_ref, near_ref.at[shard:])):
        at = slice(d * shard, (d + 1) * shard)
        target[...] = pairs_of(a0_ref[at], a1_ref[at], a2_ref[at], a3_ref[at])
    e_ref[:lead] = small_ref[...]
    e_ref[lead:] = total_of(c0_ref[...], got_ref[...])


def fold_z_body(got_ref, s0_ref, s2_ref, s0_out, s2_out):
    size = s0_ref.shape[0]
    s0_out[...] = total_of(s0_ref[...], got_ref[:size])
    s2_out[...] = total_of(s2_ref[...], got_ref[size:])


def fold_last_body(
    s0_ref, got_ref, e0_ref, e1_ref, e2_ref, e3_ref, total_ref, c_ref, small_ref
):
    lead = small_ref.shape[0]
    total_ref[...] = total_of(s0_ref[...], got_ref[...])
    small_ref[...] = pairs_of(e0_ref[:lead], e1_ref[:lead], e2_ref[:lead], e3_ref[:lead])
    c_ref[...] = pairs_of(e0_ref[lead:], e1_ref[lead:], e2_ref[lead:], e3_ref[lead:])


def join_body(shared, t0_ref, t1_ref, t2_ref, t3_ref, c_ref, small_ref, other_ref, _after, mine_ref, c_mine_ref):
    shard, size = t0_ref.shape[0], c_ref.shape[0]
    for d, ref in enumerate((t0_ref, t1_ref, t2_ref, t3_ref)):
        mine_ref[d * shard : (d + 1) * shard] = ref[...]
    c_mine_ref[:size] = c_ref[...]
    own = small_ref[...].astype(F32)
    both = own + other_ref[...].astype(F32)
    c_mine_ref[size:] = jnp.where(iota(own.shape, 0) < shared, both, own).astype(BF)


def stack_body(a_ref, b_ref, out_ref):
    size = a_ref.shape[0]
    out_ref[:size] = a_ref[...]
    out_ref[size:] = b_ref[...]


def tokens_body(
    place_ref, scaled_ref, residual_ref, own_ref, got_ref, x_ref, gain_ref, grad_res_ref, _after, out_ref, grad_ref
):
    out_ref[...] = (residual_ref[...] + mm_tn(place_ref[...], scaled_ref[...])).astype(BF)
    passed, _ = norm_back(
        own_ref[...] + got_ref[...], x_ref[...].astype(F32), gain_ref[...].astype(F32)
    )
    grad_ref[...] = grad_res_ref[...] + passed


def unpack_body(
    bits_ref, a0_ref, a1_ref, a2_ref, a3_ref, c0_ref, c2_ref, near_ref,
    router_ref, norm_gain_ref, moe_gain_ref, bias_ref, qkv_out, w_out_out,
    wide_ref, w_out_ref, qkv_sems, out_sems,
):
    local = qkv_out.shape[2]
    shard = a0_ref.shape[0] // 4
    plane, depth = bits_ref[0], bits_ref[1]
    copies = []
    for number, ref in enumerate((a0_ref, a1_ref, a2_ref, a3_ref)):
        quarter = plane ^ number
        wide_ref[number] = ref[...].astype(F32)
        for d in range(4):
            at = pl.multiple_of((quarter * 4 + (depth ^ d)) * shard, shard)
            for c in range(3):
                copy = pltpu.make_async_copy(
                    wide_ref.at[number, pl.ds(d * shard, shard), pl.ds(c * local, local)],
                    qkv_out.at[c, pl.ds(at, shard), :],
                    qkv_sems.at[number, d, c],
                )
                copy.start()
                copies.append(copy)
    size = c0_ref.shape[0]
    others = (c0_ref, near_ref.at[:size], c2_ref, near_ref.at[size:])
    for number, ref in enumerate(others):
        w_out_ref[number] = ref[: 4 * shard].astype(F32)
        slab = depth ^ number
        lane = pl.multiple_of((slab // 2) * local, local)
        at = pl.multiple_of((slab % 2) * 4 * shard, 4 * shard)
        copy = pltpu.make_async_copy(
            w_out_ref.at[number], w_out_out.at[pl.ds(at, 4 * shard), pl.ds(lane, local)], out_sems.at[number]
        )
        copy.start()
        copies.append(copy)
    parts = [ref[4 * shard :].astype(F32) for ref in others]
    small = (parts[0] + parts[1]) + (parts[2] + parts[3])
    experts = router_ref.shape[0]
    router_ref[:, :local] = small[:experts]
    router_ref[:, local:] = small[experts : 2 * experts]
    rest = small[2 * experts :]
    for number, ref in enumerate((moe_gain_ref, norm_gain_ref)):
        ref[:local] = rest[2 * number]
        ref[local:] = rest[2 * number + 1]
    bias_ref[...] = rest[8 : 8 + bias_ref.shape[0], : bias_ref.shape[1]]
    for copy in copies:
        copy.wait()


def per_device(
    tokens, lengths, routes, norm_gain, w_qkv, rel_bias, w_out, moe_gain, w_router, w_in, w_down, cotangent
):
    rows, width = tokens.shape
    sources = lax.axis_size("expert")
    group = rows * lax.axis_size("tensor")
    experts = w_router.shape[1]
    capacity = max(2, 4 * rows // (3 * experts))
    slots = experts * capacity
    local = w_qkv.shape[2]
    heads = local // HEAD
    buckets = rel_bias.shape[0]
    ff = w_in.shape[2]
    ff_half = ff // 2
    half = lax.axis_index("tensor").astype(jnp.int32)
    expert = lax.axis_index("expert").astype(jnp.int32)
    half_one = half.reshape(1)
    gain_a = norm_gain.reshape(1, width)
    gain_b = moe_gain.reshape(1, width)

    def swap(value):
        return lax.ppermute(value, "tensor", [(0, 1), (1, 0)])

    def exchange(value):
        return lax.all_to_all(
            value.reshape(experts, capacity, width), "expert", split_axis=0, concat_axis=0, tiled=True
        ).reshape(slots, width)

    def ordered(value, after):
        return pl.pallas_call(
            order_body,
            out_shape=hbm(value.shape, value.dtype),
            in_specs=[ANY, ANY],
            out_specs=ANY,
            input_output_aliases={0: 0},
            name="order",
        )(value, after)

    x_other = swap(tokens)
    place, cot_slots = pl.pallas_call(
        functools.partial(prep_body, capacity, experts),
        out_shape=(hbm((slots, rows), BF),) + shape_of(((slots, width), BF)),
        in_specs=vmem_specs(2),
        out_specs=[ANY] + vmem_specs(1),
        scratch_shapes=[pltpu.VMEM((slots, rows), BF), pltpu.SemaphoreType.DMA],
        cost_estimate=cost(2e9, 1e6),
        name="place_cotangent",
    )(routes.reshape(1, rows), cotangent)
    cot_rows = exchange(cot_slots)

    bias_rows = jnp.pad(rel_bias.T, ((0, 8 - heads), (0, 0)))
    own_sum, other_sum, context, qkv, probs, normed = pl.pallas_call(
        attend_body,
        out_shape=shape_of(((rows, width), F32), ((rows, width), F32))
        + (
            hbm((group, local), BF),
            hbm((group, 3 * local), BF),
            hbm((heads, group, group), BF),
            hbm((group, width), BF),
        ),
        in_specs=[SMEM, SMEM] + vmem_specs(3) + [ANY] + vmem_specs(1) + [ANY],
        out_specs=vmem_specs(2) + [ANY] * 4,
        scratch_shapes=[
            pltpu.VMEM((3, width, local), BF),
            pltpu.VMEM((local, width), BF),
            pltpu.VMEM((group, local), BF),
            pltpu.VMEM((group, 3 * local), BF),
            pltpu.VMEM((heads, group, group), BF),
            pltpu.VMEM((group, width), BF),
            pltpu.VMEM((group, group), F32),
            pltpu.SemaphoreType.DMA((4,)),
            pltpu.SemaphoreType.DMA((heads + 3,)),
        ],
        compiler_params=params(20),
        cost_estimate=cost(8e9, 4e6),
        name="attention",
    )(half_one, lengths, tokens, x_other, gain_a, in_hbm(w_qkv), bias_rows, in_hbm(w_out))
    got_sum = swap(other_sum)

    expert_one = expert.reshape(1)
    moe_slots, router, residual = pl.pallas_call(
        project_body,
        out_shape=shape_of(((slots, width), BF), ((width, experts), BF)) + (hbm((rows, width), F32),),
        in_specs=[SMEM] + vmem_specs(5) + [ANY, ANY],
        out_specs=vmem_specs(2) + [ANY],
        scratch_shapes=[
            pltpu.VMEM((slots, rows), BF),
            pltpu.VMEM((rows, width), F32),
            pltpu.SemaphoreType.DMA((2,)),
        ],
        compiler_params=params(12),
        cost_estimate=cost(2e9, 2e6),
        name="projection",
    )(expert_one, own_sum, got_sum, tokens, gain_b, w_router, in_hbm(place), cot_rows)
    stacked = exchange(moe_slots)

    count = sources * capacity
    tile = FF_TILE
    steps = ff // tile
    half_steps = steps // 2

    back, router_grad, scaled, gp, send, act, pre = pl.pallas_call(
        expert_body,
        out_shape=shape_of(((count, width), BF), ((experts, width), F32))
        + (
            hbm((count, width), BF),
            hbm((count, width), BF),
            hbm((count, 2 * ff_half + 2 * width), BF),
            hbm((count, ff_half), BF),
            hbm((count, ff_half), BF),
        ),
        in_specs=[SMEM, SMEM] + vmem_specs(3) + [ANY, ANY],
        out_specs=vmem_specs(2) + [ANY] * 5,
        scratch_shapes=[
            pltpu.VMEM((steps, width, tile), BF),
            pltpu.VMEM((steps, tile, width), BF),
            pltpu.VMEM((count, width), BF),
            pltpu.VMEM((count, width), BF),
            pltpu.VMEM((count, 2 * ff_half + 2 * width), BF),
            pltpu.VMEM((count, ff_half), BF),
            pltpu.VMEM((count, ff_half), BF),
            pltpu.VMEM((count, width), F32),
            pltpu.VMEM((count, width), F32),
            pltpu.SemaphoreType.DMA((steps, 2)),
            pltpu.SemaphoreType.DMA((5,)),
        ],
        compiler_params=params(32),
        cost_estimate=cost(10e9, 14e6),
        name="expert",
    )(half_one, expert_one, stacked, cot_rows, router, in_hbm(w_in[0]), in_hbm(w_down[0]))
    back_rows = exchange(back)
    peer = swap(send)

    col = lambda first: pl.BlockSpec((count, tile), lambda i: (0, first + i))
    fixed = lambda block: pl.BlockSpec((count, width), lambda i: (0, block))
    grad_down, grad_up = pl.pallas_call(
        expert_grads_body,
        grid=(half_steps,),
        in_specs=[
            col(0), col(0), fixed(0), fixed(0),
            col(0), col(half_steps), fixed(2 * ff_half // width), fixed(2 * ff_half // width + 1),
        ],
        out_specs=[
            pl.BlockSpec((tile, width), lambda i: (i, 0)),
            pl.BlockSpec((width, tile), lambda i: (0, i)),
        ],
        out_shape=shape_of(((ff_half, width), F32), ((width, ff_half), F32)),
        compiler_params=params(20),
        cost_estimate=cost(5e9, 14e6),
        name="expert_grads",
    )(in_hbm(act), in_hbm(pre), stacked, in_hbm(gp), *[in_hbm(peer)] * 4)

    grad_low, moe_gain_grad, grad_res, scaled_late = pl.pallas_call(
        moe_back_body,
        out_shape=shape_of(((rows, width), BF), ((1, width), F32))
        + (hbm((rows, width), F32), hbm((count, width), BF)),
        in_specs=[ANY] + vmem_specs(1) + [ANY] + vmem_specs(1) + [ANY] * 3,
        out_specs=vmem_specs(2) + [ANY, ANY],
        input_output_aliases={5: 3},
        scratch_shapes=[
            pltpu.VMEM((slots, rows), BF),
            pltpu.VMEM((rows, width), F32),
            pltpu.VMEM((rows, width), BF),
            pltpu.VMEM((rows, width), F32),
            pltpu.SemaphoreType.DMA((4,)),
        ],
        compiler_params=params(12),
        cost_estimate=cost(1e9, 2e6),
        name="norm_back",
    )(in_hbm(place), back_rows, in_hbm(residual), gain_b, in_hbm(cotangent), scaled, in_hbm(grad_down))
    grad_other = swap(grad_low)
    scaled_rows = exchange(scaled_late)

    position = jnp.stack([expert & 3, (expert >> 2) & 3])
    shard = width // 16
    lead = 2 * experts + 16
    big, slab = (4 * shard, 3 * local), (4 * shard, local)
    folded, edges, a0, a1, a2, a3, c0, c2, c_near, grad_joined = pl.pallas_call(
        attend_back_body,
        out_shape=(
            *shape_of(((3 * heads, 8, 2 * TILE), F32), ((8, 2 * TILE), F32)),
            *[hbm(big, BF)] * 4, *[hbm(slab, BF)] * 2, hbm((8 * shard, local), BF), hbm((group, 3 * local), BF),
        ),
        in_specs=[SMEM, SMEM] + vmem_specs(2) + [ANY] * 5,
        out_specs=vmem_specs(2) + [ANY] * 8,
        scratch_shapes=[pltpu.VMEM(big, BF)] * 4
        + [pltpu.VMEM(slab, BF)] * 4
        + [
            pltpu.VMEM((group, 3 * local), BF),
            pltpu.VMEM((group, local), BF),
            pltpu.VMEM((group, width), BF),
            pltpu.VMEM((2 * local, group), F32),
            pltpu.VMEM((3 * heads, TILE, TILE), F32),
            pltpu.VMEM((local, width), BF),
            pltpu.VMEM((group, 3 * local), BF),
            pltpu.VMEM((heads, group, group), BF),
            pltpu.VMEM((group, local), BF),
            pltpu.VMEM((group, width), BF),
            pltpu.SemaphoreType.DMA((4 + heads,)),
            pltpu.SemaphoreType.DMA((9,)),
        ],
        compiler_params=params(32),
        cost_estimate=cost(10e9, 10e6),
        name="attention_back",
    )(
        half_one, position, grad_low, grad_other, in_hbm(w_out), in_hbm(qkv), in_hbm(probs), in_hbm(context),
        in_hbm(normed),
    )
    a1 = ordered(a1, scaled_rows)

    def moves(flip):
        pairs = [(2 * e + t, 2 * (e ^ flip) + t) for e in range(sources) for t in range(2)]
        return lambda value: lax.ppermute(value, ("expert", "tensor"), pairs)

    flat = [moves(d) for d in range(1, 4)]
    along = [moves(4 * d) for d in range(1, 4)]

    def add(*values):
        return functools.reduce(jnp.add, [v.astype(F32) for v in values]).astype(BF)

    def fused(name, body, shapes, values, before=(), mib=8):
        return pl.pallas_call(
            body,
            out_shape=[jax.ShapeDtypeStruct(shape, dtype) for shape, dtype in shapes],
            in_specs=vmem_specs(len(values)) + [ANY] * len(before),
            out_specs=vmem_specs(len(shapes)),
            compiler_params=params(mib),
            cost_estimate=cost(1e3, 1e3),
            name=name,
        )(*values, *before)

    quarter = 4 * shard
    wide = 3 * local
    got_a = [flat[d](a) for d, a in enumerate((a1, a2, a3))]
    c0, c2 = pl.pallas_call(
        fold_near_body,
        out_shape=shape_of(*[(slab, BF)] * 2),
        in_specs=vmem_specs(1) + [ANY] * 2,
        out_specs=vmem_specs(2),
        scratch_shapes=[pltpu.VMEM(slab, BF)] * 2 + [pltpu.SemaphoreType.DMA((2,))],
        compiler_params=params(8),
        cost_estimate=cost(1e3, 1e3),
        name="fold_near",
    )(along[0](c_near), in_hbm(c0), in_hbm(c2))
    got_c = along[1](c2)
    small, own_gn, other_gn = pl.pallas_call(
        small_grads_body,
        out_shape=shape_of(((lead, local), BF), ((rows, width), F32), ((rows, width), F32)),
        in_specs=[SMEM] + vmem_specs(4) + [ANY] * 5,
        out_specs=vmem_specs(3),
        scratch_shapes=[
            pltpu.VMEM((group, 3 * local), BF),
            pltpu.VMEM((3, width, local), BF),
            pltpu.VMEM((rows, width), BF),
            pltpu.VMEM((rows, width), BF),
            pltpu.VMEM((group, width), F32),
            pltpu.SemaphoreType.DMA((4,)),
        ],
        compiler_params=params(16),
        cost_estimate=cost(1e3, 1e3),
        name="small_grads",
    )(
        half_one, folded, edges, router_grad, moe_gain_grad, in_hbm(grad_joined), in_hbm(w_qkv), in_hbm(tokens),
        in_hbm(x_other), c0,
    )
    got_gn = swap(other_gn)
    output, grad_tokens = pl.pallas_call(
        tokens_body,
        out_shape=shape_of(((rows, width), BF), ((rows, width), F32)),
        in_specs=vmem_specs(8) + [ANY],
        out_specs=vmem_specs(2),
        compiler_params=params(12),
        cost_estimate=cost(1e3, 1e3),
        name="token_outputs",
    )(place, scaled_rows, residual, own_gn, got_gn, tokens, gain_a, grad_res, c0)

    s0, s2, s_near, part_c = pl.pallas_call(
        fold_first_body,
        out_shape=shape_of(
            *[((shard, wide), BF)] * 2, ((2 * shard, wide), BF), ((lead + 4 * shard, local), BF)
        ),
        in_specs=vmem_specs(5) + [ANY] + vmem_specs(1),
        out_specs=vmem_specs(4),
        scratch_shapes=[pltpu.VMEM(big, BF), pltpu.SemaphoreType.DMA],
        compiler_params=params(8),
        cost_estimate=cost(1e3, 1e3),
        name="fold_first",
    )(*got_a, c0, got_c, in_hbm(a0), small)
    s0, s2 = fused("fold_z", fold_z_body, [((shard, wide), BF)] * 2, (along[0](s_near), s0, s2))
    got_z = along[1](s2)
    got_e = [flat[d](part_c) for d in range(3)]
    total, c_full, small = fused(
        "fold_last",
        fold_last_body,
        [((shard, wide), BF), (slab, BF), ((lead, local), BF)],
        (s0, got_z, part_c, *got_e),
    )
    for b in range(4, sources.bit_length() - 1):
        further = moves(1 << b)
        total = add(total, further(total))
        c_full = add(c_full, further(c_full))
        small = add(small, further(small))

    others = [along[d](total) for d in range(3)]
    mine, c_mine = fused(
        "join",
        functools.partial(join_body, 2 * experts + 8),
        [((quarter, wide), BF), ((quarter + lead, local), BF)],
        (total, *others, c_full, small, swap(small)),
        (grad_tokens,),
    )
    all_mine = [mine] + [flat[d](mine) for d in range(3)]
    c_far = along[1](c_mine)
    (c_two,) = fused("stack", stack_body, [((2 * (quarter + lead), local), BF)], (c_mine, c_far))
    c_near = along[0](c_two)
    grad_router, grad_norm_gain, grad_moe_gain, grad_rel, grad_qkv, grad_out = pl.pallas_call(
        unpack_body,
        out_shape=shape_of(
            ((experts, width), F32), ((width,), F32), ((width,), F32), ((heads, buckets), F32)
        )
        + (hbm((3, width, local), F32), hbm((local, width), F32)),
        in_specs=[SMEM] + vmem_specs(7),
        out_specs=vmem_specs(4) + [ANY] * 2,
        scratch_shapes=[
            pltpu.VMEM((4, quarter, wide), F32),
            pltpu.VMEM((4, quarter, local), F32),
            pltpu.SemaphoreType.DMA((4, 4, 3)),
            pltpu.SemaphoreType.DMA((4,)),
        ],
        compiler_params=params(12),
        cost_estimate=cost(1e3, 1e3),
        name="unpack",
    )(position, *all_mine, c_mine, c_far, c_near)

    return (
        output,
        grad_tokens,
        grad_norm_gain,
        grad_qkv,
        grad_rel.T,
        grad_out,
        grad_moe_gain,
        grad_router.T,
        grad_up[None],
        grad_down[None],
    )


def solution(mesh):
    return jax.shard_map(
        per_device,
        mesh=mesh,
        in_specs=(
            P(("expert", "tensor"), None),
            P("expert", None),
            P(("expert", "tensor"), None),
            P(),
            P(None, None, "tensor"),
            P(None, "tensor"),
            P("tensor", None),
            P(),
            P(),
            P("expert", None, None),
            P("expert", None, None),
            P(("expert", "tensor"), None),
        ),
        out_specs=(
            P(("expert", "tensor"), None),
            P(("expert", "tensor"), None),
            P(),
            P(None, None, "tensor"),
            P(None, "tensor"),
            P("tensor", None),
            P(),
            P(),
            P("expert", None, "tensor"),
            P("expert", "tensor", None),
        ),
        check_vma=False,
    )
```

```python
import functools

import jax
import jax.numpy as jnp
from jax import lax
from jax.experimental import pallas as pl
from jax.experimental.pallas import tpu as pltpu
from jax.sharding import PartitionSpec as P

HEAD = 64
TILE = 128
FF_TILE = 512

epsilon = 1e-06
THRESHOLDS = (1, 2, 3, 4, 5, 6, 7, 8, 12, 16, 23, 32, 46, 64, 91)
halfway = 16
BF = jnp.bfloat16
F32 = jnp.float32
HIGH = lax.Precision.HIGHEST
MIB = 1 << 20


def mm(a, b):
    return lax.dot_general(a, b, (((1,), (0,)), ((), ())), preferred_element_type=F32)


def mm_nt(a, b):
    return lax.dot_general(a, b, (((1,), (1,)), ((), ())), preferred_element_type=F32)


def mm_tn(a, b):
    return lax.dot_general(a, b, (((0,), (0,)), ((), ())), preferred_element_type=F32)


def iota(shape, dim):
    return lax.broadcasted_iota(jnp.int32, shape, dim)


def vmem_specs(count):
    return [pl.BlockSpec(memory_space=pltpu.VMEM)] * count


SMEM = pl.BlockSpec(memory_space=pltpu.SMEM)


def shape_of(*pairs):
    return tuple(jax.ShapeDtypeStruct(shape, dtype) for shape, dtype in pairs)


ANY = pl.BlockSpec(memory_space=pl.ANY)


def params(mib):
    return pltpu.CompilerParams(vmem_limit_bytes=mib * MIB)


def hbm(shape, dtype):
    return pltpu.HBM(shape, dtype)


def in_hbm(value):
    return pltpu.with_memory_space_constraint(value, pltpu.HBM)


def fetch(sources, targets, sems):
    copies = []
    for number, (source, target) in enumerate(zip(sources, targets, strict=True)):
        copies.append(pltpu.make_async_copy(source, target, sems.at[number]))
        copies[-1].start()
    return copies


def cost(flops, loaded):
    return pl.CostEstimate(flops=int(flops), bytes_accessed=int(loaded), transcendentals=0)


def bucket_of(distance):
    magnitude = jnp.abs(distance)
    bucket = jnp.zeros(distance.shape, jnp.int32)
    for border in THRESHOLDS:
        bucket = bucket + (magnitude >= border).astype(jnp.int32)
    return bucket + jnp.where(distance > 0, halfway, 0).astype(jnp.int32)


def distance_hot(buckets, delta):
    distance = iota((buckets, 2 * TILE), 1) + (TILE * delta - (TILE - 1))
    return bucket_of(distance) == iota((buckets, 2 * TILE), 0)


def prep_body(capacity, experts, routes_ref, cot_hbm, place_out, out_ref, place_ref, cot_ref, sem, load_sem):
    load = pltpu.make_async_copy(cot_hbm, cot_ref, load_sem)
    load.start()
    rows = cot_ref.shape[0]
    chosen = routes_ref[...]
    hot = chosen == iota((experts, rows), 0)
    above = (iota((rows, rows), 0) < iota((rows, rows), 1)).astype(F32).astype(BF)
    earlier = mm(hot.astype(F32).astype(BF), above)
    ordinal = jnp.sum(jnp.where(hot, earlier, 0.0), axis=0, keepdims=True)
    slot = chosen * capacity + ordinal.astype(jnp.int32)
    place = (slot == iota((experts * capacity, rows), 0)).astype(F32).astype(BF)
    place_ref[...] = place
    store = pltpu.make_async_copy(place_ref, place_out, sem)
    store.start()
    load.wait()
    out_ref[...] = mm(place, cot_ref[...]).astype(BF)
    store.wait()


def attend_body(
    half_ref, lengths_ref, x_ref, x_other_ref, gain_ref, w_ref, bias_ref, w_out_ref,
    own_ref, other_ref, context_out, qkv_out, probs_out, normed_out,
    w_vmem, w_out_vmem, context_ref, qkv_ref, probs_ref, normed_ref, mask_ref, load_sems, store_sems,
):
    loads = fetch(
        [w_ref.at[c] for c in range(3)] + [w_out_ref],
        [w_vmem.at[c] for c in range(3)] + [w_out_vmem],
        load_sems,
    )
    stores = []

    def store(source, target):
        stores.append(pltpu.make_async_copy(source, target, store_sems.at[len(stores)]))
        stores[-1].start()

    group = normed_ref.shape[0]
    rows = own_ref.shape[0]
    local = w_ref.shape[2]
    heads = local // HEAD
    blocks = group // TILE
    own_at = pl.multiple_of(half_ref[0] * rows, rows)
    other_at = pl.multiple_of((1 - half_ref[0]) * rows, rows)
    for ref, at in ((x_ref, own_at), (x_other_ref, other_at)):
        x = ref[...].astype(F32)
        factor = lax.rsqrt(jnp.mean(x * x, axis=-1, keepdims=True) + epsilon)
        normed_ref[pl.ds(at, rows), :] = (x * factor * gain_ref[...].astype(F32)).astype(BF)
    normed = normed_ref[...]
    store(normed_ref, normed_out)
    for c in range(3):
        loads[c].wait()
        qkv_ref[:, c * local : (c + 1) * local] = mm(normed, w_vmem[c]).astype(BF)
    store(qkv_ref, qkv_out)
    buckets = bias_ref.shape[1]
    tables = {
        delta: mm(bias_ref[...], distance_hot(buckets, delta).astype(F32).astype(BF))
        for delta in (-1, 0, 1)
    }
    bias = bias_ref[...].astype(F32)
    far = {-1: bias[:, halfway - 1 : halfway], 1: bias[:, 2 * halfway - 1 : 2 * halfway]}
    segment_rows = jnp.zeros((group, 1), jnp.int32)
    segment_lanes = jnp.zeros((1, group), jnp.int32)
    border = jnp.int32(0)
    for s in range(lengths_ref.shape[1]):
        border = border + lengths_ref[0, s]
        segment_rows = segment_rows + (iota((group, 1), 0) >= border).astype(jnp.int32)
        segment_lanes = segment_lanes + (iota((1, group), 1) >= border).astype(jnp.int32)
    mask_ref[...] = jnp.where(segment_rows == segment_lanes, 0.0, -1e30)
    for h in range(heads):
        lo = h * HEAD
        keys = qkv_ref[:, local + lo : local + lo + HEAD]
        values = qkv_ref[:, 2 * local + lo : 2 * local + lo + HEAD]
        bands = []
        for delta in range(1 - blocks, blocks):
            if abs(delta) > 1:
                value = far[1 if delta > 0 else -1][h : h + 1]
                bands.append(jnp.broadcast_to(value, (TILE, TILE)))
            else:
                wide = jnp.broadcast_to(tables[delta][h : h + 1, :], (TILE, 2 * TILE))
                band = pltpu.roll(wide, TILE + 1, 1, stride=1, stride_axis=0)
                bands.append(band[:, :TILE])
        bias = jnp.concatenate(
            [
                jnp.concatenate([bands[k - b + blocks - 1] for k in range(blocks)], axis=1)
                for b in range(blocks)
            ],
            axis=0,
        )
        queries = qkv_ref[:, lo : lo + HEAD] * (HEAD**-0.5)
        scores = mm_nt(queries, keys) + (bias + mask_ref[...])
        exponent = jnp.exp(scores - jnp.max(scores, axis=-1, keepdims=True))
        probs = exponent * (1.0 / jnp.sum(exponent, axis=-1, keepdims=True))
        low = probs.astype(BF)
        probs_ref[h] = low
        context_ref[:, lo : lo + HEAD] = mm(low, values).astype(BF)
        store(probs_ref.at[h], probs_out.at[h])
    store(context_ref, context_out)
    loads[3].wait()
    other_ref[...] = mm(context_ref[pl.ds(other_at, rows), :], w_out_vmem[...])
    own_ref[...] = mm(context_ref[pl.ds(own_at, rows), :], w_out_vmem[...])
    for copy in stores:
        copy.wait()


def project_body(
    _expert, own_ref, other_ref, x_ref, gain_ref, router_ref, place_hbm, _after,
    out_ref, router_out, residual_out,
    place_ref, residual_ref, sems,
):
    loads = fetch([place_hbm], [place_ref], sems)
    router_out[...] = router_ref[...]
    residual = x_ref[...].astype(F32) + (own_ref[...] + other_ref[...])
    residual_ref[...] = residual
    store = pltpu.make_async_copy(residual_ref, residual_out, sems.at[1])
    store.start()
    factor = lax.rsqrt(jnp.mean(residual * residual, axis=-1, keepdims=True) + epsilon)
    moe_rows = (residual * factor * gain_ref[...].astype(F32)).astype(BF)
    loads[0].wait()
    out_ref[...] = mm(place_ref[...], moe_rows).astype(BF)
    store.wait()


def expert_body(
    half_ref, expert_ref, rows_ref, cot_ref, router_ref, up_ref, down_ref,
    back_ref, router_grad_ref, scaled_out, gp_out, send_out, act_out, pre_out,
    up_vmem, down_vmem, scaled_ref, gp_ref, send_ref, act_ref, pre_ref, out_acc, back_acc, load_sems, store_sems,
):
    steps, _, tile = up_vmem.shape
    half_steps = steps // 2
    width = rows_ref.shape[1]
    ff_half = act_ref.shape[1]
    loads = []
    for step in range(steps):
        side = 1 - half_ref[0] if step < half_steps else half_ref[0]
        at = pl.multiple_of((side * half_steps + step % half_steps) * tile, tile)
        loads.append(
            fetch(
                [up_ref.at[:, pl.ds(at, tile)], down_ref.at[pl.ds(at, tile), :]],
                [up_vmem.at[step], down_vmem.at[step]],
                load_sems.at[step],
            )
        )
    stores = []

    def store(source, target):
        stores.append(pltpu.make_async_copy(source, target, store_sems.at[len(stores)]))
        stores[-1].start()

    rows = rows_ref[...]
    logits = mm(rows, router_ref[...])
    exponent = jnp.exp(logits - jnp.max(logits, axis=-1, keepdims=True))
    chances = exponent / jnp.sum(exponent, axis=-1, keepdims=True)
    mine = iota(chances.shape, 1) == expert_ref[0]
    gating = jnp.sum(jnp.where(mine, chances, 0.0), axis=-1, keepdims=True)
    gp = (gating * cot_ref[...].astype(F32)).astype(BF)
    gp_ref[...] = gp
    store(gp_ref, gp_out)
    send_ref[:, 2 * ff_half : 2 * ff_half + width] = rows
    send_ref[:, 2 * ff_half + width :] = gp
    for step in range(steps):
        for copy in loads[step]:
            copy.wait()
        hidden = mm(rows, up_vmem[step])
        phi = 0.5 * (1.0 + lax.erf(hidden * (2.0**-0.5)))
        act = (hidden * phi).astype(BF)
        slope = phi + hidden * (jnp.exp(-0.5 * hidden * hidden) * 0.3989422804014327)
        pre = (mm_nt(gp, down_vmem[step]) * slope).astype(BF)
        if step == 0:
            out_acc[...] = mm(act, down_vmem[step])
            back_acc[...] = mm_nt(pre, up_vmem[step])
        else:
            out_acc[...] += mm(act, down_vmem[step])
            back_acc[...] += mm_nt(pre, up_vmem[step])
        if step < half_steps:
            send_ref[:, step * tile : (step + 1) * tile] = act
            send_ref[:, ff_half + step * tile : ff_half + (step + 1) * tile] = pre
        else:
            at = (step - half_steps) * tile
            act_ref[:, at : at + tile] = act
            pre_ref[:, at : at + tile] = pre
        if step == half_steps - 1:
            store(send_ref, send_out)
    store(act_ref, act_out)
    store(pre_ref, pre_out)
    produced = out_acc[...].astype(BF).astype(F32)
    scaled_ref[...] = (gating * produced).astype(BF)
    store(scaled_ref, scaled_out)
    grad_gate = jnp.sum(cot_ref[...].astype(F32) * produced, axis=-1, keepdims=True)
    grad_logits = gating * (mine.astype(F32) - chances) * grad_gate
    low = grad_logits.astype(BF)
    rest = (grad_logits - low.astype(F32)).astype(BF)
    back = back_acc[...] + (mm_nt(low, router_ref[...]) + mm_nt(rest, router_ref[...]))
    back_ref[...] = back.astype(BF)
    router_grad_ref[...] = mm_tn(low, rows) + mm_tn(rest, rows)
    for copy in stores:
        copy.wait()


def expert_grads_body(
    act_ref, pre_ref, rows_ref, gp_ref, act2_ref, pre2_ref, rows2_ref, gp2_ref, down_ref, up_ref
):
    down_ref[...] = mm_tn(act_ref[...], gp_ref[...]) + mm_tn(act2_ref[...], gp2_ref[...])
    up_ref[...] = mm_tn(rows_ref[...], pre_ref[...]) + mm_tn(rows2_ref[...], pre2_ref[...])


def norm_back(grad, source, gain):
    factor = lax.rsqrt(jnp.mean(source * source, axis=-1, keepdims=True) + epsilon)
    unit = source * factor
    scaled = grad * gain
    inner = jnp.mean(scaled * unit, axis=-1, keepdims=True)
    return factor * (scaled - unit * inner), grad * unit


def moe_back_body(
    place_hbm, back_ref, residual_hbm, gain_ref, cot_hbm, _scaled, _after,
    low_ref, gain_grad_ref, grad_out, _passed,
    place_ref, residual_ref, cot_ref, grad_ref, sems,
):
    loads = fetch([place_hbm, residual_hbm, cot_hbm], [place_ref, residual_ref, cot_ref], sems)
    loads[0].wait()
    grad_in = mm_tn(place_ref[...], back_ref[...])
    loads[1].wait()
    passed, terms = norm_back(grad_in, residual_ref[...], gain_ref[...].astype(F32))
    loads[2].wait()
    grad = cot_ref[...].astype(F32) + passed
    grad_ref[...] = grad
    store = pltpu.make_async_copy(grad_ref, grad_out, sems.at[3])
    store.start()
    low_ref[...] = grad.astype(BF)
    gain_grad_ref[...] = jnp.sum(terms, axis=0, keepdims=True)
    store.wait()


def fold_diagonals(squares):
    wide = jnp.concatenate([squares, jnp.zeros_like(squares)], axis=2)
    count = TILE
    while count > 8:
        count //= 2
        wide = wide[:, :count] + pltpu.roll(wide[:, count:], 2 * TILE - count, 2)
    return wide


def attend_back_body(
    half_ref, bits_ref, grad_own_ref, grad_other_ref, w_out_hbm, qkv_hbm, probs_hbm, context_hbm, normed_hbm,
    folded_ref, edge_ref, a0_out, a1_out, a2_out, a3_out, c0_out, c2_out, near_out, gqkv_out,
    a0_ref, a1_ref, a2_ref, a3_ref, c0_ref, c1_ref, c2_ref, c3_ref,
    gqkv_ref, gctx_ref, grad_ref, kv_ref, band_ref,
    w_out_ref, qkv_ref, probs_ref, context_ref, normed_ref, sems, store_sems,
):
    heads = probs_ref.shape[0]
    w_out_in, qkv_in, *probs_in = fetch(
        [w_out_hbm, qkv_hbm] + [probs_hbm.at[h] for h in range(heads)],
        [w_out_ref, qkv_ref] + [probs_ref.at[h] for h in range(heads)],
        sems,
    )
    context_in, normed_in = fetch(
        [context_hbm, normed_hbm], [context_ref, normed_ref], sems.at[pl.ds(2 + heads, 2)]
    )
    stores = []

    def store(source, target):
        stores.append(pltpu.make_async_copy(source, target, store_sems.at[len(stores)]))
        stores[-1].start()

    group, width = normed_ref.shape
    rows = grad_own_ref.shape[0]
    local = context_ref.shape[1]
    blocks = group // TILE
    own_at = pl.multiple_of(half_ref[0] * rows, rows)
    other_at = pl.multiple_of((1 - half_ref[0]) * rows, rows)
    grad_ref[pl.ds(own_at, rows), :] = grad_own_ref[...]
    grad_ref[pl.ds(other_at, rows), :] = grad_other_ref[...]
    grad = grad_ref[...]
    w_out_in.wait()
    gctx_ref[...] = mm_nt(grad, w_out_ref[...]).astype(BF)
    qkv_in.wait()
    scale = HEAD**-0.5
    buckets = 2 * halfway
    edges = [[], []]
    for h in range(heads):
        lo = h * HEAD
        queries = qkv_ref[:, lo : lo + HEAD]
        keys = qkv_ref[:, local + lo : local + lo + HEAD]
        values = qkv_ref[:, 2 * local + lo : 2 * local + lo + HEAD]
        gctx = gctx_ref[:, lo : lo + HEAD]
        if h == 0:
            context_in.wait()
        terms = gctx.astype(F32) * context_ref[:, lo : lo + HEAD].astype(F32)
        inner = jnp.sum(terms, axis=-1, keepdims=True)
        grad_probs = mm_nt(gctx, values)
        probs_in[h].wait()
        low_probs = probs_ref[h]
        grad_scores = low_probs.astype(F32) * (grad_probs - inner)
        low = grad_scores.astype(BF)
        gqkv_ref[:, lo : lo + HEAD] = (mm(low, keys) * scale).astype(BF)
        kv_ref[lo : lo + HEAD, :] = mm_tn(queries, low) * scale
        kv_ref[local + lo : local + lo + HEAD, :] = mm_tn(gctx, low_probs)
        for number, delta in enumerate((-1, 0, 1)):
            band = None
            for b in range(blocks):
                k = b + delta
                if 0 <= k < blocks:
                    piece = grad_scores[
                        b * TILE : (b + 1) * TILE, k * TILE : (k + 1) * TILE
                    ]
                    band = piece if band is None else band + piece
            band_ref[number * heads + h] = band
        for number, sign in enumerate((-1, 1)):
            total = jnp.zeros((1, 1), F32)
            for b in range(blocks):
                for k in range(blocks):
                    if (k - b) * sign > 1:
                        piece = grad_scores[
                            b * TILE : (b + 1) * TILE, k * TILE : (k + 1) * TILE
                        ]
                        total = total + jnp.sum(
                            jnp.sum(piece, axis=0, keepdims=True), axis=1, keepdims=True
                        )
            edges[number].append(total)
    gqkv_ref[:, local : 2 * local] = kv_ref[:local].T.astype(BF)
    gqkv_ref[:, 2 * local :] = kv_ref[local:].T.astype(BF)
    plane, depth = bits_ref[0], bits_ref[1]
    shard = width // 16
    half = width // 2
    targets = (c0_ref, c1_ref, c2_ref, c3_ref)
    dense = mm_tn(context_ref[...], grad).astype(BF)
    for a in range(2):
        for z in range(2):
            for number, target in enumerate(targets):

                @pl.when((depth ^ (2 * a + z)) == number)
                def _(target=target, dense=dense, a=a, z=z):
                    rows_of = slice(z * 4 * shard, (z + 1) * 4 * shard)
                    target[...] = dense[rows_of, a * half : (a + 1) * half]
    size = 4 * shard
    outs = (c0_out, near_out.at[pl.ds(0, size), :], c2_out, near_out.at[pl.ds(size, size), :])
    for target, out in zip(targets, outs):
        store(target, out)
    normed_in.wait()
    targets = (a0_ref, a1_ref, a2_ref, a3_ref)
    dense = mm_tn(normed_ref[...], gqkv_ref[...]).astype(BF)
    for p in range(4):
        for number, target in enumerate(targets):

            @pl.when((plane ^ p) == number)
            def _(target=target, p=p):
                for z in range(4):
                    piece = dense[(p * 4 + z) * shard : (p * 4 + z + 1) * shard]
                    at = pl.multiple_of((depth ^ z) * shard, shard)
                    target[pl.ds(at, shard), :] = piece
    for target, out in zip(targets, (a0_out, a1_out, a2_out, a3_out)):
        store(target, out)
    store(gqkv_ref, gqkv_out)
    folded_ref[...] = fold_diagonals(band_ref[...])
    for number in range(2):
        for h in range(heads):
            edge_ref[h : h + 1, number * TILE : (number + 1) * TILE] = jnp.broadcast_to(
                edges[number][h], (1, TILE)
            )
    for copy in stores:
        copy.wait()


def small_grads_body(
    half_ref, folded_ref, edge_ref, router_grad_ref, moe_gain_grad_ref, gqkv_hbm, w_hbm, x_hbm, x_other_hbm,
    _after, small_ref, own_ref, other_ref,
    gqkv_ref, w_ref, x_ref, x_other_ref, all_ref, sems,
):
    loads = fetch([gqkv_hbm, w_hbm, x_hbm, x_other_hbm], [gqkv_ref, w_ref, x_ref, x_other_ref], sems)
    rows, width = own_ref.shape
    local = w_ref.shape[2]
    heads = local // HEAD
    buckets = 2 * halfway
    own_at = pl.multiple_of(half_ref[0] * rows, rows)
    other_at = pl.multiple_of((1 - half_ref[0]) * rows, rows)
    folded = folded_ref[...]
    spread = jnp.zeros((heads * 8, 8 * buckets), F32)
    for number, delta in enumerate((-1, 0, 1)):
        distance = iota((8, 2 * TILE), 1) - iota((8, 2 * TILE), 0)
        distance = jnp.where(distance >= TILE, distance - 2 * TILE, distance) + TILE * delta
        bucket = bucket_of(distance)
        hot = jnp.concatenate(
            [bucket[r : r + 1] == iota((buckets, 2 * TILE), 0) for r in range(8)], axis=0
        )
        hot = hot.astype(F32).astype(BF)
        sums = folded[number * heads : (number + 1) * heads].reshape(heads * 8, 2 * TILE)
        for _ in range(3):
            low = sums.astype(BF)
            spread = spread + mm_nt(low, hot)
            sums = sums - low.astype(F32)
    same = iota(spread.shape, 0) % 8 == iota(spread.shape, 1) // buckets
    table = jnp.sum(jnp.where(same, spread, 0.0).reshape(heads, 8, 8 * buckets), axis=1)
    step = 4 * buckets
    while step >= buckets:
        table = table + pltpu.roll(table, step, 1)
        step //= 2
    table = table[:, :buckets]
    table = jnp.concatenate([table, jnp.zeros((8 - heads, buckets), F32)], axis=0)
    for number, bucket in enumerate((halfway - 1, 2 * halfway - 1)):
        column = jnp.concatenate(
            [edge_ref[:heads, number * TILE : number * TILE + 1], jnp.zeros((8 - heads, 1), F32)], axis=0
        )
        table = table + jnp.where(iota((8, buckets), 1) == bucket, column, 0.0)
    for copy in loads:
        copy.wait()
    total = None
    for c in range(3):
        part = mm_nt(gqkv_ref[:, c * local : (c + 1) * local], w_ref[c])
        total = part if total is None else total + part
    all_ref[...] = total
    own_ref[...] = all_ref[pl.ds(own_at, rows), :]
    other_ref[...] = all_ref[pl.ds(other_at, rows), :]
    gain_grad = jnp.zeros((1, width), F32)
    for ref, part in ((x_ref, own_ref), (x_other_ref, other_ref)):
        x = ref[...].astype(F32)
        factor = lax.rsqrt(jnp.mean(x * x, axis=-1, keepdims=True) + epsilon)
        gain_grad = gain_grad + jnp.sum(part[...] * (x * factor), axis=0, keepdims=True)
    moe_gain_grad = moe_gain_grad_ref[...]
    row = iota((16, local), 0)
    extra = jnp.concatenate([table, jnp.zeros((8, local - buckets), F32)], axis=1)
    extra = jnp.concatenate([jnp.zeros((8, local), F32), extra], axis=0)
    for number, value in enumerate((moe_gain_grad, gain_grad)):
        for part in range(2):
            piece = value[:, part * local : (part + 1) * local]
            extra = extra + jnp.where(row == 2 * number + part, piece, 0.0)
    small = jnp.concatenate(
        [router_grad_ref[:, :local], router_grad_ref[:, local:], extra], axis=0
    ).astype(BF)
    small_ref[...] = small


def order_body(_value, _after, _out):
    pass


def total_of(*values):
    return functools.reduce(jnp.add, [v.astype(F32) for v in values]).astype(BF)


def pairs_of(a, b, c, d):
    return ((a.astype(F32) + b.astype(F32)) + (c.astype(F32) + d.astype(F32))).astype(BF)


def fold_near_body(got_ref, c0_hbm, c2_hbm, c0_out, c2_out, c0_ref, c2_ref, sems):
    for copy in fetch([c0_hbm, c2_hbm], [c0_ref, c2_ref], sems):
        copy.wait()
    size = c0_ref.shape[0]
    c0_out[...] = total_of(c0_ref[...], got_ref[:size])
    c2_out[...] = total_of(c2_ref[...], got_ref[size:])


def fold_first_body(
    a1_ref, a2_ref, a3_ref, c0_ref, got_ref, a0_hbm, small_ref,
    s0_ref, s2_ref, near_ref, e_ref,
    a0_ref, sem,
):
    load = pltpu.make_async_copy(a0_hbm, a0_ref, sem)
    load.start()
    load.wait()
    shard, lead = s0_ref.shape[0], small_ref.shape[0]
    for d, target in enumerate((s0_ref, near_ref.at[:shard], s2_ref, near_ref.at[shard:])):
        at = slice(d * shard, (d + 1) * shard)
        target[...] = pairs_of(a0_ref[at], a1_ref[at], a2_ref[at], a3_ref[at])
    e_ref[:lead] = small_ref[...]
    e_ref[lead:] = total_of(c0_ref[...], got_ref[...])


def fold_z_body(got_ref, s0_ref, s2_ref, s0_out, s2_out):
    size = s0_ref.shape[0]
    s0_out[...] = total_of(s0_ref[...], got_ref[:size])
    s2_out[...] = total_of(s2_ref[...], got_ref[size:])


def fold_last_body(
    s0_ref, got_ref, e0_ref, e1_ref, e2_ref, e3_ref, total_ref, c_ref, small_ref
):
    lead = small_ref.shape[0]
    total_ref[...] = total_of(s0_ref[...], got_ref[...])
    small_ref[...] = pairs_of(e0_ref[:lead], e1_ref[:lead], e2_ref[:lead], e3_ref[:lead])
    c_ref[...] = pairs_of(e0_ref[lead:], e1_ref[lead:], e2_ref[lead:], e3_ref[lead:])


def join_body(shared, t0_ref, t1_ref, t2_ref, t3_ref, c_ref, small_ref, other_ref, _after, mine_ref, c_mine_ref):
    shard, size = t0_ref.shape[0], c_ref.shape[0]
    for d, ref in enumerate((t0_ref, t1_ref, t2_ref, t3_ref)):
        mine_ref[d * shard : (d + 1) * shard] = ref[...]
    c_mine_ref[:size] = c_ref[...]
    own = small_ref[...].astype(F32)
    both = own + other_ref[...].astype(F32)
    c_mine_ref[size:] = jnp.where(iota(own.shape, 0) < shared, both, own).astype(BF)


def stack_body(a_ref, b_ref, out_ref):
    size = a_ref.shape[0]
    out_ref[:size] = a_ref[...]
    out_ref[size:] = b_ref[...]


def tokens_body(
    place_ref, scaled_ref, residual_ref, own_ref, got_ref, x_ref, gain_ref, grad_res_ref, _after, out_ref, grad_ref
):
    out_ref[...] = (residual_ref[...] + mm_tn(place_ref[...], scaled_ref[...])).astype(BF)
    passed, _ = norm_back(
        own_ref[...] + got_ref[...], x_ref[...].astype(F32), gain_ref[...].astype(F32)
    )
    grad_ref[...] = grad_res_ref[...] + passed


def unpack_mine_body(bits_ref, a0_ref, qkv_out, wide_ref, sems):
    put_quarter(0, a0_ref, bits_ref, wide_ref, qkv_out, sems, True)


def put_quarter(number, ref, bits_ref, wide_ref, qkv_out, sems, wait=False):
    shard = ref.shape[0] // 4
    local = qkv_out.shape[2]
    wide_ref[...] = ref[...].astype(F32)
    copies = []
    for d in range(4):
        at = pl.multiple_of(((bits_ref[0] ^ number) * 4 + (bits_ref[1] ^ d)) * shard, shard)
        for c in range(3):
            copy = pltpu.make_async_copy(
                wide_ref.at[pl.ds(d * shard, shard), pl.ds(c * local, local)],
                qkv_out.at[c, pl.ds(at, shard), :],
                sems.at[d, c],
            )
            copy.start()
            copies.append(copy)
    if wait:
        for copy in copies:
            copy.wait()
    return copies


def unpack_body(
    bits_ref, a1_ref, a2_ref, a3_ref, c0_ref, c2_ref, near_ref, _begun,
    router_ref, norm_gain_ref, moe_gain_ref, bias_ref, qkv_out, w_out_out,
    wide_ref, w_out_ref, qkv_sems, out_sems,
):
    local = qkv_out.shape[2]
    shard = a1_ref.shape[0] // 4
    depth = bits_ref[1]
    copies = []
    for number, ref in enumerate((a1_ref, a2_ref, a3_ref)):
        copies += put_quarter(number + 1, ref, bits_ref, wide_ref.at[number], qkv_out, qkv_sems.at[number])
    size = c0_ref.shape[0]
    others = (c0_ref, near_ref.at[:size], c2_ref, near_ref.at[size:])
    for number, ref in enumerate(others):
        w_out_ref[number] = ref[: 4 * shard].astype(F32)
        slab = depth ^ number
        lane = pl.multiple_of((slab // 2) * local, local)
        at = pl.multiple_of((slab % 2) * 4 * shard, 4 * shard)
        copy = pltpu.make_async_copy(
            w_out_ref.at[number], w_out_out.at[pl.ds(at, 4 * shard), pl.ds(lane, local)], out_sems.at[number]
        )
        copy.start()
        copies.append(copy)
    parts = [ref[4 * shard :].astype(F32) for ref in others]
    small = (parts[0] + parts[1]) + (parts[2] + parts[3])
    experts = router_ref.shape[0]
    router_ref[:, :local] = small[:experts]
    router_ref[:, local:] = small[experts : 2 * experts]
    rest = small[2 * experts :]
    for number, ref in enumerate((moe_gain_ref, norm_gain_ref)):
        ref[:local] = rest[2 * number]
        ref[local:] = rest[2 * number + 1]
    bias_ref[...] = rest[8 : 8 + bias_ref.shape[0], : bias_ref.shape[1]]
    for copy in copies:
        copy.wait()


def per_device(
    tokens, lengths, routes, norm_gain, w_qkv, rel_bias, w_out, moe_gain, w_router, w_in, w_down, cotangent
):
    rows, width = tokens.shape
    sources = lax.axis_size("expert")
    group = rows * lax.axis_size("tensor")
    experts = w_router.shape[1]
    capacity = max(2, 4 * rows // (3 * experts))
    slots = experts * capacity
    local = w_qkv.shape[2]
    heads = local // HEAD
    buckets = rel_bias.shape[0]
    ff = w_in.shape[2]
    ff_half = ff // 2
    half = lax.axis_index("tensor").astype(jnp.int32)
    expert = lax.axis_index("expert").astype(jnp.int32)
    half_one = half.reshape(1)
    gain_a = norm_gain.reshape(1, width)
    gain_b = moe_gain.reshape(1, width)

    def swap(value):
        return lax.ppermute(value, "tensor", [(0, 1), (1, 0)])

    def exchange(value):
        return lax.all_to_all(
            value.reshape(experts, capacity, width), "expert", split_axis=0, concat_axis=0, tiled=True
        ).reshape(slots, width)

    def ordered(value, after):
        return pl.pallas_call(
            order_body,
            out_shape=hbm(value.shape, value.dtype),
            in_specs=[ANY, ANY],
            out_specs=ANY,
            input_output_aliases={0: 0},
            name="order",
        )(value, after)

    x_other = swap(tokens)
    place, cot_slots = pl.pallas_call(
        functools.partial(prep_body, capacity, experts),
        out_shape=(hbm((slots, rows), BF),) + shape_of(((slots, width), BF)),
        in_specs=vmem_specs(1) + [ANY],
        out_specs=[ANY] + vmem_specs(1),
        scratch_shapes=[
            pltpu.VMEM((slots, rows), BF),
            pltpu.VMEM((rows, width), BF),
            pltpu.SemaphoreType.DMA,
            pltpu.SemaphoreType.DMA,
        ],
        cost_estimate=cost(2e9, 1e6),
        name="place_cotangent",
    )(routes.reshape(1, rows), in_hbm(cotangent))
    cot_rows = exchange(cot_slots)

    bias_rows = jnp.pad(rel_bias.T, ((0, 8 - heads), (0, 0)))
    own_sum, other_sum, context, qkv, probs, normed = pl.pallas_call(
        attend_body,
        out_shape=shape_of(((rows, width), F32), ((rows, width), F32))
        + (
            hbm((group, local), BF),
            hbm((group, 3 * local), BF),
            hbm((heads, group, group), BF),
            hbm((group, width), BF),
        ),
        in_specs=[SMEM, SMEM] + vmem_specs(3) + [ANY] + vmem_specs(1) + [ANY],
        out_specs=vmem_specs(2) + [ANY] * 4,
        scratch_shapes=[
            pltpu.VMEM((3, width, local), BF),
            pltpu.VMEM((local, width), BF),
            pltpu.VMEM((group, local), BF),
            pltpu.VMEM((group, 3 * local), BF),
            pltpu.VMEM((heads, group, group), BF),
            pltpu.VMEM((group, width), BF),
            pltpu.VMEM((group, group), F32),
            pltpu.SemaphoreType.DMA((4,)),
            pltpu.SemaphoreType.DMA((heads + 3,)),
        ],
        compiler_params=params(20),
        cost_estimate=cost(8e9, 4e6),
        name="attention",
    )(half_one, lengths, tokens, x_other, gain_a, in_hbm(w_qkv), bias_rows, in_hbm(w_out))
    got_sum = swap(other_sum)

    expert_one = expert.reshape(1)
    moe_slots, router, residual = pl.pallas_call(
        project_body,
        out_shape=shape_of(((slots, width), BF), ((width, experts), BF)) + (hbm((rows, width), F32),),
        in_specs=[SMEM] + vmem_specs(5) + [ANY, ANY],
        out_specs=vmem_specs(2) + [ANY],
        scratch_shapes=[
            pltpu.VMEM((slots, rows), BF),
            pltpu.VMEM((rows, width), F32),
            pltpu.SemaphoreType.DMA((2,)),
        ],
        compiler_params=params(12),
        cost_estimate=cost(2e9, 2e6),
        name="projection",
    )(expert_one, own_sum, got_sum, tokens, gain_b, w_router, in_hbm(place), cot_rows)
    stacked = exchange(moe_slots)

    count = sources * capacity
    tile = FF_TILE
    steps = ff // tile
    half_steps = steps // 2

    back, router_grad, scaled, gp, send, act, pre = pl.pallas_call(
        expert_body,
        out_shape=shape_of(((count, width), BF), ((experts, width), F32))
        + (
            hbm((count, width), BF),
            hbm((count, width), BF),
            hbm((count, 2 * ff_half + 2 * width), BF),
            hbm((count, ff_half), BF),
            hbm((count, ff_half), BF),
        ),
        in_specs=[SMEM, SMEM] + vmem_specs(3) + [ANY, ANY],
        out_specs=vmem_specs(2) + [ANY] * 5,
        scratch_shapes=[
            pltpu.VMEM((steps, width, tile), BF),
            pltpu.VMEM((steps, tile, width), BF),
            pltpu.VMEM((count, width), BF),
            pltpu.VMEM((count, width), BF),
            pltpu.VMEM((count, 2 * ff_half + 2 * width), BF),
            pltpu.VMEM((count, ff_half), BF),
            pltpu.VMEM((count, ff_half), BF),
            pltpu.VMEM((count, width), F32),
            pltpu.VMEM((count, width), F32),
            pltpu.SemaphoreType.DMA((steps, 2)),
            pltpu.SemaphoreType.DMA((5,)),
        ],
        compiler_params=params(32),
        cost_estimate=cost(10e9, 14e6),
        name="expert",
    )(half_one, expert_one, stacked, cot_rows, router, in_hbm(w_in[0]), in_hbm(w_down[0]))
    back_rows = exchange(back)
    peer = swap(send)

    col = lambda first: pl.BlockSpec((count, tile), lambda i: (0, first + i))
    fixed = lambda block: pl.BlockSpec((count, width), lambda i: (0, block))
    grad_down, grad_up = pl.pallas_call(
        expert_grads_body,
        grid=(half_steps,),
        in_specs=[
            col(0), col(0), fixed(0), fixed(0),
            col(0), col(half_steps), fixed(2 * ff_half // width), fixed(2 * ff_half // width + 1),
        ],
        out_specs=[
            pl.BlockSpec((tile, width), lambda i: (i, 0)),
            pl.BlockSpec((width, tile), lambda i: (0, i)),
        ],
        out_shape=shape_of(((ff_half, width), F32), ((width, ff_half), F32)),
        compiler_params=params(20),
        cost_estimate=cost(5e9, 14e6),
        name="expert_grads",
    )(in_hbm(act), in_hbm(pre), stacked, in_hbm(gp), *[in_hbm(peer)] * 4)

    grad_low, moe_gain_grad, grad_res, scaled_late = pl.pallas_call(
        moe_back_body,
        out_shape=shape_of(((rows, width), BF), ((1, width), F32))
        + (hbm((rows, width), F32), hbm((count, width), BF)),
        in_specs=[ANY] + vmem_specs(1) + [ANY] + vmem_specs(1) + [ANY] * 3,
        out_specs=vmem_specs(2) + [ANY, ANY],
        input_output_aliases={5: 3},
        scratch_shapes=[
            pltpu.VMEM((slots, rows), BF),
            pltpu.VMEM((rows, width), F32),
            pltpu.VMEM((rows, width), BF),
            pltpu.VMEM((rows, width), F32),
            pltpu.SemaphoreType.DMA((4,)),
        ],
        compiler_params=params(12),
        cost_estimate=cost(1e9, 2e6),
        name="norm_back",
    )(in_hbm(place), back_rows, in_hbm(residual), gain_b, in_hbm(cotangent), scaled, in_hbm(grad_down))
    grad_other = swap(grad_low)
    scaled_rows = exchange(scaled_late)

    position = jnp.stack([expert & 3, (expert >> 2) & 3])
    shard = width // 16
    lead = 2 * experts + 16
    big, slab = (4 * shard, 3 * local), (4 * shard, local)
    folded, edges, a0, a1, a2, a3, c0, c2, c_near, grad_joined = pl.pallas_call(
        attend_back_body,
        out_shape=(
            *shape_of(((3 * heads, 8, 2 * TILE), F32), ((8, 2 * TILE), F32)),
            *[hbm(big, BF)] * 4, *[hbm(slab, BF)] * 2, hbm((8 * shard, local), BF), hbm((group, 3 * local), BF),
        ),
        in_specs=[SMEM, SMEM] + vmem_specs(2) + [ANY] * 5,
        out_specs=vmem_specs(2) + [ANY] * 8,
        scratch_shapes=[pltpu.VMEM(big, BF)] * 4
        + [pltpu.VMEM(slab, BF)] * 4
        + [
            pltpu.VMEM((group, 3 * local), BF),
            pltpu.VMEM((group, local), BF),
            pltpu.VMEM((group, width), BF),
            pltpu.VMEM((2 * local, group), F32),
            pltpu.VMEM((3 * heads, TILE, TILE), F32),
            pltpu.VMEM((local, width), BF),
            pltpu.VMEM((group, 3 * local), BF),
            pltpu.VMEM((heads, group, group), BF),
            pltpu.VMEM((group, local), BF),
            pltpu.VMEM((group, width), BF),
            pltpu.SemaphoreType.DMA((4 + heads,)),
            pltpu.SemaphoreType.DMA((9,)),
        ],
        compiler_params=params(32),
        cost_estimate=cost(10e9, 10e6),
        name="attention_back",
    )(
        half_one, position, grad_low, grad_other, in_hbm(w_out), in_hbm(qkv), in_hbm(probs), in_hbm(context),
        in_hbm(normed),
    )
    a1 = ordered(a1, scaled_rows)

    def moves(flip):
        pairs = [(2 * e + t, 2 * (e ^ flip) + t) for e in range(sources) for t in range(2)]
        return lambda value: lax.ppermute(value, ("expert", "tensor"), pairs)

    flat = [moves(d) for d in range(1, 4)]
    along = [moves(4 * d) for d in range(1, 4)]

    def add(*values):
        return functools.reduce(jnp.add, [v.astype(F32) for v in values]).astype(BF)

    def fused(name, body, shapes, values, before=(), mib=8):
        return pl.pallas_call(
            body,
            out_shape=[jax.ShapeDtypeStruct(shape, dtype) for shape, dtype in shapes],
            in_specs=vmem_specs(len(values)) + [ANY] * len(before),
            out_specs=vmem_specs(len(shapes)),
            compiler_params=params(mib),
            cost_estimate=cost(1e3, 1e3),
            name=name,
        )(*values, *before)

    quarter = 4 * shard
    wide = 3 * local
    got_a = [flat[d](a) for d, a in enumerate((a1, a2, a3))]
    c0, c2 = pl.pallas_call(
        fold_near_body,
        out_shape=shape_of(*[(slab, BF)] * 2),
        in_specs=vmem_specs(1) + [ANY] * 2,
        out_specs=vmem_specs(2),
        scratch_shapes=[pltpu.VMEM(slab, BF)] * 2 + [pltpu.SemaphoreType.DMA((2,))],
        compiler_params=params(8),
        cost_estimate=cost(1e3, 1e3),
        name="fold_near",
    )(along[0](c_near), in_hbm(c0), in_hbm(c2))
    got_c = along[1](c2)
    small, own_gn, other_gn = pl.pallas_call(
        small_grads_body,
        out_shape=shape_of(((lead, local), BF), ((rows, width), F32), ((rows, width), F32)),
        in_specs=[SMEM] + vmem_specs(4) + [ANY] * 5,
        out_specs=vmem_specs(3),
        scratch_shapes=[
            pltpu.VMEM((group, 3 * local), BF),
            pltpu.VMEM((3, width, local), BF),
            pltpu.VMEM((rows, width), BF),
            pltpu.VMEM((rows, width), BF),
            pltpu.VMEM((group, width), F32),
            pltpu.SemaphoreType.DMA((4,)),
        ],
        compiler_params=params(16),
        cost_estimate=cost(1e3, 1e3),
        name="small_grads",
    )(
        half_one, folded, edges, router_grad, moe_gain_grad, in_hbm(grad_joined), in_hbm(w_qkv), in_hbm(tokens),
        in_hbm(x_other), c0,
    )
    got_gn = swap(other_gn)
    output, grad_tokens = pl.pallas_call(
        tokens_body,
        out_shape=shape_of(((rows, width), BF), ((rows, width), F32)),
        in_specs=vmem_specs(8) + [ANY],
        out_specs=vmem_specs(2),
        compiler_params=params(12),
        cost_estimate=cost(1e3, 1e3),
        name="token_outputs",
    )(place, scaled_rows, residual, own_gn, got_gn, tokens, gain_a, grad_res, c0)

    s0, s2, s_near, part_c = pl.pallas_call(
        fold_first_body,
        out_shape=shape_of(
            *[((shard, wide), BF)] * 2, ((2 * shard, wide), BF), ((lead + 4 * shard, local), BF)
        ),
        in_specs=vmem_specs(5) + [ANY] + vmem_specs(1),
        out_specs=vmem_specs(4),
        scratch_shapes=[pltpu.VMEM(big, BF), pltpu.SemaphoreType.DMA],
        compiler_params=params(8),
        cost_estimate=cost(1e3, 1e3),
        name="fold_first",
    )(*got_a, c0, got_c, in_hbm(a0), small)
    s0, s2 = fused("fold_z", fold_z_body, [((shard, wide), BF)] * 2, (along[0](s_near), s0, s2))
    got_z = along[1](s2)
    got_e = [flat[d](part_c) for d in range(3)]
    total, c_full, small = fused(
        "fold_last",
        fold_last_body,
        [((shard, wide), BF), (slab, BF), ((lead, local), BF)],
        (s0, got_z, part_c, *got_e),
    )
    for b in range(4, sources.bit_length() - 1):
        further = moves(1 << b)
        total = add(total, further(total))
        c_full = add(c_full, further(c_full))
        small = add(small, further(small))

    others = [along[d](total) for d in range(3)]
    mine, c_mine = fused(
        "join",
        functools.partial(join_body, 2 * experts + 8),
        [((quarter, wide), BF), ((quarter + lead, local), BF)],
        (total, *others, c_full, small, swap(small)),
        (grad_tokens,),
    )
    all_mine = [mine] + [flat[d](mine) for d in range(3)]
    c_far = along[1](c_mine)
    (c_two,) = fused("stack", stack_body, [((2 * (quarter + lead), local), BF)], (c_mine, c_far))
    c_near = along[0](c_two)
    begun = pl.pallas_call(
        unpack_mine_body,
        out_shape=hbm((3, width, local), F32),
        in_specs=[SMEM] + vmem_specs(1),
        out_specs=ANY,
        scratch_shapes=[pltpu.VMEM((quarter, wide), F32), pltpu.SemaphoreType.DMA((4, 3))],
        compiler_params=params(8),
        cost_estimate=cost(1e3, 1e3),
        name="unpack_mine",
    )(position, mine)
    grad_router, grad_norm_gain, grad_moe_gain, grad_rel, grad_qkv, grad_out = pl.pallas_call(
        unpack_body,
        out_shape=shape_of(
            ((experts, width), F32), ((width,), F32), ((width,), F32), ((heads, buckets), F32)
        )
        + (hbm((3, width, local), F32), hbm((local, width), F32)),
        in_specs=[SMEM] + vmem_specs(6) + [ANY],
        out_specs=vmem_specs(4) + [ANY] * 2,
        input_output_aliases={7: 4},
        scratch_shapes=[
            pltpu.VMEM((3, quarter, wide), F32),
            pltpu.VMEM((4, quarter, local), F32),
            pltpu.SemaphoreType.DMA((3, 4, 3)),
            pltpu.SemaphoreType.DMA((4,)),
        ],
        compiler_params=params(12),
        cost_estimate=cost(1e3, 1e3),
        name="unpack",
    )(position, *all_mine[1:], c_mine, c_far, c_near, begun)

    return (
        output,
        grad_tokens,
        grad_norm_gain,
        grad_qkv,
        grad_rel.T,
        grad_out,
        grad_moe_gain,
        grad_router.T,
        grad_up[None],
        grad_down[None],
    )


def solution(mesh):
    return jax.shard_map(
        per_device,
        mesh=mesh,
        in_specs=(
            P(("expert", "tensor"), None),
            P("expert", None),
            P(("expert", "tensor"), None),
            P(),
            P(None, None, "tensor"),
            P(None, "tensor"),
            P("tensor", None),
            P(),
            P(),
            P("expert", None, None),
            P("expert", None, None),
            P(("expert", "tensor"), None),
        ),
        out_specs=(
            P(("expert", "tensor"), None),
            P(("expert", "tensor"), None),
            P(),
            P(None, None, "tensor"),
            P(None, "tensor"),
            P("tensor", None),
            P(),
            P(),
            P("expert", None, "tensor"),
            P("expert", "tensor", None),
        ),
        check_vma=False,
    )
```
